32 devices in a mesh: ctx: 8 (over z, x), fsdp: 4 (over y, core).
Axes of the slice: x: 2, y: 2, z: 4, core: 2. Of those that a mesh axis runs over, the one named last changes fastest.
Arguments:
- queries: bfloat16 [1024, 2048], P('ctx', 'fsdp'), may hold values from -120 to 120
- keys: bfloat16 [1024, 256], P('ctx'), may hold values from -5 to 5
- values: bfloat16 [1024, 256], P('ctx'), may hold values from -5 to 5
- out_grad: bfloat16 [1024, 2048], P('ctx', 'fsdp'), may hold values from -5 to 5
- hidden: bfloat16 [1024, 8192], P('ctx', 'fsdp'), may hold values from -40 to 40
- key_weight: bfloat16 [8192, 256], P('fsdp'), may hold values from -10 to 10
- value_weight: bfloat16 [8192, 256], P('fsdp'), may hold values from -10 to 10
- stretch_owner: int32 [8], replicated, may hold values from 0 to 7, as said below
- positions: int32 [1024], P('ctx'), may hold values from 0 to 511, as said below
Outputs:
- query_grad: bfloat16 [1024, 2048], P('ctx', 'fsdp')
- key_weight_grad: float32 [8192, 256], P('fsdp')
- value_weight_grad: float32 [8192, 256], P('fsdp')
The draws below stay inside these ranges and needn't reach their ends.
Inputs may be any that keep to these rules, and one draw needn't show every extreme that they name: A permutation; index b of ctx holds sequence stretch stretch_owner[b] in its first 64 rows and stretch 2 * 8 - 1 - stretch_owner[b] in the others. `positions`: documents are contiguous in sequence order; a row's position counts from its document's first token, and the sequence's first token has position 0.
All inputs are finite; a program needn't handle non-finite values.
Results may differ from the reference program's by a relative error of at most 0.015.
Values may be sent and summed in bfloat16 or wider, within the bound.
No kernel may reach another device: no remote copies, remote signals or barrier semaphores. Data moves between devices by JAX's collectives and lax.ppermute only.
A program may use at most 64 MiB of HBM per device.

```python
import math
import jax
import jax.numpy as jnp
from jax import lax

D = 8192
DH = 128
HPG = 8
KVG = 2
TOK_DEV = 128
TOKENS = 1024
HEADS = 16
PAIRS = 8


def draw_stretch_owner(key, part):
    return jax.random.permutation(jax.random.fold_in(key, 7), PAIRS).astype(jnp.int32)


def sequence_positions(key):
    span = TOKENS // 2
    begin = jax.random.randint(jax.random.fold_in(key, 31), (), 0, TOKENS - span + 1)
    index = jnp.arange(TOKENS, dtype=jnp.int32)
    starts = jax.random.randint(jax.random.fold_in(key, 32), (TOKENS,), 0, 256) == 0
    inside = (index >= begin) & (index < begin + span)
    starts = starts & jnp.logical_not(inside) | (index == begin) | (index == begin + span) | (index == 0)
    marks = jnp.where(starts, index, 0)
    last = lax.cummax(marks, axis=0)
    return (index - last).astype(jnp.int32)


def layout_rows(key):
    owners = draw_stretch_owner(key, 0)
    half = TOK_DEV // 2
    stretches = jnp.stack([owners, 2 * PAIRS - 1 - owners], axis=1)
    offsets = jnp.arange(half, dtype=jnp.int32)
    return (stretches[:, :, None] * half + offsets[None, None, :]).reshape(TOKENS)


def draw_positions(key, part):
    return sequence_positions(key)[layout_rows(key)].astype(jnp.int32)


def attention_pair(key):
    keys = jnp.clip(jax.random.normal(jax.random.fold_in(key, 41), (TOKENS, KVG * DH), jnp.float32), -5.0, 5.0)
    queries = jnp.clip(jax.random.normal(jax.random.fold_in(key, 42), (TOKENS, KVG * HPG * DH), jnp.float32), -5.0, 5.0)
    return (queries, keys)


def draw_queries(key, part):
    return attention_pair(key)[0].astype(jnp.bfloat16)


def draw_keys(key, part):
    return attention_pair(key)[1].astype(jnp.bfloat16)


def draw_hidden(key, part):
    rows = jnp.arange(TOKENS, dtype=jnp.float32)[:, None] / (TOKENS - 1)
    cols = jnp.arange(D, dtype=jnp.float32)[None, :] / (D - 1)
    gain = jnp.exp(jax.random.uniform(jax.random.fold_in(key, 51), (1, D), jnp.float32, math.log(0.03), math.log(0.3)))
    base = jnp.clip(jax.random.normal(jax.random.fold_in(key, 52), (TOKENS, D), jnp.float32), -5.0, 5.0)
    ramp = (1.0 + 2.0 * rows) * (3.0 - 2.0 * cols)
    return (base * gain * ramp).astype(jnp.bfloat16)


def weight_law(key, salt):
    cols = jnp.exp(jax.random.uniform(jax.random.fold_in(key, salt), (1, KVG * DH), jnp.float32, math.log(0.1), math.log(10.0)))
    rows = 1.0 + 2.0 * jnp.arange(D, dtype=jnp.float32)[:, None] / (D - 1)
    base = jnp.clip(jax.random.normal(jax.random.fold_in(key, salt + 1), (D, KVG * DH), jnp.float32), -5.0, 5.0)
    return base * rows * cols / math.sqrt(D)


def draw_key_weight(key, part):
    return weight_law(key, 61).astype(jnp.bfloat16)


def draw_value_weight(key, part):
    return weight_law(key, 71).astype(jnp.bfloat16)


def levels(stream_key, shape, shards, least, high):
    level = 1.0
    for axis_at, parts in shards:
        heights = jax.random.uniform(jax.random.fold_in(jax.random.fold_in(stream_key, 6), axis_at), (parts,), jnp.float32, least / len(shards), high / len(shards))
        level = level * jnp.repeat(jnp.exp(heights), shape[axis_at] // parts).reshape((-1,) + (1,) * (len(shape) - 1 - axis_at))
    return level


def bell_draw(rng, shape, deviation, limit, pieces=(), kind=jnp.bfloat16):
    array = jax.random.normal(rng, shape, jnp.float32) * deviation
    if len(pieces) > 0:
        array = levels(rng, shape, pieces, -0.22, 0.18) * array
    return jnp.clip(array, min=-limit, max=limit).astype(kind)


def setup_inputs(seed: int = 0) -> dict:
    arg_keys = jax.random.split(jax.random.key(seed), 10)
    return {
        "queries": draw_queries(jax.random.fold_in(arg_keys[9], 71), 0),
        "keys": draw_keys(jax.random.fold_in(arg_keys[9], 71), 0),
        "values": bell_draw(arg_keys[2], (TOKENS, KVG * DH), 1.0, 5.0, ((0, 8),)),
        "out_grad": bell_draw(arg_keys[3], (TOKENS, HEADS * DH), 1.0, 5.0, ((0, 8), (1, 4))),
        "hidden": draw_hidden(jax.random.fold_in(arg_keys[9], 71), 0),
        "key_weight": draw_key_weight(jax.random.fold_in(arg_keys[9], 71), 0),
        "value_weight": draw_value_weight(jax.random.fold_in(arg_keys[9], 71), 0),
        "stretch_owner": draw_stretch_owner(jax.random.fold_in(arg_keys[9], 71), 0),
        "positions": draw_positions(jax.random.fold_in(arg_keys[9], 71), 0),
    }


CLIP_RATE = 0.02
EPSILON = 1e-06
NEGATIVE = -1e+30

def head_grads(query_head, grad_head, key_group, value_group, place, floor):
    scale = 1.0 / math.sqrt(DH)
    block = min(512, TOKENS)

    def step(carry, index):
        key_acc, value_acc = carry
        start = index * block
        q_block = lax.dynamic_slice_in_dim(query_head, start, block, 0)
        g_block = lax.dynamic_slice_in_dim(grad_head, start, block, 0)
        q_place = lax.dynamic_slice_in_dim(place, start, block, 0)
        q_floor = lax.dynamic_slice_in_dim(floor, start, block, 0)
        seen = (place[None, :] <= q_place[:, None]) & (place[None, :] >= q_floor[:, None])
        raw = jnp.dot(q_block, key_group.T, precision=lax.Precision.HIGHEST) * scale
        scores = jnp.where(seen, raw, NEGATIVE)
        top = lax.optimization_barrier(jnp.max(scores, axis=1))
        mass = lax.optimization_barrier(jnp.sum(jnp.where(seen, jnp.exp(scores - top[:, None]), 0.0), axis=1))
        lse = top + jnp.log(mass)
        probs = jnp.where(seen, jnp.exp(scores - lse[:, None]), 0.0)
        dprobs = jnp.dot(g_block, value_group.T, precision=lax.Precision.HIGHEST)
        delta = lax.optimization_barrier(jnp.sum(probs * dprobs, axis=1))
        slopes = (probs * (dprobs - delta[:, None]) * scale).astype(jnp.bfloat16)
        slopes = lax.optimization_barrier(slopes).astype(jnp.float32)
        probs_b = lax.optimization_barrier(probs.astype(jnp.bfloat16)).astype(jnp.float32)
        query_part = jnp.dot(slopes, key_group, precision=lax.Precision.HIGHEST).astype(jnp.bfloat16)
        key_acc = key_acc + jnp.dot(slopes.T, q_block, precision=lax.Precision.HIGHEST)
        value_acc = value_acc + jnp.dot(probs_b.T, g_block, precision=lax.Precision.HIGHEST)
        return ((key_acc, value_acc), query_part)
    zero = jnp.zeros((TOKENS, DH), jnp.float32)
    (key_acc, value_acc), query_parts = lax.scan(step, (zero, zero), jnp.arange(TOKENS // block))
    return (key_acc, value_acc, query_parts.reshape(TOKENS, DH))

def reference(queries, keys, values, out_grad, hidden, key_weight, value_weight, stretch_owner, positions):
    half = TOK_DEV // 2
    owners = stretch_owner.astype(jnp.int32)
    stretches = jnp.stack([owners, 2 * PAIRS - 1 - owners], axis=1)
    offsets = jnp.arange(half, dtype=jnp.int32)
    place = (stretches[:, :, None] * half + offsets[None, None, :]).reshape(TOKENS).astype(jnp.int32)
    floor = place - positions.astype(jnp.int32)
    query_all = queries.astype(jnp.float32)
    grad_all = out_grad.astype(jnp.float32)
    key_parts = []
    value_parts = []
    query_parts = []
    for group in range(KVG):
        key_group = keys[:, group * DH:(group + 1) * DH].astype(jnp.float32)
        value_group = values[:, group * DH:(group + 1) * DH].astype(jnp.float32)
        key_acc = jnp.zeros((TOKENS, DH), jnp.float32)
        value_acc = jnp.zeros((TOKENS, DH), jnp.float32)
        for member in range(HPG):
            head = group * HPG + member
            key_term, value_term, query_part = head_grads(query_all[:, head * DH:(head + 1) * DH], grad_all[:, head * DH:(head + 1) * DH], key_group, value_group, place, floor)
            key_acc = key_acc + key_term
            value_acc = value_acc + value_term
            query_parts.append(query_part)
        key_parts.append(key_acc)
        value_parts.append(value_acc)
    query_grad = jnp.concatenate(query_parts, axis=1)
    key_grads = jnp.concatenate(key_parts, axis=1).astype(jnp.bfloat16)
    value_grads = jnp.concatenate(value_parts, axis=1).astype(jnp.bfloat16)
    raw_key = jnp.dot(hidden.T, key_grads, preferred_element_type=jnp.float32)
    raw_value = jnp.dot(hidden.T, value_grads, preferred_element_type=jnp.float32)
    key_f = key_weight.astype(jnp.float32)
    value_f = value_weight.astype(jnp.float32)

    def clip(raw, weight):
        weight_norm = jnp.sqrt(lax.optimization_barrier(jnp.sum(weight * weight, axis=0)) + EPSILON)
        grad_norm = jnp.sqrt(lax.optimization_barrier(jnp.sum(raw * raw, axis=0)) + EPSILON)
        factor = jnp.minimum(1.0, CLIP_RATE * TOKENS * weight_norm / grad_norm)
        return raw * factor[None, :]
    return (query_grad, clip(raw_key, key_f), clip(raw_value, value_f))
```

```python
import functools
import math

import jax
import jax.numpy as jnp
from jax import lax
from jax.experimental import pallas as pl
from jax.experimental.pallas import tpu as pltpu
from jax.sharding import PartitionSpec as P

DH = 128
HPG = 8
KVG = 2


CLIP_RATE = 0.02
EPSILON = 1e-06
NEGATIVE = -1e30
GATHER_LIMIT = 8 * 2**20

CONTRACT_LAST = (((1,), (1,)), ((), ()))
CONTRACT_FIRST = (((0,), (0,)), ((), ()))
VMEM = pl.BlockSpec(memory_space=pltpu.VMEM)
SMEM = pl.BlockSpec(memory_space=pltpu.SMEM)


def rows_by_head(block, heads, width):
    count = block.shape[0]
    return block.reshape(count, heads, width).transpose(1, 0, 2).reshape(heads * count, width)


def local_large(
    queries, keys, values, out_grad, hidden, key_weight, value_weight, stretch_owner, positions
):
    tok_dev = queries.shape[0]
    heads = queries.shape[1] // DH
    ctx_count = lax.axis_size("ctx")
    total = tok_dev * ctx_count
    half = tok_dev // 2
    ctx_index = lax.axis_index("ctx")
    group = lax.axis_index("fsdp") * heads // HPG
    scale = 1.0 / math.sqrt(DH)
    block = min(512, total)
    blocks = total // block
    query_count = heads * tok_dev
    own_keys = lax.dynamic_slice_in_dim(keys, group * DH, DH, 1)
    own_values = lax.dynamic_slice_in_dim(values, group * DH, DH, 1)
    all_keys, all_values = (
        lax.all_gather(own_keys, "ctx", axis=0, tiled=True),
        lax.all_gather(own_values, "ctx", axis=0, tiled=True),
    )
    offsets = jnp.arange(half, dtype=jnp.int32)
    stretches = jnp.stack([stretch_owner, 2 * ctx_count - 1 - stretch_owner], axis=1)
    key_place = (stretches[:, :, None] * half + offsets[None, None, :]).reshape(total)
    mine = lax.dynamic_slice_in_dim(stretches, ctx_index, 1, 0)[0]
    local_place = (mine[:, None] * half + offsets[None, :]).reshape(tok_dev)
    query_place = jnp.tile(local_place, heads)
    query_floor = jnp.tile(local_place - positions, heads)
    query_rows = rows_by_head(queries, heads, DH)
    grad_rows = rows_by_head(out_grad, heads, DH)

    def scores_at(start, width):
        key_block = lax.dynamic_slice_in_dim(all_keys, start, width, 0)
        place = lax.dynamic_slice_in_dim(key_place, start, width, 0)
        raw = (
            lax.dot_general(
                query_rows, key_block, CONTRACT_LAST, preferred_element_type=jnp.float32
            )
            * scale
        )
        seen = (place[None, :] <= query_place[:, None]) & (place[None, :] >= query_floor[:, None])
        return (jnp.where(seen, raw, NEGATIVE), seen, key_block)

    def stats_step(step, carry):
        top, mass = carry
        masked, seen, key_block = scores_at(step * block, block)
        new_top = jnp.maximum(top, jnp.max(masked, axis=1))
        weights = jnp.where(seen, jnp.exp(masked - new_top[:, None]), 0.0)
        mass = mass * jnp.exp(top - new_top) + jnp.sum(weights, axis=1)
        return (new_top, mass)

    start_top = jnp.full((query_count,), NEGATIVE, jnp.float32)
    start_mass = jnp.zeros((query_count,), jnp.float32)
    top, mass = lax.fori_loop(0, blocks, stats_step, (start_top, start_mass))
    lse = top + jnp.log(mass)

    def probs_at(start, width):
        masked, seen, key_block = scores_at(start, width)
        probs = jnp.where(seen, jnp.exp(masked - lse[:, None]), 0.0)
        value_block = lax.dynamic_slice_in_dim(all_values, start, width, 0)
        dprobs = lax.dot_general(
            grad_rows, value_block, CONTRACT_LAST, preferred_element_type=jnp.float32
        )
        return (probs, dprobs, key_block)

    def delta_step(step, acc):
        probs, dprobs, key_block = probs_at(step * block, block)
        return acc + jnp.sum(probs * dprobs, axis=1)

    delta = lax.fori_loop(0, blocks, delta_step, jnp.zeros((query_count,), jnp.float32))

    def slopes_at(start, width):
        probs, dprobs, key_block = probs_at(start, width)
        slopes = (probs * (dprobs - delta[:, None]) * scale).astype(jnp.bfloat16)
        return (probs.astype(jnp.bfloat16), slopes, key_block)

    def key_terms(probs_b, slopes):
        key_part = lax.dot_general(
            slopes, query_rows, CONTRACT_FIRST, preferred_element_type=jnp.float32
        )
        value_part = lax.dot_general(
            probs_b, grad_rows, CONTRACT_FIRST, preferred_element_type=jnp.float32
        )
        return jnp.concatenate([key_part, value_part], axis=1)

    start_query = jnp.zeros((query_count, DH), jnp.float32)

    def query_step(step, query_acc):
        probs_b, slopes, key_block = slopes_at(step * block, block)
        return query_acc + jnp.dot(slopes, key_block, preferred_element_type=jnp.float32)

    query_acc = lax.fori_loop(0, blocks, query_step, start_query)
    width = math.gcd(tok_dev * lax.axis_size("ctx"), block)

    def inner(step, acc):
        offset = step * width
        probs_b, slopes, key_block = slopes_at(offset, width)
        return lax.dynamic_update_slice_in_dim(acc, key_terms(probs_b, slopes), offset, 0)

    own_grads = lax.psum_scatter(
        lax.fori_loop(
            0,
            tok_dev * lax.axis_size("ctx") // width,
            inner,
            jnp.zeros((tok_dev * lax.axis_size("ctx"), 2 * DH), jnp.float32),
        ),
        "ctx",
        scatter_dimension=0,
        tiled=True,
    )
    query_grad = (
        query_acc.reshape(heads, tok_dev, DH)
        .transpose(1, 0, 2)
        .reshape(tok_dev, heads * DH)
        .astype(jnp.bfloat16)
    )
    members = lax.all_gather(own_grads.astype(jnp.bfloat16), "fsdp", axis=0, tiled=True).astype(
        own_grads.dtype
    )
    per_group = members.reshape(KVG, -1, tok_dev, 2 * DH).sum(axis=1)
    key_grads = (
        per_group[:, :, :DH].transpose(1, 0, 2).reshape(tok_dev, KVG * DH).astype(jnp.bfloat16)
    )
    value_grads = (
        per_group[:, :, DH:].transpose(1, 0, 2).reshape(tok_dev, KVG * DH).astype(jnp.bfloat16)
    )
    both_grads = jnp.concatenate([key_grads, value_grads], axis=1)
    columns = KVG * DH
    raw = lax.psum(
        lax.dot_general(hidden, both_grads, CONTRACT_FIRST, preferred_element_type=jnp.float32),
        "ctx",
    )
    key_f = key_weight.astype(jnp.float32)
    value_f = value_weight.astype(jnp.float32)
    grad_sq, key_sq, value_sq = lax.psum(
        (
            jnp.sum(raw * raw, axis=0),
            jnp.sum(key_f * key_f, axis=0),
            jnp.sum(value_f * value_f, axis=0),
        ),
        "fsdp",
    )
    weight_norm = jnp.sqrt(jnp.concatenate([key_sq, value_sq]) + EPSILON)
    grad_norm = jnp.sqrt(grad_sq + EPSILON)
    clipped = raw * jnp.minimum(1.0, CLIP_RATE * total * weight_norm / grad_norm)[None, :]
    return (query_grad, clipped[:, :columns], clipped[:, columns:])


SIDES = 2
MEMBERS = 2
DIGIT = 64


def pack_kernel(ids, keys, values, queries, out_grad, positions, kv_out, qd_out):
    half = kv_out.shape[0]
    tok_dev = queries.shape[0]
    rows = pl.ds(pl.multiple_of(ids[3] * half, half), half)
    columns = pl.ds(pl.multiple_of(ids[2] * DH, DH), DH)
    kv_out[:, :DH] = keys[rows, columns]
    kv_out[:, DH:] = values[rows, columns]
    qd_out[:tok_dev] = queries[...]
    qd_out[tok_dev : 2 * tok_dev] = out_grad[...]
    place = positions[...]
    high = place // DIGIT
    low = place - high * DIGIT
    pad = jnp.zeros((qd_out.shape[0] - 2 * tok_dev - 2, tok_dev), jnp.float32)
    digits = jnp.concatenate([high.astype(jnp.float32), low.astype(jnp.float32), pad], axis=0)
    qd_out[2 * tok_dev :, :tok_dev] = digits.astype(jnp.bfloat16)
    rest = qd_out.shape[1] - tok_dev
    if rest > 0:
        qd_out[2 * tok_dev :, tok_dev:] = jnp.zeros((qd_out.shape[0] - 2 * tok_dev, rest), jnp.bfloat16)


def turn_kernel(hidden, out):
    out[...] = hidden[...].T


def seen_pairs(ids, owner, planes, half, qd):
    last = 2 * planes * SIDES - 1
    tok_dev = 2 * half
    key_rows = []
    row = lax.broadcasted_iota(jnp.int32, (half, tok_dev), 0)
    for j in range(planes):
        stretch = owner[(ids[0] ^ j) * SIDES + ids[1]]
        stretch = jnp.where(ids[3] == 0, stretch, last - stretch)
        key_rows.append(row + stretch * half)
    key_place = jnp.concatenate(key_rows, axis=0)
    lane = lax.broadcasted_iota(jnp.int32, (1, tok_dev), 1)
    seen = []
    for side in range(SIDES):
        stretch = owner[ids[0] * SIDES + (ids[1] ^ side)]
        place = jnp.where(lane < half, lane + stretch * half, lane - half + (last - stretch) * half)
        digits = qd[side * MEMBERS][2 * tok_dev :, :tok_dev].astype(jnp.float32)
        back = (digits[0:1] * DIGIT + digits[1:2]).astype(jnp.int32)
        seen.append((key_place <= place) & (key_place >= place - back))
    return seen


def scaled_scores(k, q, scale):
    return lax.dot_general(k, q, CONTRACT_LAST, preferred_element_type=jnp.float32) * scale


def stats_kernel(planes, ids, owner, *refs):
    kv_refs, qd, stats = refs[:planes], refs[planes : planes + SIDES * MEMBERS], refs[-1]
    half = kv_refs[0].shape[0]
    tok_dev = 2 * half
    heads = qd[0].shape[1] // DH
    scale = 1.0 / math.sqrt(DH)
    kv = jnp.concatenate([ref[...] for ref in kv_refs], axis=0)
    k, v = kv[:, :DH], kv[:, DH:]
    seen = seen_pairs(ids, owner, planes, half, qd)
    tiles = SIDES * MEMBERS * heads
    for source in range(SIDES * MEMBERS):
        for head in range(heads):
            q = qd[source][:tok_dev, head * DH : (head + 1) * DH]
            d = qd[source][tok_dev : 2 * tok_dev, head * DH : (head + 1) * DH]
            mask = seen[source // MEMBERS]
            scores = jnp.where(mask, scaled_scores(k, q, scale), NEGATIVE)
            dprobs = lax.dot_general(v, d, CONTRACT_LAST, preferred_element_type=jnp.float32)
            top = jnp.max(scores, axis=0, keepdims=True)
            weights = jnp.where(mask, jnp.exp(scores - top), 0.0)
            tile = source * heads + head
            stats[tile : tile + 1] = top
            stats[tiles + tile : tiles + tile + 1] = jnp.sum(weights, axis=0, keepdims=True)
            stats[2 * tiles + tile : 2 * tiles + tile + 1] = jnp.sum(
                weights * dprobs, axis=0, keepdims=True
            )


def grads_kernel(planes, ids, owner, *refs):
    sources = SIDES * MEMBERS
    kv_refs, refs = refs[:planes], refs[planes:]
    qd, refs = refs[:sources], refs[sources:]
    stats, refs = refs[:sources], refs[sources:]
    kv_out, q_out = refs[:planes], refs[planes:]
    half = kv_refs[0].shape[0]
    tok_dev = 2 * half
    heads = qd[0].shape[1] // DH
    scale = 1.0 / math.sqrt(DH)
    kv = jnp.concatenate([ref[...] for ref in kv_refs], axis=0)
    k, v = kv[:, :DH], kv[:, DH:]
    seen = seen_pairs(ids, owner, planes, half, qd)
    tiles = sources * heads
    key_acc = jnp.zeros((planes * half, DH), jnp.float32)
    value_acc = jnp.zeros((planes * half, DH), jnp.float32)
    for source in range(sources):
        q_rows, d_rows, slope_tiles, prob_tiles = [], [], [], []
        mask = seen[source // MEMBERS]
        first = source * heads
        parts = [
            [
                stats[other][kind * tiles + (source ^ other) * heads :][:heads]
                for other in range(sources)
            ]
            for kind in range(3)
        ]
        top = functools.reduce(jnp.maximum, parts[0])
        shares = [jnp.exp(part - top) for part in parts[0]]
        mass = sum(share * part for share, part in zip(shares, parts[1], strict=True))
        lse = top + jnp.log(mass)
        delta = sum(share * part for share, part in zip(shares, parts[2], strict=True)) / mass
        for head in range(heads):
            q = qd[source][:tok_dev, head * DH : (head + 1) * DH]
            d = qd[source][tok_dev : 2 * tok_dev, head * DH : (head + 1) * DH]
            scores = scaled_scores(k, q, scale)
            dprobs = lax.dot_general(v, d, CONTRACT_LAST, preferred_element_type=jnp.float32)
            probs = jnp.where(mask, jnp.exp(scores - lse[head : head + 1]), 0.0)
            slopes = (probs * (dprobs - delta[head : head + 1]) * scale).astype(jnp.bfloat16)
            q_rows.append(q)
            d_rows.append(d)
            slope_tiles.append(slopes)
            prob_tiles.append(probs.astype(jnp.bfloat16))
            q_part = lax.dot_general(slopes, k, CONTRACT_FIRST, preferred_element_type=jnp.float32)
            q_out[source][:, head * DH : (head + 1) * DH] = q_part.astype(q_out[source].dtype)
        key_acc += jnp.dot(
            jnp.concatenate(slope_tiles, axis=1),
            jnp.concatenate(q_rows, axis=0),
            preferred_element_type=jnp.float32,
        )
        value_acc += jnp.dot(
            jnp.concatenate(prob_tiles, axis=1),
            jnp.concatenate(d_rows, axis=0),
            preferred_element_type=jnp.float32,
        )
    for j in range(planes):
        kv_out[j][:, :DH] = key_acc[j * half : (j + 1) * half].astype(kv_out[j].dtype)
        kv_out[j][:, DH:] = value_acc[j * half : (j + 1) * half].astype(kv_out[j].dtype)


def sum_kernel(*refs):
    total = refs[0][...].astype(jnp.float32)
    for ref in refs[1:-1]:
        total += ref[...].astype(jnp.float32)
    refs[-1][...] = total.astype(refs[-1].dtype)


def square_kernel(key_weight, value_weight, out):
    width = key_weight.shape[1]
    step = 256

    def body(i, acc):
        rows = pl.ds(pl.multiple_of(i * step, step), step)
        k = key_weight[rows].astype(jnp.float32)
        v = value_weight[rows].astype(jnp.float32)
        return (
            acc[0] + jnp.sum((k * k).reshape(-1, 8, width), axis=0),
            acc[1] + jnp.sum((v * v).reshape(-1, 8, width), axis=0),
        )

    zero = jnp.zeros((8, width), jnp.float32)
    k, v = lax.fori_loop(0, key_weight.shape[0] // step, body, (zero, zero))
    out[:, :width] = jnp.broadcast_to(jnp.sum(k, axis=0, keepdims=True), (8, width))
    out[:, width:] = jnp.broadcast_to(jnp.sum(v, axis=0, keepdims=True), (8, width))


def project_kernel(planes, ids, squares, *refs):
    count = planes * SIDES
    turned, refs = refs[: count + 1], refs[count + 1 :]
    pieces, refs = refs[:8], refs[8:]
    raw, sums, all_turned, grads, acc = refs
    step = pl.program_id(0)
    steps = pl.num_programs(0)
    tok_dev = turned[0].shape[1]
    half = tok_dev // 2
    mine = jnp.where(ids[1] == 0, ids[0], count - 1 - ids[0])

    @pl.when(step == 0)
    def _():
        for index, piece in enumerate(pieces):
            side = ids[1] ^ (index & 1)
            group = ids[2] ^ ((index >> 1) & 1)
            member = ids[3] ^ ((index >> 2) & 1)
            for j in range(planes):
                block = (ids[0] ^ j) * SIDES + side
                rows = pl.ds(pl.multiple_of(block * tok_dev + member * half, half), half)
                for kind in range(2):
                    columns = pl.ds(pl.multiple_of((kind * KVG + group) * DH, DH), DH)
                    grads[rows, columns] = piece[
                        j * half : (j + 1) * half, kind * DH : (kind + 1) * DH
                    ]
        acc[...] = jnp.zeros_like(acc)

    for r in range(count):
        spot = mine + r
        spot = jnp.where(spot >= count, spot - count, spot)
        block = jnp.where(spot < planes, spot * SIDES, (count - 1 - spot) * SIDES + 1)
        columns = pl.ds(pl.multiple_of(block * tok_dev, tok_dev), tok_dev)
        if r == count // 2:
            tile = jnp.where(step < steps // 2, turned[r][...], turned[count][...])
        else:
            tile = turned[r][...]
        all_turned[:, columns] = tile
    out = jnp.dot(all_turned[...], grads[...], preferred_element_type=jnp.float32)
    raw[...] = out
    acc[...] += jnp.sum((out * out).reshape(-1, 8, out.shape[1]), axis=0)

    @pl.when(step == steps - 1)
    def _():
        total = jnp.sum(acc[...], axis=0, keepdims=True)
        row = lax.broadcasted_iota(jnp.int32, sums.shape, 0)
        sums[...] = jnp.where(row == 0, total, squares[...])


def scale_kernel(factor, sums, sums_1, sums_2, sums_3, raw, key_out, value_out):
    total = (sums[...] + sums_1[...]) + (sums_2[...] + sums_3[...])
    grad_norm = jnp.sqrt(total[0:1] + EPSILON)
    weight_norm = jnp.sqrt(total[1:2] + EPSILON)
    clip = jnp.minimum(1.0, factor * weight_norm / grad_norm)
    width = key_out.shape[1]
    key_out[...] = raw[:, :width] * clip[:, :width]
    value_out[...] = raw[:, width:] * clip[:, width:]


def local_small(
    queries, keys, values, out_grad, hidden, key_weight, value_weight, stretch_owner, positions
):
    tok_dev, width = queries.shape
    half = tok_dev // 2
    count = lax.axis_size("ctx")
    planes = count // SIDES
    groups = lax.axis_size("fsdp") // MEMBERS
    total = tok_dev * count
    ctx, fsdp = lax.axis_index("ctx"), lax.axis_index("fsdp")
    ids = jnp.stack([ctx // SIDES, ctx % SIDES, fsdp // MEMBERS, fsdp % MEMBERS]).astype(jnp.int32)
    bf16, f32 = jnp.bfloat16, jnp.float32
    shape = jax.ShapeDtypeStruct

    def call(kernel, ins, outs, **more):
        return pl.pallas_call(
            kernel,
            out_shape=outs,
            in_specs=ins,
            out_specs=jax.tree.map(lambda _: VMEM, outs),
            compiler_params=pltpu.CompilerParams(vmem_limit_bytes=32 * 2**20),
            **more,
        )

    def move(x, plane=0, side=0, group=0, member=0):
        pairs = []
        fs = groups * MEMBERS
        for i in range(count):
            for j in range(fs):
                p, s = i // SIDES ^ plane, i % SIDES ^ side
                g, m = j // MEMBERS ^ group, j % MEMBERS ^ member
                pairs.append((i * fs + j, (p * SIDES + s) * fs + g * MEMBERS + m))
        return lax.ppermute(x, ("ctx", "fsdp"), pairs)

    def around(x, step):
        ring = [p * SIDES for p in range(planes)] + [p * SIDES + 1 for p in reversed(range(planes))]
        pairs = [(ring[i], ring[(i + step) % count]) for i in range(count)]
        return lax.ppermute(x, "ctx", pairs)

    kv, qd = call(
        pack_kernel,
        [SMEM] + [VMEM] * 5,
        (shape((half, 2 * DH), bf16), shape((2 * tok_dev + 16, width), bf16)),
    )(ids, keys, values, queries, out_grad, positions.reshape(1, tok_dev))
    qd_side = move(qd, side=1)
    kv_all = [kv] + [move(kv, plane=j) for j in range(1, planes)]
    qd_member = move(qd, member=1)
    qd_both = move(qd_side, member=1)
    qd_all = [qd, qd_member, qd_side, qd_both]

    turned = call(turn_kernel, [VMEM], shape(hidden.shape[::-1], bf16))(hidden)
    up = down = turned
    blocks = {0: turned}
    for step in range(1, count // 2):
        up, down = around(up, 1), around(down, -1)
        blocks[count - step], blocks[step] = up, down
    middle = turned.shape[0] // 2
    blocks[count // 2] = around(up[:middle], 1)
    blocks[count] = around(down[middle:], -1)

    squares = call(square_kernel, [VMEM] * 2, shape((8, 2 * key_weight.shape[1]), f32))(
        key_weight, value_weight
    )

    tiles = SIDES * MEMBERS * width // DH
    stats = call(
        functools.partial(stats_kernel, planes),
        [SMEM] * 2 + [VMEM] * (planes + 4),
        shape((3 * tiles, tok_dev), f32),
    )(ids, stretch_owner, *kv_all, *qd_all)
    stats_all = [stats, move(stats, member=1), move(stats, side=1), move(stats, side=1, member=1)]
    outs = call(
        functools.partial(grads_kernel, planes),
        [SMEM] * 2 + [VMEM] * (planes + 8),
        tuple(shape((half, 2 * DH), bf16 if j else f32) for j in range(planes))
        + tuple(shape((tok_dev, width), bf16 if j else f32) for j in range(4)),
    )(ids, stretch_owner, *kv_all, *qd_all, *stats_all)
    kv_parts, q_parts = outs[:planes], outs[planes:]
    piece = call(sum_kernel, [VMEM] * planes, shape((half, 2 * DH), bf16))(
        kv_parts[0], *[move(kv_parts[j], plane=j) for j in range(1, planes)]
    )
    piece_all = jnp.concatenate([piece] + [move(piece, plane=j) for j in range(1, planes)], axis=0)
    near = [
        piece_all,
        move(piece_all, side=1),
        move(piece_all, group=1),
        move(piece_all, side=1, group=1),
    ]
    pieces = near + [move(part, member=1) for part in near]

    query_grad = call(sum_kernel, [VMEM] * 4, shape((tok_dev, width), bf16))(
        q_parts[0],
        move(q_parts[1], member=1),
        move(q_parts[2], side=1),
        move(q_parts[3], side=1, member=1),
    )

    columns = 2 * KVG * DH
    steps = 8
    tile = turned.shape[0] // steps
    block = pl.BlockSpec((tile, tok_dev), lambda i: (i, 0))
    low = pl.BlockSpec((tile, tok_dev), lambda i: (jnp.minimum(i, steps // 2 - 1), 0))
    high = pl.BlockSpec((tile, tok_dev), lambda i: (jnp.maximum(i - steps // 2, 0), 0))
    turned_specs = [low if r == count // 2 else block for r in range(count)] + [high]
    whole = lambda *dims: pl.BlockSpec(dims, lambda i: (0,) * len(dims))
    raw, sums = pl.pallas_call(
        functools.partial(project_kernel, planes),
        grid=(steps,),
        out_shape=(shape((turned.shape[0], columns), f32), shape((8, columns), f32)),
        in_specs=[SMEM, whole(8, columns)]
        + turned_specs
        + [whole(planes * half, 2 * DH)] * len(pieces),
        out_specs=(pl.BlockSpec((tile, columns), lambda i: (i, 0)), whole(8, columns)),
        scratch_shapes=[
            pltpu.VMEM((tile, total), bf16),
            pltpu.VMEM((total, columns), bf16),
            pltpu.VMEM((8, columns), f32),
        ],
        compiler_params=pltpu.CompilerParams(vmem_limit_bytes=32 * 2**20),
    )(ids, squares, *[blocks[r] for r in range(count + 1)], *pieces)
    sums_all = [sums, move(sums, member=1), move(sums, group=1), move(sums, group=1, member=1)]
    out_block = pl.BlockSpec((tile, columns // 2), lambda i: (i, 0))
    key_grad, value_grad = pl.pallas_call(
        functools.partial(scale_kernel, CLIP_RATE * total),
        grid=(steps,),
        out_shape=(shape((turned.shape[0], columns // 2), f32),) * 2,
        in_specs=[whole(8, columns)] * 4 + [pl.BlockSpec((tile, columns), lambda i: (i, 0))],
        out_specs=(out_block, out_block),
        compiler_params=pltpu.CompilerParams(vmem_limit_bytes=32 * 2**20),
    )(*sums_all, raw)
    return (query_grad, key_grad, value_grad)


def solution(mesh):
    ctx_count, fsdp_count = mesh.shape["ctx"], mesh.shape["fsdp"]

    def program(queries, keys, values, out_grad, hidden, *rest):
        tok_dev = queries.shape[0] // ctx_count
        heads = queries.shape[1] // fsdp_count // DH
        gathered = hidden.size // fsdp_count * hidden.dtype.itemsize
        planes = ctx_count // SIDES
        small = (
            gathered <= GATHER_LIMIT
            and planes * SIDES == ctx_count
            and planes & (planes - 1) == 0
            and heads * MEMBERS == HPG
            and fsdp_count == KVG * MEMBERS
            and tok_dev == DH
        )
        return jax.shard_map(
            local_small if small else local_large,
            mesh=mesh,
            in_specs=(
                P("ctx", "fsdp"),
                P("ctx", None),
                P("ctx", None),
                P("ctx", "fsdp"),
                P("ctx", "fsdp"),
                P("fsdp", None),
                P("fsdp", None),
                P(),
                P("ctx"),
            ),
            out_specs=(P("ctx", "fsdp"), P("fsdp", None), P("fsdp", None)),
            check_vma=False,
        )(queries, keys, values, out_grad, hidden, *rest)

    return program
```

```python
import functools
import math

import jax
import jax.numpy as jnp
from jax import lax
from jax.experimental import pallas as pl
from jax.experimental.pallas import tpu as pltpu
from jax.sharding import PartitionSpec as P

DH = 128
HPG = 8
KVG = 2


CLIP_RATE = 0.02
EPSILON = 1e-06
NEGATIVE = -1e30
GATHER_LIMIT = 8 * 2**20

CONTRACT_LAST = (((1,), (1,)), ((), ()))
CONTRACT_FIRST = (((0,), (0,)), ((), ()))
VMEM = pl.BlockSpec(memory_space=pltpu.VMEM)
SMEM = pl.BlockSpec(memory_space=pltpu.SMEM)
ANY = pl.BlockSpec(memory_space=pl.ANY)


def rows_by_head(block, heads, width):
    count = block.shape[0]
    return block.reshape(count, heads, width).transpose(1, 0, 2).reshape(heads * count, width)


def local_large(
    queries, keys, values, out_grad, hidden, key_weight, value_weight, stretch_owner, positions
):
    tok_dev = queries.shape[0]
    heads = queries.shape[1] // DH
    ctx_count = lax.axis_size("ctx")
    total = tok_dev * ctx_count
    half = tok_dev // 2
    ctx_index = lax.axis_index("ctx")
    group = lax.axis_index("fsdp") * heads // HPG
    scale = 1.0 / math.sqrt(DH)
    block = min(512, total)
    blocks = total // block
    query_count = heads * tok_dev
    own_keys = lax.dynamic_slice_in_dim(keys, group * DH, DH, 1)
    own_values = lax.dynamic_slice_in_dim(values, group * DH, DH, 1)
    all_keys, all_values = (
        lax.all_gather(own_keys, "ctx", axis=0, tiled=True),
        lax.all_gather(own_values, "ctx", axis=0, tiled=True),
    )
    offsets = jnp.arange(half, dtype=jnp.int32)
    stretches = jnp.stack([stretch_owner, 2 * ctx_count - 1 - stretch_owner], axis=1)
    key_place = (stretches[:, :, None] * half + offsets[None, None, :]).reshape(total)
    mine = lax.dynamic_slice_in_dim(stretches, ctx_index, 1, 0)[0]
    local_place = (mine[:, None] * half + offsets[None, :]).reshape(tok_dev)
    query_place = jnp.tile(local_place, heads)
    query_floor = jnp.tile(local_place - positions, heads)
    query_rows = rows_by_head(queries, heads, DH)
    grad_rows = rows_by_head(out_grad, heads, DH)

    def scores_at(start, width):
        key_block = lax.dynamic_slice_in_dim(all_keys, start, width, 0)
        place = lax.dynamic_slice_in_dim(key_place, start, width, 0)
        raw = (
            lax.dot_general(
                query_rows, key_block, CONTRACT_LAST, preferred_element_type=jnp.float32
            )
            * scale
        )
        seen = (place[None, :] <= query_place[:, None]) & (place[None, :] >= query_floor[:, None])
        return (jnp.where(seen, raw, NEGATIVE), seen, key_block)

    def stats_step(step, carry):
        top, mass = carry
        masked, seen, key_block = scores_at(step * block, block)
        new_top = jnp.maximum(top, jnp.max(masked, axis=1))
        weights = jnp.where(seen, jnp.exp(masked - new_top[:, None]), 0.0)
        mass = mass * jnp.exp(top - new_top) + jnp.sum(weights, axis=1)
        return (new_top, mass)

    start_top = jnp.full((query_count,), NEGATIVE, jnp.float32)
    start_mass = jnp.zeros((query_count,), jnp.float32)
    top, mass = lax.fori_loop(0, blocks, stats_step, (start_top, start_mass))
    lse = top + jnp.log(mass)

    def probs_at(start, width):
        masked, seen, key_block = scores_at(start, width)
        probs = jnp.where(seen, jnp.exp(masked - lse[:, None]), 0.0)
        value_block = lax.dynamic_slice_in_dim(all_values, start, width, 0)
        dprobs = lax.dot_general(
            grad_rows, value_block, CONTRACT_LAST, preferred_element_type=jnp.float32
        )
        return (probs, dprobs, key_block)

    def delta_step(step, acc):
        probs, dprobs, key_block = probs_at(step * block, block)
        return acc + jnp.sum(probs * dprobs, axis=1)

    delta = lax.fori_loop(0, blocks, delta_step, jnp.zeros((query_count,), jnp.float32))

    def slopes_at(start, width):
        probs, dprobs, key_block = probs_at(start, width)
        slopes = (probs * (dprobs - delta[:, None]) * scale).astype(jnp.bfloat16)
        return (probs.astype(jnp.bfloat16), slopes, key_block)

    def key_terms(probs_b, slopes):
        key_part = lax.dot_general(
            slopes, query_rows, CONTRACT_FIRST, preferred_element_type=jnp.float32
        )
        value_part = lax.dot_general(
            probs_b, grad_rows, CONTRACT_FIRST, preferred_element_type=jnp.float32
        )
        return jnp.concatenate([key_part, value_part], axis=1)

    start_query = jnp.zeros((query_count, DH), jnp.float32)

    def query_step(step, query_acc):
        probs_b, slopes, key_block = slopes_at(step * block, block)
        return query_acc + jnp.dot(slopes, key_block, preferred_element_type=jnp.float32)

    query_acc = lax.fori_loop(0, blocks, query_step, start_query)
    width = math.gcd(tok_dev * lax.axis_size("ctx"), block)

    def inner(step, acc):
        offset = step * width
        probs_b, slopes, key_block = slopes_at(offset, width)
        return lax.dynamic_update_slice_in_dim(acc, key_terms(probs_b, slopes), offset, 0)

    own_grads = lax.psum_scatter(
        lax.fori_loop(
            0,
            tok_dev * lax.axis_size("ctx") // width,
            inner,
            jnp.zeros((tok_dev * lax.axis_size("ctx"), 2 * DH), jnp.float32),
        ),
        "ctx",
        scatter_dimension=0,
        tiled=True,
    )
    query_grad = (
        query_acc.reshape(heads, tok_dev, DH)
        .transpose(1, 0, 2)
        .reshape(tok_dev, heads * DH)
        .astype(jnp.bfloat16)
    )
    members = lax.all_gather(own_grads.astype(jnp.bfloat16), "fsdp", axis=0, tiled=True).astype(
        own_grads.dtype
    )
    per_group = members.reshape(KVG, -1, tok_dev, 2 * DH).sum(axis=1)
    key_grads = (
        per_group[:, :, :DH].transpose(1, 0, 2).reshape(tok_dev, KVG * DH).astype(jnp.bfloat16)
    )
    value_grads = (
        per_group[:, :, DH:].transpose(1, 0, 2).reshape(tok_dev, KVG * DH).astype(jnp.bfloat16)
    )
    both_grads = jnp.concatenate([key_grads, value_grads], axis=1)
    columns = KVG * DH
    raw = lax.psum(
        lax.dot_general(hidden, both_grads, CONTRACT_FIRST, preferred_element_type=jnp.float32),
        "ctx",
    )
    key_f = key_weight.astype(jnp.float32)
    value_f = value_weight.astype(jnp.float32)
    grad_sq, key_sq, value_sq = lax.psum(
        (
            jnp.sum(raw * raw, axis=0),
            jnp.sum(key_f * key_f, axis=0),
            jnp.sum(value_f * value_f, axis=0),
        ),
        "fsdp",
    )
    weight_norm = jnp.sqrt(jnp.concatenate([key_sq, value_sq]) + EPSILON)
    grad_norm = jnp.sqrt(grad_sq + EPSILON)
    clipped = raw * jnp.minimum(1.0, CLIP_RATE * total * weight_norm / grad_norm)[None, :]
    return (query_grad, clipped[:, :columns], clipped[:, columns:])


SIDES = 2
MEMBERS = 2
DIGIT = 64


def pack_kernel(
    ids, keys, values, queries, out_grad, positions, hidden, kv_out, qd_out, turned, place, held, sems
):
    half = kv_out.shape[0]
    tok_dev = queries.shape[0]
    rows = pl.ds(pl.multiple_of(ids[3] * half, half), half)
    columns = pl.ds(pl.multiple_of(ids[2] * DH, DH), DH)
    copies = [
        pltpu.make_async_copy(source, target, sems.at[i])
        for i, (source, target) in enumerate(
            (
                (hidden, held),
                (positions, place),
                (keys.at[rows, columns], kv_out.at[:, :DH]),
                (values.at[rows, columns], kv_out.at[:, DH:]),
                (queries, qd_out.at[:tok_dev]),
                (out_grad, qd_out.at[tok_dev : 2 * tok_dev]),
            )
        )
    ]
    for copy in copies:
        copy.start()
    rest = qd_out.shape[1] - tok_dev
    if rest > 0:
        qd_out[2 * tok_dev :, tok_dev:] = jnp.zeros((qd_out.shape[0] - 2 * tok_dev, rest), jnp.bfloat16)
    copies[0].wait()
    turned[...] = held[...].T
    copies[1].wait()
    high = place[...] // DIGIT
    low = place[...] - high * DIGIT
    pad = jnp.zeros((qd_out.shape[0] - 2 * tok_dev - 2, tok_dev), jnp.float32)
    digits = jnp.concatenate([high.astype(jnp.float32), low.astype(jnp.float32), pad], axis=0)
    qd_out[2 * tok_dev :, :tok_dev] = digits.astype(jnp.bfloat16)
    for copy in copies[2:]:
        copy.wait()


def nothing_kernel(*refs):
    pass


def after(x, *events):
    return pl.pallas_call(
        nothing_kernel,
        out_shape=jax.ShapeDtypeStruct(x.shape, x.dtype),
        in_specs=[ANY] * (1 + len(events)),
        out_specs=ANY,
        input_output_aliases={0: 0},
        compiler_params=pltpu.CompilerParams(vmem_limit_bytes=2**20),
    )(x, *events)


def seen_pairs(ids, owner, planes, half, qd):
    last = 2 * planes * SIDES - 1
    tok_dev = 2 * half
    key_rows = []
    row = lax.broadcasted_iota(jnp.int32, (half, tok_dev), 0)
    for j in range(planes):
        stretch = owner[(ids[0] ^ j) * SIDES + ids[1]]
        stretch = jnp.where(ids[3] == 0, stretch, last - stretch)
        key_rows.append(row + stretch * half)
    key_place = jnp.concatenate(key_rows, axis=0)
    lane = lax.broadcasted_iota(jnp.int32, (1, tok_dev), 1)
    seen = []
    for side in range(SIDES):
        stretch = owner[ids[0] * SIDES + (ids[1] ^ side)]
        place = jnp.where(lane < half, lane + stretch * half, lane - half + (last - stretch) * half)
        digits = qd[side * MEMBERS][2 * tok_dev :, :tok_dev].astype(jnp.float32)
        back = (digits[0:1] * DIGIT + digits[1:2]).astype(jnp.int32)
        seen.append((key_place <= place) & (key_place >= place - back))
    return seen


def scaled_scores(k, q, scale):
    return lax.dot_general(k, q, CONTRACT_LAST, preferred_element_type=jnp.float32) * scale


def stats_kernel(planes, ids, owner, *refs):
    kv_refs, qd, stats = refs[:planes], refs[planes : planes + SIDES * MEMBERS], refs[-1]
    half = kv_refs[0].shape[0]
    tok_dev = 2 * half
    heads = qd[0].shape[1] // DH
    scale = 1.0 / math.sqrt(DH)
    kv = jnp.concatenate([ref[...] for ref in kv_refs], axis=0)
    k, v = kv[:, :DH], kv[:, DH:]
    seen = seen_pairs(ids, owner, planes, half, qd)
    tiles = SIDES * MEMBERS * heads
    for source in range(SIDES * MEMBERS):
        for head in range(heads):
            q = qd[source][:tok_dev, head * DH : (head + 1) * DH]
            d = qd[source][tok_dev : 2 * tok_dev, head * DH : (head + 1) * DH]
            mask = seen[source // MEMBERS]
            scores = jnp.where(mask, scaled_scores(k, q, scale), NEGATIVE)
            dprobs = lax.dot_general(v, d, CONTRACT_LAST, preferred_element_type=jnp.float32)
            top = jnp.max(scores, axis=0, keepdims=True)
            weights = jnp.where(mask, jnp.exp(scores - top), 0.0)
            tile = source * heads + head
            stats[tile : tile + 1] = top
            stats[tiles + tile : tiles + tile + 1] = jnp.sum(weights, axis=0, keepdims=True)
            stats[2 * tiles + tile : 2 * tiles + tile + 1] = jnp.sum(
                weights * dprobs, axis=0, keepdims=True
            )


def grads_kernel(planes, ids, owner, *refs):
    sources = SIDES * MEMBERS
    kv_refs, refs = refs[:planes], refs[planes:]
    qd, refs = refs[:sources], refs[sources:]
    stats, refs = refs[:sources], refs[sources:]
    kv_out, slopes_out = refs[:planes], refs[planes]
    half = kv_refs[0].shape[0]
    tok_dev = 2 * half
    heads = qd[0].shape[1] // DH
    scale = 1.0 / math.sqrt(DH)
    kv = jnp.concatenate([ref[...] for ref in kv_refs], axis=0)
    k, v = kv[:, :DH], kv[:, DH:]
    seen = seen_pairs(ids, owner, planes, half, qd)
    tiles = sources * heads
    key_acc = jnp.zeros((planes * half, DH), jnp.float32)
    value_acc = jnp.zeros((planes * half, DH), jnp.float32)
    for source in range(sources):
        q_rows, d_rows, slope_tiles, prob_tiles = [], [], [], []
        mask = seen[source // MEMBERS]
        first = source * heads
        parts = [
            [
                stats[other][kind * tiles + (source ^ other) * heads :][:heads]
                for other in range(sources)
            ]
            for kind in range(3)
        ]
        top = functools.reduce(jnp.maximum, parts[0])
        shares = [jnp.exp(part - top) for part in parts[0]]
        mass = sum(share * part for share, part in zip(shares, parts[1], strict=True))
        lse = top + jnp.log(mass)
        delta = sum(share * part for share, part in zip(shares, parts[2], strict=True)) / mass
        for head in range(heads):
            q = qd[source][:tok_dev, head * DH : (head + 1) * DH]
            d = qd[source][tok_dev : 2 * tok_dev, head * DH : (head + 1) * DH]
            scores = scaled_scores(k, q, scale)
            dprobs = lax.dot_general(v, d, CONTRACT_LAST, preferred_element_type=jnp.float32)
            probs = jnp.where(mask, jnp.exp(scores - lse[head : head + 1]), 0.0)
            slopes = (probs * (dprobs - delta[head : head + 1]) * scale).astype(jnp.bfloat16)
            q_rows.append(q)
            d_rows.append(d)
            slope_tiles.append(slopes)
            prob_tiles.append(probs.astype(jnp.bfloat16))
        slope_tile = jnp.concatenate(slope_tiles, axis=1)
        slopes_out[source] = slope_tile
        key_acc += jnp.dot(
            slope_tile,
            jnp.concatenate(q_rows, axis=0),
            preferred_element_type=jnp.float32,
        )
        value_acc += jnp.dot(
            jnp.concatenate(prob_tiles, axis=1),
            jnp.concatenate(d_rows, axis=0),
            preferred_element_type=jnp.float32,
        )
    for j in range(planes):
        kv_out[j][:, :DH] = key_acc[j * half : (j + 1) * half].astype(kv_out[j].dtype)
        kv_out[j][:, DH:] = value_acc[j * half : (j + 1) * half].astype(kv_out[j].dtype)


def query_kernel(planes, *refs):
    kv_refs, slopes, q_out = refs[:planes], refs[planes], refs[planes + 2 :]
    k = jnp.concatenate([ref[:, :DH] for ref in kv_refs], axis=0)
    for source, out in enumerate(q_out):
        tok_dev, width = out.shape
        for head in range(width // DH):
            tile = slopes[source, :, head * tok_dev : (head + 1) * tok_dev]
            part = lax.dot_general(tile, k, CONTRACT_FIRST, preferred_element_type=jnp.float32)
            out[:, head * DH : (head + 1) * DH] = part.astype(out.dtype)


def join_kernel(*refs):
    rows = refs[0].shape[0]
    for i, ref in enumerate(refs[:-1]):
        refs[-1][i * rows : (i + 1) * rows] = ref[...]


def sum_kernel(*refs):
    total = refs[0][...].astype(jnp.float32)
    for ref in refs[1:-1]:
        total += ref[...].astype(jnp.float32)
    refs[-1][...] = total.astype(refs[-1].dtype)


def square_kernel(key_weight, value_weight, out):
    width = key_weight.shape[1]

    @pl.when(pl.program_id(0) == 0)
    def _():
        out[...] = jnp.zeros_like(out)

    k = key_weight[...].astype(jnp.float32)
    v = value_weight[...].astype(jnp.float32)
    out[:, :width] += jnp.sum((k * k).reshape(-1, 8, width), axis=0)
    out[:, width:] += jnp.sum((v * v).reshape(-1, 8, width), axis=0)


def project_kernel(planes, steps, ids, squares, turned, *refs):
    count = planes * SIDES
    pieces, (raw, sums, grads, held, sems) = refs[:8], refs[8:]
    tok_dev = turned.shape[2]
    half = tok_dev // 2
    tile = raw.shape[0] // steps
    copies = [
        pltpu.make_async_copy(turned.at[:, rows], held.at[:, rows], sems.at[i])
        for i, rows in enumerate(pl.ds(i * tile, tile) for i in range(steps))
    ]
    for copy in copies:
        copy.start()
    for index, piece in enumerate(pieces):
        side = ids[1] ^ (index & 1)
        group = ids[2] ^ ((index >> 1) & 1)
        member = ids[3] ^ ((index >> 2) & 1)
        for j in range(planes):
            plane = ids[0] ^ j
            spot = jnp.where(side == 0, plane, count - 1 - plane)
            rows = pl.ds(pl.multiple_of(spot * tok_dev + member * half, half), half)
            for kind in range(2):
                columns = pl.ds(pl.multiple_of((kind * KVG + group) * DH, DH), DH)
                grads[rows, columns] = piece[
                    j * half : (j + 1) * half, kind * DH : (kind + 1) * DH
                ]
    width = raw.shape[1]
    acc = jnp.zeros((8, width), jnp.float32)
    for i in range(steps):
        copies[i].wait()
        rows = slice(i * tile, (i + 1) * tile)
        block = jnp.concatenate([held[spot, rows] for spot in range(count)], axis=1)
        out = jnp.dot(block, grads[...], preferred_element_type=jnp.float32)
        raw[rows] = out
        acc += jnp.sum((out * out).reshape(-1, 8, width), axis=0)
    total = jnp.sum(acc, axis=0, keepdims=True)
    weights = jnp.sum(squares[...], axis=0, keepdims=True)
    row = lax.broadcasted_iota(jnp.int32, sums.shape, 0)
    sums[...] = jnp.where(row == 0, total, weights)


def scale_kernel(factor, steps, sums, sums_1, sums_2, sums_3, raw, *refs):
    outs, helds, sems = refs[:2], refs[2:4], refs[4]
    total = (sums[...] + sums_1[...]) + (sums_2[...] + sums_3[...])
    grad_norm = jnp.sqrt(total[0:1] + EPSILON)
    weight_norm = jnp.sqrt(total[1:2] + EPSILON)
    clip = jnp.minimum(1.0, factor * weight_norm / grad_norm)
    width = outs[0].shape[1]
    tile = raw.shape[0] // steps
    copies = []
    for i in range(steps):
        rows = pl.ds(i * tile, tile)
        for kind, (out, held) in enumerate(zip(outs, helds, strict=True)):
            columns = slice(kind * width, (kind + 1) * width)
            held[rows] = raw[rows, columns] * clip[:, columns]
            copy = pltpu.make_async_copy(held.at[rows], out.at[rows], sems.at[2 * i + kind])
            copy.start()
            copies.append(copy)
    for copy in copies:
        copy.wait()


def local_small(
    queries, keys, values, out_grad, hidden, key_weight, value_weight, stretch_owner, positions
):
    tok_dev, width = queries.shape
    half = tok_dev // 2
    count = lax.axis_size("ctx")
    planes = count // SIDES
    groups = lax.axis_size("fsdp") // MEMBERS
    total = tok_dev * count
    ctx, fsdp = lax.axis_index("ctx"), lax.axis_index("fsdp")
    ids = jnp.stack([ctx // SIDES, ctx % SIDES, fsdp // MEMBERS, fsdp % MEMBERS]).astype(jnp.int32)
    bf16, f32 = jnp.bfloat16, jnp.float32
    shape = jax.ShapeDtypeStruct

    def call(kernel, ins, outs, mib=8, **more):
        return pl.pallas_call(
            kernel,
            out_shape=outs,
            in_specs=ins,
            out_specs=jax.tree.map(lambda _: VMEM, outs),
            compiler_params=pltpu.CompilerParams(vmem_limit_bytes=mib * 2**20),
            **more,
        )

    def move(x, plane=0, side=0, group=0, member=0):
        pairs = []
        fs = groups * MEMBERS
        for i in range(count):
            for j in range(fs):
                p, s = i // SIDES ^ plane, i % SIDES ^ side
                g, m = j // MEMBERS ^ group, j % MEMBERS ^ member
                pairs.append((i * fs + j, (p * SIDES + s) * fs + g * MEMBERS + m))
        return lax.ppermute(x, ("ctx", "fsdp"), pairs)

    far = [
        pltpu.with_memory_space_constraint(x, pltpu.HBM)
        for x in (keys, values, queries, out_grad, positions.reshape(1, tok_dev), hidden)
    ]
    kv, qd, turned = call(
        pack_kernel,
        [SMEM] + [ANY] * 6,
        (
            shape((half, 2 * DH), bf16),
            shape((2 * tok_dev + 16, width), bf16),
            shape(hidden.shape[::-1], bf16),
        ),
        scratch_shapes=[
            pltpu.VMEM((1, tok_dev), jnp.int32),
            pltpu.VMEM(hidden.shape, bf16),
            pltpu.SemaphoreType.DMA((6,)),
        ],
    )(ids, *far)
    qd_side = move(qd, side=1)
    kv_all = [kv] + [move(kv, plane=j) for j in range(1, planes)]
    qd_member = move(qd, member=1)
    qd_side = after(qd_side, qd_member, *kv_all)
    qd_both = move(qd_side, member=1)
    qd_all = [qd, qd_member, qd_side, qd_both]

    ring = [p * SIDES for p in range(planes)] + [p * SIDES + 1 for p in reversed(range(planes))]
    turned = lax.all_gather(turned, "ctx", axis_index_groups=[ring])
    rows = turned.shape[1]

    columns = 2 * KVG * DH
    steps = 8
    tile = rows // steps
    weight = pl.BlockSpec((tile, columns // 2), lambda i: (i, 0))
    squares = pl.pallas_call(
        square_kernel,
        grid=(steps,),
        out_shape=shape((8, columns), f32),
        in_specs=[weight] * 2,
        out_specs=pl.BlockSpec((8, columns), lambda i: (0, 0)),
        compiler_params=pltpu.CompilerParams(vmem_limit_bytes=8 * 2**20),
    )(key_weight, value_weight)

    tiles = SIDES * MEMBERS * width // DH
    stats = call(
        functools.partial(stats_kernel, planes),
        [SMEM] * 2 + [VMEM] * (planes + 4),
        shape((3 * tiles, tok_dev), f32),
    )(ids, stretch_owner, *kv_all, *qd_all)
    stats_all = [stats, move(stats, member=1), move(stats, side=1), move(stats, side=1, member=1)]
    outs = call(
        functools.partial(grads_kernel, planes),
        [SMEM] * 2 + [VMEM] * (planes + 8),
        tuple(shape((half, 2 * DH), bf16 if j else f32) for j in range(planes))
        + (shape((4, planes * half, tok_dev * width // DH), bf16),),
    )(ids, stretch_owner, *kv_all, *qd_all, *stats_all)
    kv_parts, slopes = outs[:planes], outs[planes]
    piece = call(sum_kernel, [VMEM] * planes, shape((half, 2 * DH), bf16))(
        kv_parts[0], *[move(kv_parts[j], plane=j) for j in range(1, planes)]
    )
    piece_all = call(join_kernel, [VMEM] * planes, shape((planes * half, 2 * DH), bf16))(
        piece, *[move(piece, plane=j) for j in range(1, planes)]
    )
    near = [
        piece_all,
        move(piece_all, side=1),
        move(piece_all, group=1),
        move(piece_all, side=1, group=1),
    ]
    pieces = near + [move(part, member=1) for part in near]

    q_parts = call(
        functools.partial(query_kernel, planes),
        [VMEM] * (planes + 1) + [ANY],
        tuple(shape((tok_dev, width), bf16 if j else f32) for j in range(4)),
    )(*kv_all, slopes, pieces[-1])
    query_grad = call(sum_kernel, [VMEM] * 4, shape((tok_dev, width), bf16))(
        q_parts[0],
        move(q_parts[1], member=1),
        move(q_parts[2], side=1),
        move(q_parts[3], side=1, member=1),
    )

    steps = 4
    raw, sums = call(
        functools.partial(project_kernel, planes, steps),
        [SMEM, VMEM, ANY] + [VMEM] * len(pieces),
        (pltpu.VMEM((rows, columns), f32), shape((8, columns), f32)),
        mib=24,
        scratch_shapes=[
            pltpu.VMEM((total, columns), bf16),
            pltpu.VMEM(turned.shape, bf16),
            pltpu.SemaphoreType.DMA((steps,)),
        ],
    )(ids, squares, pltpu.with_memory_space_constraint(turned, pltpu.HBM), *pieces)
    sums_all = [sums, move(sums, member=1), move(sums, group=1), move(sums, group=1, member=1)]
    steps = 8
    key_grad, value_grad = pl.pallas_call(
        functools.partial(scale_kernel, CLIP_RATE * total, steps),
        out_shape=(shape((rows, columns // 2), f32),) * 2,
        in_specs=[VMEM] * 5,
        out_specs=(ANY, ANY),
        scratch_shapes=[pltpu.VMEM((rows, columns // 2), f32)] * 2
        + [pltpu.SemaphoreType.DMA((2 * steps,))],
        compiler_params=pltpu.CompilerParams(vmem_limit_bytes=24 * 2**20),
    )(*sums_all, pltpu.with_memory_space_constraint(raw, pltpu.VMEM))
    return (query_grad, key_grad, value_grad)


def solution(mesh):
    ctx_count, fsdp_count = mesh.shape["ctx"], mesh.shape["fsdp"]

    def program(queries, keys, values, out_grad, hidden, *rest):
        tok_dev = queries.shape[0] // ctx_count
        heads = queries.shape[1] // fsdp_count // DH
        gathered = hidden.size // fsdp_count * hidden.dtype.itemsize
        planes = ctx_count // SIDES
        small = (
            gathered <= GATHER_LIMIT
            and planes * SIDES == ctx_count
            and planes & (planes - 1) == 0
            and heads * MEMBERS == HPG
            and fsdp_count == KVG * MEMBERS
            and tok_dev == DH
        )
        return jax.shard_map(
            local_small if small else local_large,
            mesh=mesh,
            in_specs=(
                P("ctx", "fsdp"),
                P("ctx", None),
                P("ctx", None),
                P("ctx", "fsdp"),
                P("ctx", "fsdp"),
                P("fsdp", None),
                P("fsdp", None),
                P(),
                P("ctx"),
            ),
            out_specs=(P("ctx", "fsdp"), P("fsdp", None), P("fsdp", None)),
            check_vma=False,
        )(queries, keys, values, out_grad, hidden, *rest)

    return program
```

```python
import functools
import math

import jax
import jax.numpy as jnp
from jax import lax
from jax.experimental import pallas as pl
from jax.experimental.pallas import tpu as pltpu
from jax.sharding import PartitionSpec as P

DH = 128
HPG = 8
KVG = 2


CLIP_RATE = 0.02
EPSILON = 1e-06
NEGATIVE = -1e30
GATHER_LIMIT = 8 * 2**20

CONTRACT_LAST = (((1,), (1,)), ((), ()))
CONTRACT_FIRST = (((0,), (0,)), ((), ()))
VMEM = pl.BlockSpec(memory_space=pltpu.VMEM)
SMEM = pl.BlockSpec(memory_space=pltpu.SMEM)
ANY = pl.BlockSpec(memory_space=pl.ANY)


def rows_by_head(block, heads, width):
    count = block.shape[0]
    return block.reshape(count, heads, width).transpose(1, 0, 2).reshape(heads * count, width)


def local_large(
    queries, keys, values, out_grad, hidden, key_weight, value_weight, stretch_owner, positions
):
    tok_dev = queries.shape[0]
    heads = queries.shape[1] // DH
    ctx_count = lax.axis_size("ctx")
    total = tok_dev * ctx_count
    half = tok_dev // 2
    ctx_index = lax.axis_index("ctx")
    group = lax.axis_index("fsdp") * heads // HPG
    scale = 1.0 / math.sqrt(DH)
    block = min(512, total)
    blocks = total // block
    query_count = heads * tok_dev
    own_keys = lax.dynamic_slice_in_dim(keys, group * DH, DH, 1)
    own_values = lax.dynamic_slice_in_dim(values, group * DH, DH, 1)
    all_keys, all_values = (
        lax.all_gather(own_keys, "ctx", axis=0, tiled=True),
        lax.all_gather(own_values, "ctx", axis=0, tiled=True),
    )
    offsets = jnp.arange(half, dtype=jnp.int32)
    stretches = jnp.stack([stretch_owner, 2 * ctx_count - 1 - stretch_owner], axis=1)
    key_place = (stretches[:, :, None] * half + offsets[None, None, :]).reshape(total)
    mine = lax.dynamic_slice_in_dim(stretches, ctx_index, 1, 0)[0]
    local_place = (mine[:, None] * half + offsets[None, :]).reshape(tok_dev)
    query_place = jnp.tile(local_place, heads)
    query_floor = jnp.tile(local_place - positions, heads)
    query_rows = rows_by_head(queries, heads, DH)
    grad_rows = rows_by_head(out_grad, heads, DH)

    def scores_at(start, width):
        key_block = lax.dynamic_slice_in_dim(all_keys, start, width, 0)
        place = lax.dynamic_slice_in_dim(key_place, start, width, 0)
        raw = (
            lax.dot_general(
                query_rows, key_block, CONTRACT_LAST, preferred_element_type=jnp.float32
            )
            * scale
        )
        seen = (place[None, :] <= query_place[:, None]) & (place[None, :] >= query_floor[:, None])
        return (jnp.where(seen, raw, NEGATIVE), seen, key_block)

    def stats_step(step, carry):
        top, mass = carry
        masked, seen, key_block = scores_at(step * block, block)
        new_top = jnp.maximum(top, jnp.max(masked, axis=1))
        weights = jnp.where(seen, jnp.exp(masked - new_top[:, None]), 0.0)
        mass = mass * jnp.exp(top - new_top) + jnp.sum(weights, axis=1)
        return (new_top, mass)

    start_top = jnp.full((query_count,), NEGATIVE, jnp.float32)
    start_mass = jnp.zeros((query_count,), jnp.float32)
    top, mass = lax.fori_loop(0, blocks, stats_step, (start_top, start_mass))
    lse = top + jnp.log(mass)

    def probs_at(start, width):
        masked, seen, key_block = scores_at(start, width)
        probs = jnp.where(seen, jnp.exp(masked - lse[:, None]), 0.0)
        value_block = lax.dynamic_slice_in_dim(all_values, start, width, 0)
        dprobs = lax.dot_general(
            grad_rows, value_block, CONTRACT_LAST, preferred_element_type=jnp.float32
        )
        return (probs, dprobs, key_block)

    def delta_step(step, acc):
        probs, dprobs, key_block = probs_at(step * block, block)
        return acc + jnp.sum(probs * dprobs, axis=1)

    delta = lax.fori_loop(0, blocks, delta_step, jnp.zeros((query_count,), jnp.float32))

    def slopes_at(start, width):
        probs, dprobs, key_block = probs_at(start, width)
        slopes = (probs * (dprobs - delta[:, None]) * scale).astype(jnp.bfloat16)
        return (probs.astype(jnp.bfloat16), slopes, key_block)

    def key_terms(probs_b, slopes):
        key_part = lax.dot_general(
            slopes, query_rows, CONTRACT_FIRST, preferred_element_type=jnp.float32
        )
        value_part = lax.dot_general(
            probs_b, grad_rows, CONTRACT_FIRST, preferred_element_type=jnp.float32
        )
        return jnp.concatenate([key_part, value_part], axis=1)

    start_query = jnp.zeros((query_count, DH), jnp.float32)

    def query_step(step, query_acc):
        probs_b, slopes, key_block = slopes_at(step * block, block)
        return query_acc + jnp.dot(slopes, key_block, preferred_element_type=jnp.float32)

    query_acc = lax.fori_loop(0, blocks, query_step, start_query)
    width = math.gcd(tok_dev * lax.axis_size("ctx"), block)

    def inner(step, acc):
        offset = step * width
        probs_b, slopes, key_block = slopes_at(offset, width)
        return lax.dynamic_update_slice_in_dim(acc, key_terms(probs_b, slopes), offset, 0)

    own_grads = lax.psum_scatter(
        lax.fori_loop(
            0,
            tok_dev * lax.axis_size("ctx") // width,
            inner,
            jnp.zeros((tok_dev * lax.axis_size("ctx"), 2 * DH), jnp.float32),
        ),
        "ctx",
        scatter_dimension=0,
        tiled=True,
    )
    query_grad = (
        query_acc.reshape(heads, tok_dev, DH)
        .transpose(1, 0, 2)
        .reshape(tok_dev, heads * DH)
        .astype(jnp.bfloat16)
    )
    members = lax.all_gather(own_grads.astype(jnp.bfloat16), "fsdp", axis=0, tiled=True).astype(
        own_grads.dtype
    )
    per_group = members.reshape(KVG, -1, tok_dev, 2 * DH).sum(axis=1)
    key_grads = (
        per_group[:, :, :DH].transpose(1, 0, 2).reshape(tok_dev, KVG * DH).astype(jnp.bfloat16)
    )
    value_grads = (
        per_group[:, :, DH:].transpose(1, 0, 2).reshape(tok_dev, KVG * DH).astype(jnp.bfloat16)
    )
    both_grads = jnp.concatenate([key_grads, value_grads], axis=1)
    columns = KVG * DH
    raw = lax.psum(
        lax.dot_general(hidden, both_grads, CONTRACT_FIRST, preferred_element_type=jnp.float32),
        "ctx",
    )
    key_f = key_weight.astype(jnp.float32)
    value_f = value_weight.astype(jnp.float32)
    grad_sq, key_sq, value_sq = lax.psum(
        (
            jnp.sum(raw * raw, axis=0),
            jnp.sum(key_f * key_f, axis=0),
            jnp.sum(value_f * value_f, axis=0),
        ),
        "fsdp",
    )
    weight_norm = jnp.sqrt(jnp.concatenate([key_sq, value_sq]) + EPSILON)
    grad_norm = jnp.sqrt(grad_sq + EPSILON)
    clipped = raw * jnp.minimum(1.0, CLIP_RATE * total * weight_norm / grad_norm)[None, :]
    return (query_grad, clipped[:, :columns], clipped[:, columns:])


SIDES = 2
MEMBERS = 2
DIGIT = 64


def pack_kernel(
    ids, keys, values, queries, out_grad, positions, kv_out, qd_out, place, sems
):
    half = kv_out.shape[0]
    tok_dev = queries.shape[0]
    rows = pl.ds(pl.multiple_of(ids[3] * half, half), half)
    columns = pl.ds(pl.multiple_of(ids[2] * DH, DH), DH)
    copies = [
        pltpu.make_async_copy(source, target, sems.at[i])
        for i, (source, target) in enumerate(
            (
                (positions, place),
                (keys.at[rows, columns], kv_out.at[:, :DH]),
                (values.at[rows, columns], kv_out.at[:, DH:]),
                (queries, qd_out.at[:tok_dev]),
                (out_grad, qd_out.at[tok_dev : 2 * tok_dev]),
            )
        )
    ]
    for copy in copies:
        copy.start()
    rest = qd_out.shape[1] - tok_dev
    if rest > 0:
        qd_out[2 * tok_dev :, tok_dev:] = jnp.zeros((qd_out.shape[0] - 2 * tok_dev, rest), jnp.bfloat16)
    copies[0].wait()
    high = place[...] // DIGIT
    low = place[...] - high * DIGIT
    pad = jnp.zeros((qd_out.shape[0] - 2 * tok_dev - 2, tok_dev), jnp.float32)
    digits = jnp.concatenate([high.astype(jnp.float32), low.astype(jnp.float32), pad], axis=0)
    qd_out[2 * tok_dev :, :tok_dev] = digits.astype(jnp.bfloat16)
    for copy in copies[1:]:
        copy.wait()


def nothing_kernel(*refs):
    pass


def after(x, *events):
    return pl.pallas_call(
        nothing_kernel,
        out_shape=jax.ShapeDtypeStruct(x.shape, x.dtype),
        in_specs=[ANY] * (1 + len(events)),
        out_specs=ANY,
        input_output_aliases={0: 0},
        compiler_params=pltpu.CompilerParams(vmem_limit_bytes=2**20),
    )(x, *events)


def seen_pairs(ids, owner, planes, half, qd):
    last = 2 * planes * SIDES - 1
    tok_dev = 2 * half
    key_rows = []
    row = lax.broadcasted_iota(jnp.int32, (half, tok_dev), 0)
    for j in range(planes):
        stretch = owner[(ids[0] ^ j) * SIDES + ids[1]]
        stretch = jnp.where(ids[3] == 0, stretch, last - stretch)
        key_rows.append(row + stretch * half)
    key_place = jnp.concatenate(key_rows, axis=0)
    lane = lax.broadcasted_iota(jnp.int32, (1, tok_dev), 1)
    seen = []
    for side in range(SIDES):
        stretch = owner[ids[0] * SIDES + (ids[1] ^ side)]
        place = jnp.where(lane < half, lane + stretch * half, lane - half + (last - stretch) * half)
        digits = qd[side * MEMBERS][2 * tok_dev :, :tok_dev].astype(jnp.float32)
        back = (digits[0:1] * DIGIT + digits[1:2]).astype(jnp.int32)
        seen.append((key_place <= place) & (key_place >= place - back))
    return seen


def scaled_scores(k, q, scale):
    return lax.dot_general(k, q, CONTRACT_LAST, preferred_element_type=jnp.float32) * scale


def stats_kernel(planes, ids, owner, *refs):
    kv_refs, qd, stats = refs[:planes], refs[planes : planes + SIDES * MEMBERS], refs[-1]
    half = kv_refs[0].shape[0]
    tok_dev = 2 * half
    heads = qd[0].shape[1] // DH
    scale = 1.0 / math.sqrt(DH)
    kv = jnp.concatenate([ref[...] for ref in kv_refs], axis=0)
    k, v = kv[:, :DH], kv[:, DH:]
    seen = seen_pairs(ids, owner, planes, half, qd)
    tiles = SIDES * MEMBERS * heads
    for source in range(SIDES * MEMBERS):
        for head in range(heads):
            q = qd[source][:tok_dev, head * DH : (head + 1) * DH]
            d = qd[source][tok_dev : 2 * tok_dev, head * DH : (head + 1) * DH]
            mask = seen[source // MEMBERS]
            scores = jnp.where(mask, scaled_scores(k, q, scale), NEGATIVE)
            dprobs = lax.dot_general(v, d, CONTRACT_LAST, preferred_element_type=jnp.float32)
            top = jnp.max(scores, axis=0, keepdims=True)
            weights = jnp.where(mask, jnp.exp(scores - top), 0.0)
            tile = source * heads + head
            stats[tile : tile + 1] = top
            stats[tiles + tile : tiles + tile + 1] = jnp.sum(weights, axis=0, keepdims=True)
            stats[2 * tiles + tile : 2 * tiles + tile + 1] = jnp.sum(
                weights * dprobs, axis=0, keepdims=True
            )


def grads_kernel(planes, ids, owner, *refs):
    sources = SIDES * MEMBERS
    kv_refs, refs = refs[:planes], refs[planes:]
    qd, refs = refs[:sources], refs[sources:]
    stats, refs = refs[:sources], refs[sources:]
    kv_out, slopes_out = refs[:planes], refs[planes]
    half = kv_refs[0].shape[0]
    tok_dev = 2 * half
    heads = qd[0].shape[1] // DH
    scale = 1.0 / math.sqrt(DH)
    kv = jnp.concatenate([ref[...] for ref in kv_refs], axis=0)
    k, v = kv[:, :DH], kv[:, DH:]
    seen = seen_pairs(ids, owner, planes, half, qd)
    tiles = sources * heads
    key_acc = jnp.zeros((planes * half, DH), jnp.float32)
    value_acc = jnp.zeros((planes * half, DH), jnp.float32)
    for source in range(sources):
        q_rows, d_rows, slope_tiles, prob_tiles = [], [], [], []
        mask = seen[source // MEMBERS]
        first = source * heads
        parts = [
            [
                stats[other][kind * tiles + (source ^ other) * heads :][:heads]
                for other in range(sources)
            ]
            for kind in range(3)
        ]
        top = functools.reduce(jnp.maximum, parts[0])
        shares = [jnp.exp(part - top) for part in parts[0]]
        mass = sum(share * part for share, part in zip(shares, parts[1], strict=True))
        lse = top + jnp.log(mass)
        delta = sum(share * part for share, part in zip(shares, parts[2], strict=True)) / mass
        for head in range(heads):
            q = qd[source][:tok_dev, head * DH : (head + 1) * DH]
            d = qd[source][tok_dev : 2 * tok_dev, head * DH : (head + 1) * DH]
            scores = scaled_scores(k, q, scale)
            dprobs = lax.dot_general(v, d, CONTRACT_LAST, preferred_element_type=jnp.float32)
            probs = jnp.where(mask, jnp.exp(scores - lse[head : head + 1]), 0.0)
            slopes = (probs * (dprobs - delta[head : head + 1]) * scale).astype(jnp.bfloat16)
            q_rows.append(q)
            d_rows.append(d)
            slope_tiles.append(slopes)
            prob_tiles.append(probs.astype(jnp.bfloat16))
        slope_tile = jnp.concatenate(slope_tiles, axis=1)
        slopes_out[source] = slope_tile
        key_acc += jnp.dot(
            slope_tile,
            jnp.concatenate(q_rows, axis=0),
            preferred_element_type=jnp.float32,
        )
        value_acc += jnp.dot(
            jnp.concatenate(prob_tiles, axis=1),
            jnp.concatenate(d_rows, axis=0),
            preferred_element_type=jnp.float32,
        )
    for j in range(planes):
        kv_out[j][:, :DH] = key_acc[j * half : (j + 1) * half].astype(kv_out[j].dtype)
        kv_out[j][:, DH:] = value_acc[j * half : (j + 1) * half].astype(kv_out[j].dtype)


def query_kernel(planes, *refs):
    kv_refs, slopes, q_out = refs[:planes], refs[planes], refs[planes + 2 :]
    k = jnp.concatenate([ref[:, :DH] for ref in kv_refs], axis=0)
    for source, out in enumerate(q_out):
        tok_dev, width = out.shape
        for head in range(width // DH):
            tile = slopes[source, :, head * tok_dev : (head + 1) * tok_dev]
            part = lax.dot_general(tile, k, CONTRACT_FIRST, preferred_element_type=jnp.float32)
            out[:, head * DH : (head + 1) * DH] = part.astype(out.dtype)


def join_kernel(*refs):
    rows = refs[0].shape[0]
    for i, ref in enumerate(refs[:-1]):
        refs[-1][i * rows : (i + 1) * rows] = ref[...]


def sum_kernel(*refs):
    total = refs[0][...].astype(jnp.float32)
    for ref in refs[1:-1]:
        total += ref[...].astype(jnp.float32)
    refs[-1][...] = total.astype(refs[-1].dtype)


def square_kernel(key_weight, value_weight, out):
    width = key_weight.shape[1]

    @pl.when(pl.program_id(0) == 0)
    def _():
        out[...] = jnp.zeros_like(out)

    k = key_weight[...].astype(jnp.float32)
    v = value_weight[...].astype(jnp.float32)
    out[:, :width] += jnp.sum((k * k).reshape(-1, 8, width), axis=0)
    out[:, width:] += jnp.sum((v * v).reshape(-1, 8, width), axis=0)


def project_kernel(planes, steps, ids, squares, hidden, *refs):
    count = planes * SIDES
    pieces, (raw, sums, grads, held, sems) = refs[:8], refs[8:]
    tok_dev = hidden.shape[1]
    half = tok_dev // 2
    tile = raw.shape[0] // steps
    copies = [
        pltpu.make_async_copy(hidden.at[:, :, rows], held.at[:, :, rows], sems.at[i])
        for i, rows in enumerate(pl.ds(i * tile, tile) for i in range(steps))
    ]
    for copy in copies:
        copy.start()
    for index, piece in enumerate(pieces):
        side = ids[1] ^ (index & 1)
        group = ids[2] ^ ((index >> 1) & 1)
        member = ids[3] ^ ((index >> 2) & 1)
        for j in range(planes):
            plane = ids[0] ^ j
            spot = jnp.where(side == 0, plane, count - 1 - plane)
            rows = pl.ds(pl.multiple_of(spot * tok_dev + member * half, half), half)
            for kind in range(2):
                columns = pl.ds(pl.multiple_of((kind * KVG + group) * DH, DH), DH)
                grads[rows, columns] = piece[
                    j * half : (j + 1) * half, kind * DH : (kind + 1) * DH
                ]
    width = raw.shape[1]
    acc = jnp.zeros((8, width), jnp.float32)
    for i in range(steps):
        copies[i].wait()
        rows = slice(i * tile, (i + 1) * tile)
        block = held[:, :, rows].reshape(count * tok_dev, tile)
        out = lax.dot_general(
            block, grads[...], CONTRACT_FIRST, preferred_element_type=jnp.float32
        )
        raw[rows] = out
        acc += jnp.sum((out * out).reshape(-1, 8, width), axis=0)
    total = jnp.sum(acc, axis=0, keepdims=True)
    weights = jnp.sum(squares[...], axis=0, keepdims=True)
    row = lax.broadcasted_iota(jnp.int32, sums.shape, 0)
    sums[...] = jnp.where(row == 0, total, weights)


def scale_kernel(factor, steps, sums, sums_1, sums_2, sums_3, raw, *refs):
    outs, helds, sems = refs[:2], refs[2:4], refs[4]
    total = (sums[...] + sums_1[...]) + (sums_2[...] + sums_3[...])
    grad_norm = jnp.sqrt(total[0:1] + EPSILON)
    weight_norm = jnp.sqrt(total[1:2] + EPSILON)
    clip = jnp.minimum(1.0, factor * weight_norm / grad_norm)
    width = outs[0].shape[1]
    tile = raw.shape[0] // steps
    copies = []
    for i in range(steps):
        rows = pl.ds(i * tile, tile)
        for kind, (out, held) in enumerate(zip(outs, helds, strict=True)):
            columns = slice(kind * width, (kind + 1) * width)
            held[rows] = raw[rows, columns] * clip[:, columns]
            copy = pltpu.make_async_copy(held.at[rows], out.at[rows], sems.at[2 * i + kind])
            copy.start()
            copies.append(copy)
    for copy in copies:
        copy.wait()


def local_small(
    queries, keys, values, out_grad, hidden, key_weight, value_weight, stretch_owner, positions
):
    tok_dev, width = queries.shape
    half = tok_dev // 2
    count = lax.axis_size("ctx")
    planes = count // SIDES
    groups = lax.axis_size("fsdp") // MEMBERS
    total = tok_dev * count
    ctx, fsdp = lax.axis_index("ctx"), lax.axis_index("fsdp")
    ids = jnp.stack([ctx // SIDES, ctx % SIDES, fsdp // MEMBERS, fsdp % MEMBERS]).astype(jnp.int32)
    bf16, f32 = jnp.bfloat16, jnp.float32
    shape = jax.ShapeDtypeStruct

    def call(kernel, ins, outs, mib=8, **more):
        return pl.pallas_call(
            kernel,
            out_shape=outs,
            in_specs=ins,
            out_specs=jax.tree.map(lambda _: VMEM, outs),
            compiler_params=pltpu.CompilerParams(vmem_limit_bytes=mib * 2**20),
            **more,
        )

    def move(x, plane=0, side=0, group=0, member=0):
        pairs = []
        fs = groups * MEMBERS
        for i in range(count):
            for j in range(fs):
                p, s = i // SIDES ^ plane, i % SIDES ^ side
                g, m = j // MEMBERS ^ group, j % MEMBERS ^ member
                pairs.append((i * fs + j, (p * SIDES + s) * fs + g * MEMBERS + m))
        return lax.ppermute(x, ("ctx", "fsdp"), pairs)

    ring = [p * SIDES for p in range(planes)] + [p * SIDES + 1 for p in reversed(range(planes))]
    gathered = lax.all_gather(hidden, "ctx", axis_index_groups=[ring])
    rows = hidden.shape[1]

    columns = 2 * KVG * DH
    steps = 8
    tile = rows // steps
    weight = pl.BlockSpec((tile, columns // 2), lambda i: (i, 0))
    squares = pl.pallas_call(
        square_kernel,
        grid=(steps,),
        out_shape=shape((8, columns), f32),
        in_specs=[weight] * 2,
        out_specs=pl.BlockSpec((8, columns), lambda i: (0, 0)),
        compiler_params=pltpu.CompilerParams(vmem_limit_bytes=8 * 2**20),
    )(key_weight, value_weight)

    far = [
        pltpu.with_memory_space_constraint(x, pltpu.HBM)
        for x in (keys, values, queries, out_grad, positions.reshape(1, tok_dev))
    ]
    kv, qd = call(
        pack_kernel,
        [SMEM] + [ANY] * 5,
        (shape((half, 2 * DH), bf16), shape((2 * tok_dev + 16, width), bf16)),
        scratch_shapes=[
            pltpu.VMEM((1, tok_dev), jnp.int32),
            pltpu.SemaphoreType.DMA((5,)),
        ],
    )(ids, *far)
    qd_side = move(qd, side=1)
    kv_all = [kv] + [move(kv, plane=j) for j in range(1, planes)]
    qd_member = move(qd, member=1)
    qd_side = after(qd_side, qd_member, squares, *kv_all)
    qd_both = move(qd_side, member=1)
    qd_all = [qd, qd_member, qd_side, qd_both]

    tiles = SIDES * MEMBERS * width // DH
    stats = call(
        functools.partial(stats_kernel, planes),
        [SMEM] * 2 + [VMEM] * (planes + 4),
        shape((3 * tiles, tok_dev), f32),
    )(ids, stretch_owner, *kv_all, *qd_all)
    stats_all = [stats, move(stats, member=1), move(stats, side=1), move(stats, side=1, member=1)]
    outs = call(
        functools.partial(grads_kernel, planes),
        [SMEM] * 2 + [VMEM] * (planes + 8),
        tuple(shape((half, 2 * DH), bf16 if j else f32) for j in range(planes))
        + (shape((4, planes * half, tok_dev * width // DH), bf16),),
    )(ids, stretch_owner, *kv_all, *qd_all, *stats_all)
    kv_parts, slopes = outs[:planes], outs[planes]
    piece = call(sum_kernel, [VMEM] * planes, shape((half, 2 * DH), bf16))(
        kv_parts[0], *[move(kv_parts[j], plane=j) for j in range(1, planes)]
    )
    piece_all = call(join_kernel, [VMEM] * planes, shape((planes * half, 2 * DH), bf16))(
        piece, *[move(piece, plane=j) for j in range(1, planes)]
    )
    piece_side = move(piece_all, side=1)
    near = [piece_all, piece_side, move(piece_all, group=1), move(piece_side, group=1)]
    pieces = near + [move(part, member=1) for part in near]

    q_parts = call(
        functools.partial(query_kernel, planes),
        [VMEM] * (planes + 1) + [ANY],
        tuple(shape((tok_dev, width), bf16 if j else f32) for j in range(4)),
    )(*kv_all, slopes, near[2])
    query_grad = call(sum_kernel, [VMEM] * 4, shape((tok_dev, width), bf16))(
        q_parts[0],
        move(q_parts[1], member=1),
        move(q_parts[2], side=1),
        move(q_parts[3], side=1, member=1),
    )

    steps = 4
    raw, sums = call(
        functools.partial(project_kernel, planes, steps),
        [SMEM, VMEM, ANY] + [VMEM] * len(pieces),
        (pltpu.VMEM((rows, columns), f32), shape((8, columns), f32)),
        mib=24,
        scratch_shapes=[
            pltpu.VMEM((total, columns), bf16),
            pltpu.VMEM(gathered.shape, bf16),
            pltpu.SemaphoreType.DMA((steps,)),
        ],
    )(ids, squares, pltpu.with_memory_space_constraint(gathered, pltpu.HBM), *pieces)
    sums_all = [sums, move(sums, member=1), move(sums, group=1), move(sums, group=1, member=1)]
    steps = 8
    key_grad, value_grad = pl.pallas_call(
        functools.partial(scale_kernel, CLIP_RATE * total, steps),
        out_shape=(shape((rows, columns // 2), f32),) * 2,
        in_specs=[VMEM] * 5,
        out_specs=(ANY, ANY),
        scratch_shapes=[pltpu.VMEM((rows, columns // 2), f32)] * 2
        + [pltpu.SemaphoreType.DMA((2 * steps,))],
        compiler_params=pltpu.CompilerParams(vmem_limit_bytes=24 * 2**20),
    )(*sums_all, pltpu.with_memory_space_constraint(raw, pltpu.VMEM))
    return (query_grad, key_grad, value_grad)


def solution(mesh):
    ctx_count, fsdp_count = mesh.shape["ctx"], mesh.shape["fsdp"]

    def program(queries, keys, values, out_grad, hidden, *rest):
        tok_dev = queries.shape[0] // ctx_count
        heads = queries.shape[1] // fsdp_count // DH
        gathered = hidden.size // fsdp_count * hidden.dtype.itemsize
        planes = ctx_count // SIDES
        small = (
            gathered <= GATHER_LIMIT
            and planes * SIDES == ctx_count
            and planes & (planes - 1) == 0
            and heads * MEMBERS == HPG
            and fsdp_count == KVG * MEMBERS
            and tok_dev == DH
        )
        return jax.shard_map(
            local_small if small else local_large,
            mesh=mesh,
            in_specs=(
                P("ctx", "fsdp"),
                P("ctx", None),
                P("ctx", None),
                P("ctx", "fsdp"),
                P("ctx", "fsdp"),
                P("fsdp", None),
                P("fsdp", None),
                P(),
                P("ctx"),
            ),
            out_specs=(P("ctx", "fsdp"), P("fsdp", None), P("fsdp", None)),
            check_vma=False,
        )(queries, keys, values, out_grad, hidden, *rest)

    return program
```

```python
import functools
import math

import jax
import jax.numpy as jnp
from jax import lax
from jax.experimental import pallas as pl
from jax.experimental.pallas import tpu as pltpu
from jax.sharding import PartitionSpec as P

DH = 128
HPG = 8
KVG = 2


CLIP_RATE = 0.02
EPSILON = 1e-06
NEGATIVE = -1e30
GATHER_LIMIT = 8 * 2**20

CONTRACT_LAST = (((1,), (1,)), ((), ()))
CONTRACT_FIRST = (((0,), (0,)), ((), ()))
VMEM = pl.BlockSpec(memory_space=pltpu.VMEM)
SMEM = pl.BlockSpec(memory_space=pltpu.SMEM)
ANY = pl.BlockSpec(memory_space=pl.ANY)


def rows_by_head(block, heads, width):
    count = block.shape[0]
    return block.reshape(count, heads, width).transpose(1, 0, 2).reshape(heads * count, width)


def local_large(
    queries, keys, values, out_grad, hidden, key_weight, value_weight, stretch_owner, positions
):
    tok_dev = queries.shape[0]
    heads = queries.shape[1] // DH
    ctx_count = lax.axis_size("ctx")
    total = tok_dev * ctx_count
    half = tok_dev // 2
    ctx_index = lax.axis_index("ctx")
    group = lax.axis_index("fsdp") * heads // HPG
    scale = 1.0 / math.sqrt(DH)
    block = min(512, total)
    blocks = total // block
    query_count = heads * tok_dev
    own_keys = lax.dynamic_slice_in_dim(keys, group * DH, DH, 1)
    own_values = lax.dynamic_slice_in_dim(values, group * DH, DH, 1)
    all_keys, all_values = (
        lax.all_gather(own_keys, "ctx", axis=0, tiled=True),
        lax.all_gather(own_values, "ctx", axis=0, tiled=True),
    )
    offsets = jnp.arange(half, dtype=jnp.int32)
    stretches = jnp.stack([stretch_owner, 2 * ctx_count - 1 - stretch_owner], axis=1)
    key_place = (stretches[:, :, None] * half + offsets[None, None, :]).reshape(total)
    mine = lax.dynamic_slice_in_dim(stretches, ctx_index, 1, 0)[0]
    local_place = (mine[:, None] * half + offsets[None, :]).reshape(tok_dev)
    query_place = jnp.tile(local_place, heads)
    query_floor = jnp.tile(local_place - positions, heads)
    query_rows = rows_by_head(queries, heads, DH)
    grad_rows = rows_by_head(out_grad, heads, DH)

    def scores_at(start, width):
        key_block = lax.dynamic_slice_in_dim(all_keys, start, width, 0)
        place = lax.dynamic_slice_in_dim(key_place, start, width, 0)
        raw = (
            lax.dot_general(
                query_rows, key_block, CONTRACT_LAST, preferred_element_type=jnp.float32
            )
            * scale
        )
        seen = (place[None, :] <= query_place[:, None]) & (place[None, :] >= query_floor[:, None])
        return (jnp.where(seen, raw, NEGATIVE), seen, key_block)

    def stats_step(step, carry):
        top, mass = carry
        masked, seen, key_block = scores_at(step * block, block)
        new_top = jnp.maximum(top, jnp.max(masked, axis=1))
        weights = jnp.where(seen, jnp.exp(masked - new_top[:, None]), 0.0)
        mass = mass * jnp.exp(top - new_top) + jnp.sum(weights, axis=1)
        return (new_top, mass)

    start_top = jnp.full((query_count,), NEGATIVE, jnp.float32)
    start_mass = jnp.zeros((query_count,), jnp.float32)
    top, mass = lax.fori_loop(0, blocks, stats_step, (start_top, start_mass))
    lse = top + jnp.log(mass)

    def probs_at(start, width):
        masked, seen, key_block = scores_at(start, width)
        probs = jnp.where(seen, jnp.exp(masked - lse[:, None]), 0.0)
        value_block = lax.dynamic_slice_in_dim(all_values, start, width, 0)
        dprobs = lax.dot_general(
            grad_rows, value_block, CONTRACT_LAST, preferred_element_type=jnp.float32
        )
        return (probs, dprobs, key_block)

    def delta_step(step, acc):
        probs, dprobs, key_block = probs_at(step * block, block)
        return acc + jnp.sum(probs * dprobs, axis=1)

    delta = lax.fori_loop(0, blocks, delta_step, jnp.zeros((query_count,), jnp.float32))

    def slopes_at(start, width):
        probs, dprobs, key_block = probs_at(start, width)
        slopes = (probs * (dprobs - delta[:, None]) * scale).astype(jnp.bfloat16)
        return (probs.astype(jnp.bfloat16), slopes, key_block)

    def key_terms(probs_b, slopes):
        key_part = lax.dot_general(
            slopes, query_rows, CONTRACT_FIRST, preferred_element_type=jnp.float32
        )
        value_part = lax.dot_general(
            probs_b, grad_rows, CONTRACT_FIRST, preferred_element_type=jnp.float32
        )
        return jnp.concatenate([key_part, value_part], axis=1)

    start_query = jnp.zeros((query_count, DH), jnp.float32)

    def query_step(step, query_acc):
        probs_b, slopes, key_block = slopes_at(step * block, block)
        return query_acc + jnp.dot(slopes, key_block, preferred_element_type=jnp.float32)

    query_acc = lax.fori_loop(0, blocks, query_step, start_query)
    width = math.gcd(tok_dev * lax.axis_size("ctx"), block)

    def inner(step, acc):
        offset = step * width
        probs_b, slopes, key_block = slopes_at(offset, width)
        return lax.dynamic_update_slice_in_dim(acc, key_terms(probs_b, slopes), offset, 0)

    own_grads = lax.psum_scatter(
        lax.fori_loop(
            0,
            tok_dev * lax.axis_size("ctx") // width,
            inner,
            jnp.zeros((tok_dev * lax.axis_size("ctx"), 2 * DH), jnp.float32),
        ),
        "ctx",
        scatter_dimension=0,
        tiled=True,
    )
    query_grad = (
        query_acc.reshape(heads, tok_dev, DH)
        .transpose(1, 0, 2)
        .reshape(tok_dev, heads * DH)
        .astype(jnp.bfloat16)
    )
    members = lax.all_gather(own_grads.astype(jnp.bfloat16), "fsdp", axis=0, tiled=True).astype(
        own_grads.dtype
    )
    per_group = members.reshape(KVG, -1, tok_dev, 2 * DH).sum(axis=1)
    key_grads = (
        per_group[:, :, :DH].transpose(1, 0, 2).reshape(tok_dev, KVG * DH).astype(jnp.bfloat16)
    )
    value_grads = (
        per_group[:, :, DH:].transpose(1, 0, 2).reshape(tok_dev, KVG * DH).astype(jnp.bfloat16)
    )
    both_grads = jnp.concatenate([key_grads, value_grads], axis=1)
    columns = KVG * DH
    raw = lax.psum(
        lax.dot_general(hidden, both_grads, CONTRACT_FIRST, preferred_element_type=jnp.float32),
        "ctx",
    )
    key_f = key_weight.astype(jnp.float32)
    value_f = value_weight.astype(jnp.float32)
    grad_sq, key_sq, value_sq = lax.psum(
        (
            jnp.sum(raw * raw, axis=0),
            jnp.sum(key_f * key_f, axis=0),
            jnp.sum(value_f * value_f, axis=0),
        ),
        "fsdp",
    )
    weight_norm = jnp.sqrt(jnp.concatenate([key_sq, value_sq]) + EPSILON)
    grad_norm = jnp.sqrt(grad_sq + EPSILON)
    clipped = raw * jnp.minimum(1.0, CLIP_RATE * total * weight_norm / grad_norm)[None, :]
    return (query_grad, clipped[:, :columns], clipped[:, columns:])


SIDES = 2
MEMBERS = 2
DIGIT = 64


def pack_kernel(
    ids, keys, values, queries, out_grad, positions, hidden, kv_out, qd_out, held, place, sems
):
    tok_dev = queries.shape[0]
    columns = pl.ds(pl.multiple_of(ids[2] * DH, DH), DH)
    copies = [
        pltpu.make_async_copy(source, target, sems.at[i])
        for i, (source, target) in enumerate(
            (
                (positions, place),
                (keys.at[:, columns], kv_out.at[:, :DH]),
                (values.at[:, columns], kv_out.at[:, DH:]),
                (queries, qd_out.at[:tok_dev]),
                (out_grad, qd_out.at[tok_dev : 2 * tok_dev]),
                (hidden, held),
            )
        )
    ]
    for copy in copies:
        copy.start()
    rest = qd_out.shape[1] - tok_dev
    if rest > 0:
        qd_out[2 * tok_dev :, tok_dev:] = jnp.zeros((qd_out.shape[0] - 2 * tok_dev, rest), jnp.bfloat16)
    copies[0].wait()
    high = place[...] // DIGIT
    low = place[...] - high * DIGIT
    pad = jnp.zeros((qd_out.shape[0] - 2 * tok_dev - 2, tok_dev), jnp.float32)
    digits = jnp.concatenate([high.astype(jnp.float32), low.astype(jnp.float32), pad], axis=0)
    qd_out[2 * tok_dev :, :tok_dev] = digits.astype(jnp.bfloat16)
    for copy in copies[1:]:
        copy.wait()


def nothing_kernel(*refs):
    pass


def after(xs, *events):
    count = len(xs)
    return pl.pallas_call(
        nothing_kernel,
        out_shape=tuple(jax.ShapeDtypeStruct(x.shape, x.dtype) for x in xs),
        in_specs=[ANY] * (count + len(events)),
        out_specs=(ANY,) * count,
        input_output_aliases={i: i for i in range(count)},
        compiler_params=pltpu.CompilerParams(vmem_limit_bytes=2**20),
    )(*xs, *events)


def halves_kernel(*refs):
    up, down, (up_half, down_half, sems) = refs[0], refs[1], refs[-3:]
    half = up_half.shape[0]
    copies = [
        pltpu.make_async_copy(up.at[:half], up_half, sems.at[0]),
        pltpu.make_async_copy(down.at[half:], down_half, sems.at[1]),
    ]
    for copy in copies:
        copy.start()
    for copy in copies:
        copy.wait()


def halves_after(up, down, *events):
    half = jax.ShapeDtypeStruct((up.shape[0] // 2, up.shape[1]), up.dtype)
    return pl.pallas_call(
        halves_kernel,
        out_shape=(half, half),
        in_specs=[ANY] * (2 + len(events)),
        out_specs=(ANY, ANY),
        scratch_shapes=[pltpu.SemaphoreType.DMA((2,))],
        compiler_params=pltpu.CompilerParams(vmem_limit_bytes=2**20),
    )(up, down, *events)


def seen_pairs(ids, owner, planes, tok_dev, qd):
    last = 2 * planes * SIDES - 1
    half = tok_dev // 2

    def place_of(at, block):
        stretch = owner[block]
        return jnp.where(at < half, at + stretch * half, at - half + (last - stretch) * half)

    row = lax.broadcasted_iota(jnp.int32, (tok_dev, tok_dev), 0)
    key_place = jnp.concatenate(
        [place_of(row, (ids[0] ^ j) * SIDES + ids[1]) for j in range(planes)], axis=0
    )
    lane = lax.broadcasted_iota(jnp.int32, (1, tok_dev), 1)
    seen = []
    for side in range(SIDES):
        place = place_of(lane, ids[0] * SIDES + (ids[1] ^ side))
        digits = qd[side][2 * tok_dev :, :tok_dev].astype(jnp.float32)
        back = (digits[0:1] * DIGIT + digits[1:2]).astype(jnp.int32)
        seen.append((key_place <= place) & (key_place >= place - back))
    return seen


def scaled_scores(k, q, scale):
    return lax.dot_general(k, q, CONTRACT_LAST, preferred_element_type=jnp.float32) * scale


def stats_kernel(planes, ids, owner, *refs):
    kv_refs, qd, stats = refs[:planes], refs[planes : planes + SIDES], refs[-1]
    tok_dev = kv_refs[0].shape[0]
    heads = qd[0].shape[1] // DH
    scale = 1.0 / math.sqrt(DH)
    kv = jnp.concatenate([ref[...] for ref in kv_refs], axis=0)
    k, v = kv[:, :DH], kv[:, DH:]
    seen = seen_pairs(ids, owner, planes, tok_dev, qd)
    tiles = SIDES * heads
    for side in range(SIDES):
        for head in range(heads):
            q = qd[side][:tok_dev, head * DH : (head + 1) * DH]
            d = qd[side][tok_dev : 2 * tok_dev, head * DH : (head + 1) * DH]
            scores = jnp.where(seen[side], scaled_scores(k, q, scale), NEGATIVE)
            dprobs = lax.dot_general(v, d, CONTRACT_LAST, preferred_element_type=jnp.float32)
            top = jnp.max(scores, axis=0, keepdims=True)
            weights = jnp.where(seen[side], jnp.exp(scores - top), 0.0)
            tile = side * heads + head
            stats[tile : tile + 1] = top
            stats[tiles + tile : tiles + tile + 1] = jnp.sum(weights, axis=0, keepdims=True)
            stats[2 * tiles + tile : 2 * tiles + tile + 1] = jnp.sum(
                weights * dprobs, axis=0, keepdims=True
            )


def grads_kernel(planes, ids, owner, *refs):
    kv_refs, refs = refs[:planes], refs[planes:]
    qd, refs = refs[:SIDES], refs[SIDES:]
    stats, (keep, give, slopes_out, acc) = refs[:SIDES], refs[SIDES:]
    tok_dev = kv_refs[0].shape[0]
    half = tok_dev // 2
    heads = qd[0].shape[1] // DH
    scale = 1.0 / math.sqrt(DH)
    kv = jnp.concatenate([ref[...] for ref in kv_refs], axis=0)
    k, v = kv[:, :DH], kv[:, DH:]
    seen = seen_pairs(ids, owner, planes, tok_dev, qd)
    tiles = SIDES * heads
    key_acc = jnp.zeros((planes * tok_dev, DH), jnp.float32)
    value_acc = jnp.zeros((planes * tok_dev, DH), jnp.float32)
    for side in range(SIDES):
        q_rows, d_rows, slope_tiles, prob_tiles = [], [], [], []
        parts = [
            [
                stats[other][kind * tiles + (side ^ other) * heads :][:heads]
                for other in range(SIDES)
            ]
            for kind in range(3)
        ]
        top = functools.reduce(jnp.maximum, parts[0])
        shares = [jnp.exp(part - top) for part in parts[0]]
        mass = sum(share * part for share, part in zip(shares, parts[1], strict=True))
        lse = top + jnp.log(mass)
        delta = sum(share * part for share, part in zip(shares, parts[2], strict=True)) / mass
        for head in range(heads):
            q = qd[side][:tok_dev, head * DH : (head + 1) * DH]
            d = qd[side][tok_dev : 2 * tok_dev, head * DH : (head + 1) * DH]
            scores = scaled_scores(k, q, scale)
            dprobs = lax.dot_general(v, d, CONTRACT_LAST, preferred_element_type=jnp.float32)
            probs = jnp.where(seen[side], jnp.exp(scores - lse[head : head + 1]), 0.0)
            slopes = (probs * (dprobs - delta[head : head + 1]) * scale).astype(jnp.bfloat16)
            q_rows.append(q)
            d_rows.append(d)
            slope_tiles.append(slopes)
            prob_tiles.append(probs.astype(jnp.bfloat16))
        slope_tile = jnp.concatenate(slope_tiles, axis=1)
        slopes_out[side] = slope_tile
        key_acc += jnp.dot(
            slope_tile,
            jnp.concatenate(q_rows, axis=0),
            preferred_element_type=jnp.float32,
        )
        value_acc += jnp.dot(
            jnp.concatenate(prob_tiles, axis=1),
            jnp.concatenate(d_rows, axis=0),
            preferred_element_type=jnp.float32,
        )
    acc[:, :DH] = key_acc
    acc[:, DH:] = value_acc
    for j in range(planes):
        rows = slice(j * half, (j + 1) * half)
        own = pl.multiple_of(j * tok_dev + ids[3] * half, half)
        other = pl.multiple_of(j * tok_dev + (1 - ids[3]) * half, half)
        keep[rows] = acc[pl.ds(own, half)]
        give[rows] = acc[pl.ds(other, half)].astype(give.dtype)


def members_kernel(keep, got, *outs):
    half = outs[0].shape[0]
    for j, out in enumerate(outs):
        rows = slice(j * half, (j + 1) * half)
        out[...] = (keep[rows] + got[rows].astype(jnp.float32)).astype(out.dtype)


def query_kernel(planes, *refs):
    kv_refs, slopes, q_out = refs[:planes], refs[planes], refs[planes + 3 :]
    k = jnp.concatenate([ref[:, :DH] for ref in kv_refs], axis=0)
    for source, out in enumerate(q_out):
        tok_dev, width = out.shape
        for head in range(width // DH):
            tile = slopes[source, :, head * tok_dev : (head + 1) * tok_dev]
            part = lax.dot_general(tile, k, CONTRACT_FIRST, preferred_element_type=jnp.float32)
            out[:, head * DH : (head + 1) * DH] = part.astype(out.dtype)


def join_kernel(*refs):
    rows = refs[0].shape[0]
    for i, ref in enumerate(refs[:-1]):
        refs[-1][i * rows : (i + 1) * rows] = ref[...]


def sum_kernel(*refs):
    total = refs[0][...].astype(jnp.float32)
    for ref in refs[1:-1]:
        total += ref[...].astype(jnp.float32)
    refs[-1][...] = total.astype(refs[-1].dtype)


def square_kernel(key_weight, value_weight, out):
    width = key_weight.shape[1]

    @pl.when(pl.program_id(0) == 0)
    def _():
        out[...] = jnp.zeros_like(out)

    k = key_weight[...].astype(jnp.float32)
    v = value_weight[...].astype(jnp.float32)
    out[:, :width] += jnp.sum((k * k).reshape(-1, 8, width), axis=0)
    out[:, width:] += jnp.sum((v * v).reshape(-1, 8, width), axis=0)


def project_kernel(planes, steps, ids, squares, *refs):
    count = planes * SIDES
    hidden, refs = refs[: count + 1], refs[count + 1 :]
    pieces, (raw, sums, grads, held, sems) = refs[:8], refs[8:]
    tok_dev = hidden[0].shape[0]
    half = tok_dev // 2
    tile = raw.shape[0] // steps
    mine = jnp.where(ids[1] == 0, ids[0], count - 1 - ids[0])
    copies = []
    for i in range(steps):
        columns = pl.ds(i * tile, tile)
        for r, source in enumerate(hidden):
            spot = mine + (r if r < count else count // 2)
            spot = jnp.where(spot >= count, spot - count, spot)
            first = half if r == count else 0
            target = held.at[spot, pl.ds(first, source.shape[0]), columns]
            copies.append(pltpu.make_async_copy(source.at[:, columns], target, sems.at[i, r]))
            copies[-1].start()
    for index, piece in enumerate(pieces):
        side = ids[1] ^ (index & 1)
        group = ids[2] ^ ((index >> 1) & 1)
        member = ids[3] ^ ((index >> 2) & 1)
        for j in range(planes):
            plane = ids[0] ^ j
            spot = jnp.where(side == 0, plane, count - 1 - plane)
            rows = pl.ds(pl.multiple_of(spot * tok_dev + member * half, half), half)
            for kind in range(2):
                columns = pl.ds(pl.multiple_of((kind * KVG + group) * DH, DH), DH)
                grads[rows, columns] = piece[
                    j * half : (j + 1) * half, kind * DH : (kind + 1) * DH
                ]
    width = raw.shape[1]
    acc = jnp.zeros((8, width), jnp.float32)
    for i in range(steps):
        for copy in copies[i * (count + 1) : (i + 1) * (count + 1)]:
            copy.wait()
        rows = slice(i * tile, (i + 1) * tile)
        block = held[:, :, rows].reshape(count * tok_dev, tile)
        out = lax.dot_general(
            block, grads[...], CONTRACT_FIRST, preferred_element_type=jnp.float32
        )
        raw[rows] = out
        acc += jnp.sum((out * out).reshape(-1, 8, width), axis=0)
    total = jnp.sum(acc, axis=0, keepdims=True)
    weights = jnp.sum(squares[...], axis=0, keepdims=True)
    row = lax.broadcasted_iota(jnp.int32, sums.shape, 0)
    sums[...] = jnp.where(row == 0, total, weights)


def scale_kernel(factor, steps, sums, sums_1, sums_2, sums_3, raw, *refs):
    outs, helds, sems = refs[:2], refs[2:4], refs[4]
    total = (sums[...] + sums_1[...]) + (sums_2[...] + sums_3[...])
    grad_norm = jnp.sqrt(total[0:1] + EPSILON)
    weight_norm = jnp.sqrt(total[1:2] + EPSILON)
    clip = jnp.minimum(1.0, factor * weight_norm / grad_norm)
    width = outs[0].shape[1]
    tile = raw.shape[0] // steps
    copies = []
    for i in range(steps):
        rows = pl.ds(i * tile, tile)
        for kind, (out, held) in enumerate(zip(outs, helds, strict=True)):
            columns = slice(kind * width, (kind + 1) * width)
            held[rows] = raw[rows, columns] * clip[:, columns]
            copy = pltpu.make_async_copy(held.at[rows], out.at[rows], sems.at[2 * i + kind])
            copy.start()
            copies.append(copy)
    for copy in copies:
        copy.wait()


def local_small(
    queries, keys, values, out_grad, hidden, key_weight, value_weight, stretch_owner, positions
):
    tok_dev, width = queries.shape
    half = tok_dev // 2
    count = lax.axis_size("ctx")
    planes = count // SIDES
    groups = lax.axis_size("fsdp") // MEMBERS
    total = tok_dev * count
    ctx, fsdp = lax.axis_index("ctx"), lax.axis_index("fsdp")
    ids = jnp.stack([ctx // SIDES, ctx % SIDES, fsdp // MEMBERS, fsdp % MEMBERS]).astype(jnp.int32)
    bf16, f32 = jnp.bfloat16, jnp.float32
    shape = jax.ShapeDtypeStruct

    def call(kernel, ins, outs, mib=8, **more):
        return pl.pallas_call(
            kernel,
            out_shape=outs,
            in_specs=ins,
            out_specs=jax.tree.map(lambda _: VMEM, outs),
            compiler_params=pltpu.CompilerParams(vmem_limit_bytes=mib * 2**20),
            **more,
        )

    def move(x, plane=0, side=0, group=0, member=0):
        pairs = []
        fs = groups * MEMBERS
        for i in range(count):
            for j in range(fs):
                p, s = i // SIDES ^ plane, i % SIDES ^ side
                g, m = j // MEMBERS ^ group, j % MEMBERS ^ member
                pairs.append((i * fs + j, (p * SIDES + s) * fs + g * MEMBERS + m))
        return lax.ppermute(x, ("ctx", "fsdp"), pairs)

    ring = [p * SIDES for p in range(planes)] + [p * SIDES + 1 for p in reversed(range(planes))]

    def around(x, step):
        pairs = [(ring[i], ring[(i + step) % count]) for i in range(count)]
        return lax.ppermute(x, "ctx", pairs)

    rows = hidden.shape[1]

    far = [
        pltpu.with_memory_space_constraint(x, pltpu.HBM)
        for x in (keys, values, queries, out_grad, positions.reshape(1, tok_dev), hidden)
    ]
    kv, qd, held = call(
        pack_kernel,
        [SMEM] + [ANY] * 6,
        (
            shape((tok_dev, 2 * DH), bf16),
            shape((2 * tok_dev + 16, width), bf16),
            shape(hidden.shape, bf16),
        ),
        scratch_shapes=[
            pltpu.VMEM((1, tok_dev), jnp.int32),
            pltpu.SemaphoreType.DMA((6,)),
        ],
    )(ids, *far)
    qd_side = move(qd, side=1)
    kv_all = [kv] + [move(kv, plane=j) for j in range(1, planes)]
    qd_all = [qd, qd_side]
    (held,) = after((held,), qd_side, *kv_all[1:])
    blocks = {0: held}
    up, down = around(held, 1), around(held, -1)

    columns = 2 * KVG * DH
    steps = 8
    tile = rows // steps
    weight = pl.BlockSpec((tile, columns // 2), lambda i: (i, 0))
    squares = pl.pallas_call(
        square_kernel,
        grid=(steps,),
        out_shape=shape((8, columns), f32),
        in_specs=[weight] * 2,
        out_specs=pl.BlockSpec((8, columns), lambda i: (0, 0)),
        compiler_params=pltpu.CompilerParams(vmem_limit_bytes=8 * 2**20),
    )(key_weight, value_weight)

    tiles = SIDES * width // DH
    stats = call(
        functools.partial(stats_kernel, planes),
        [SMEM] * 2 + [VMEM] * (planes + SIDES),
        shape((3 * tiles, tok_dev), f32),
    )(ids, stretch_owner, *kv_all, *qd_all)
    stats_side = move(stats, side=1)
    blocks[count - 1], blocks[1] = after((up, down), stats_side)
    up, down = around(blocks[count - 1], 1), around(blocks[1], -1)
    grads_shape = (planes * half, 2 * DH)
    keep, give, slopes = call(
        functools.partial(grads_kernel, planes),
        [SMEM] * 2 + [VMEM] * (planes + 2 * SIDES),
        (
            shape(grads_shape, f32),
            shape(grads_shape, bf16),
            shape((SIDES, planes * tok_dev, tok_dev * width // DH), bf16),
        ),
        scratch_shapes=[pltpu.VMEM((planes * tok_dev, 2 * DH), f32)],
    )(ids, stretch_owner, *kv_all, *qd_all, stats, stats_side)
    kv_parts = call(
        members_kernel,
        [VMEM] * 2,
        tuple(shape((half, 2 * DH), bf16 if j else f32) for j in range(planes)),
    )(keep, move(give, member=1))
    piece = call(sum_kernel, [VMEM] * planes, shape((half, 2 * DH), bf16))(
        kv_parts[0], *[move(kv_parts[j], plane=j) for j in range(1, planes)]
    )
    blocks[count - 2], blocks[2] = after((up, down), piece)
    up, down = around(blocks[count - 2], 1), around(blocks[2], -1)
    (piece,) = after((piece,), blocks[2])
    parts = [move(piece, plane=j) for j in range(1, planes)]
    piece_all = call(join_kernel, [VMEM] * planes, shape(grads_shape, bf16))(piece, *parts)
    blocks[count - 3], blocks[3] = up, down
    up, down = halves_after(up, down, piece_all)
    blocks[4], blocks[count] = around(up, 1), around(down, -1)
    piece_side = move(piece_all, side=1)
    (piece_side,) = after((piece_side,), up)
    near = [piece_all, piece_side, move(piece_all, group=1), move(piece_side, group=1)]
    pieces = near + [move(part, member=1) for part in near]

    q_parts = call(
        functools.partial(query_kernel, planes),
        [VMEM] * (planes + 1) + [ANY] * 2,
        tuple(shape((tok_dev, width), bf16 if j else f32) for j in range(SIDES)),
    )(*kv_all, slopes, piece, squares)
    query_grad = call(sum_kernel, [VMEM] * SIDES, shape((tok_dev, width), bf16))(
        q_parts[0], move(q_parts[1], side=1)
    )

    steps = 2
    hidden_all = [
        pltpu.with_memory_space_constraint(blocks[r], pltpu.HBM) for r in range(count + 1)
    ]
    raw, sums = call(
        functools.partial(project_kernel, planes, steps),
        [SMEM, VMEM] + [ANY] * (count + 1) + [VMEM] * len(pieces),
        (pltpu.VMEM((rows, columns), f32), shape((8, columns), f32)),
        mib=12,
        scratch_shapes=[
            pltpu.VMEM((total, columns), bf16),
            pltpu.VMEM((count,) + hidden.shape, bf16),
            pltpu.SemaphoreType.DMA((steps, count + 1)),
        ],
    )(ids, squares, *hidden_all, *pieces)
    sums_all = [sums, move(sums, member=1), move(sums, group=1), move(sums, group=1, member=1)]
    steps = 8
    key_grad, value_grad = pl.pallas_call(
        functools.partial(scale_kernel, CLIP_RATE * total, steps),
        out_shape=(shape((rows, columns // 2), f32),) * 2,
        in_specs=[VMEM] * 5,
        out_specs=(ANY, ANY),
        scratch_shapes=[pltpu.VMEM((rows, columns // 2), f32)] * 2
        + [pltpu.SemaphoreType.DMA((2 * steps,))],
        compiler_params=pltpu.CompilerParams(vmem_limit_bytes=8 * 2**20),
    )(*sums_all, pltpu.with_memory_space_constraint(raw, pltpu.VMEM))
    return (query_grad, key_grad, value_grad)


def solution(mesh):
    ctx_count, fsdp_count = mesh.shape["ctx"], mesh.shape["fsdp"]

    def program(queries, keys, values, out_grad, hidden, *rest):
        tok_dev = queries.shape[0] // ctx_count
        heads = queries.shape[1] // fsdp_count // DH
        gathered = hidden.size // fsdp_count * hidden.dtype.itemsize
        planes = ctx_count // SIDES
        small = (
            ctx_count == 8
            and gathered <= GATHER_LIMIT
            and planes * SIDES == ctx_count
            and planes & (planes - 1) == 0
            and heads * MEMBERS == HPG
            and fsdp_count == KVG * MEMBERS
            and tok_dev == DH
        )
        return jax.shard_map(
            local_small if small else local_large,
            mesh=mesh,
            in_specs=(
                P("ctx", "fsdp"),
                P("ctx", None),
                P("ctx", None),
                P("ctx", "fsdp"),
                P("ctx", "fsdp"),
                P("fsdp", None),
                P("fsdp", None),
                P(),
                P("ctx"),
            ),
            out_specs=(P("ctx", "fsdp"), P("fsdp", None), P("fsdp", None)),
            check_vma=False,
        )(queries, keys, values, out_grad, hidden, *rest)

    return program
```

```python
import functools
import math

import jax
import jax.numpy as jnp
from jax import lax
from jax.experimental import pallas as pl
from jax.experimental.pallas import tpu as pltpu
from jax.sharding import PartitionSpec as P

DH = 128
HPG = 8
KVG = 2


CLIP_RATE = 0.02
EPSILON = 1e-06
NEGATIVE = -1e30
GATHER_LIMIT = 8 * 2**20

CONTRACT_LAST = (((1,), (1,)), ((), ()))
CONTRACT_FIRST = (((0,), (0,)), ((), ()))
VMEM = pl.BlockSpec(memory_space=pltpu.VMEM)
SMEM = pl.BlockSpec(memory_space=pltpu.SMEM)
ANY = pl.BlockSpec(memory_space=pl.ANY)


def rows_by_head(block, heads, width):
    count = block.shape[0]
    return block.reshape(count, heads, width).transpose(1, 0, 2).reshape(heads * count, width)


def local_large(
    queries, keys, values, out_grad, hidden, key_weight, value_weight, stretch_owner, positions
):
    tok_dev = queries.shape[0]
    heads = queries.shape[1] // DH
    ctx_count = lax.axis_size("ctx")
    total = tok_dev * ctx_count
    half = tok_dev // 2
    ctx_index = lax.axis_index("ctx")
    group = lax.axis_index("fsdp") * heads // HPG
    scale = 1.0 / math.sqrt(DH)
    block = min(512, total)
    blocks = total // block
    query_count = heads * tok_dev
    own_keys = lax.dynamic_slice_in_dim(keys, group * DH, DH, 1)
    own_values = lax.dynamic_slice_in_dim(values, group * DH, DH, 1)
    all_keys, all_values = (
        lax.all_gather(own_keys, "ctx", axis=0, tiled=True),
        lax.all_gather(own_values, "ctx", axis=0, tiled=True),
    )
    offsets = jnp.arange(half, dtype=jnp.int32)
    stretches = jnp.stack([stretch_owner, 2 * ctx_count - 1 - stretch_owner], axis=1)
    key_place = (stretches[:, :, None] * half + offsets[None, None, :]).reshape(total)
    mine = lax.dynamic_slice_in_dim(stretches, ctx_index, 1, 0)[0]
    local_place = (mine[:, None] * half + offsets[None, :]).reshape(tok_dev)
    query_place = jnp.tile(local_place, heads)
    query_floor = jnp.tile(local_place - positions, heads)
    query_rows = rows_by_head(queries, heads, DH)
    grad_rows = rows_by_head(out_grad, heads, DH)

    def scores_at(start, width):
        key_block = lax.dynamic_slice_in_dim(all_keys, start, width, 0)
        place = lax.dynamic_slice_in_dim(key_place, start, width, 0)
        raw = (
            lax.dot_general(
                query_rows, key_block, CONTRACT_LAST, preferred_element_type=jnp.float32
            )
            * scale
        )
        seen = (place[None, :] <= query_place[:, None]) & (place[None, :] >= query_floor[:, None])
        return (jnp.where(seen, raw, NEGATIVE), seen, key_block)

    def stats_step(step, carry):
        top, mass = carry
        masked, seen, key_block = scores_at(step * block, block)
        new_top = jnp.maximum(top, jnp.max(masked, axis=1))
        weights = jnp.where(seen, jnp.exp(masked - new_top[:, None]), 0.0)
        mass = mass * jnp.exp(top - new_top) + jnp.sum(weights, axis=1)
        return (new_top, mass)

    start_top = jnp.full((query_count,), NEGATIVE, jnp.float32)
    start_mass = jnp.zeros((query_count,), jnp.float32)
    top, mass = lax.fori_loop(0, blocks, stats_step, (start_top, start_mass))
    lse = top + jnp.log(mass)

    def probs_at(start, width):
        masked, seen, key_block = scores_at(start, width)
        probs = jnp.where(seen, jnp.exp(masked - lse[:, None]), 0.0)
        value_block = lax.dynamic_slice_in_dim(all_values, start, width, 0)
        dprobs = lax.dot_general(
            grad_rows, value_block, CONTRACT_LAST, preferred_element_type=jnp.float32
        )
        return (probs, dprobs, key_block)

    def delta_step(step, acc):
        probs, dprobs, key_block = probs_at(step * block, block)
        return acc + jnp.sum(probs * dprobs, axis=1)

    delta = lax.fori_loop(0, blocks, delta_step, jnp.zeros((query_count,), jnp.float32))

    def slopes_at(start, width):
        probs, dprobs, key_block = probs_at(start, width)
        slopes = (probs * (dprobs - delta[:, None]) * scale).astype(jnp.bfloat16)
        return (probs.astype(jnp.bfloat16), slopes, key_block)

    def key_terms(probs_b, slopes):
        key_part = lax.dot_general(
            slopes, query_rows, CONTRACT_FIRST, preferred_element_type=jnp.float32
        )
        value_part = lax.dot_general(
            probs_b, grad_rows, CONTRACT_FIRST, preferred_element_type=jnp.float32
        )
        return jnp.concatenate([key_part, value_part], axis=1)

    start_query = jnp.zeros((query_count, DH), jnp.float32)

    def query_step(step, query_acc):
        probs_b, slopes, key_block = slopes_at(step * block, block)
        return query_acc + jnp.dot(slopes, key_block, preferred_element_type=jnp.float32)

    query_acc = lax.fori_loop(0, blocks, query_step, start_query)
    width = math.gcd(tok_dev * lax.axis_size("ctx"), block)

    def inner(step, acc):
        offset = step * width
        probs_b, slopes, key_block = slopes_at(offset, width)
        return lax.dynamic_update_slice_in_dim(acc, key_terms(probs_b, slopes), offset, 0)

    own_grads = lax.psum_scatter(
        lax.fori_loop(
            0,
            tok_dev * lax.axis_size("ctx") // width,
            inner,
            jnp.zeros((tok_dev * lax.axis_size("ctx"), 2 * DH), jnp.float32),
        ),
        "ctx",
        scatter_dimension=0,
        tiled=True,
    )
    query_grad = (
        query_acc.reshape(heads, tok_dev, DH)
        .transpose(1, 0, 2)
        .reshape(tok_dev, heads * DH)
        .astype(jnp.bfloat16)
    )
    members = lax.all_gather(own_grads.astype(jnp.bfloat16), "fsdp", axis=0, tiled=True).astype(
        own_grads.dtype
    )
    per_group = members.reshape(KVG, -1, tok_dev, 2 * DH).sum(axis=1)
    key_grads = (
        per_group[:, :, :DH].transpose(1, 0, 2).reshape(tok_dev, KVG * DH).astype(jnp.bfloat16)
    )
    value_grads = (
        per_group[:, :, DH:].transpose(1, 0, 2).reshape(tok_dev, KVG * DH).astype(jnp.bfloat16)
    )
    both_grads = jnp.concatenate([key_grads, value_grads], axis=1)
    columns = KVG * DH
    raw = lax.psum(
        lax.dot_general(hidden, both_grads, CONTRACT_FIRST, preferred_element_type=jnp.float32),
        "ctx",
    )
    key_f = key_weight.astype(jnp.float32)
    value_f = value_weight.astype(jnp.float32)
    grad_sq, key_sq, value_sq = lax.psum(
        (
            jnp.sum(raw * raw, axis=0),
            jnp.sum(key_f * key_f, axis=0),
            jnp.sum(value_f * value_f, axis=0),
        ),
        "fsdp",
    )
    weight_norm = jnp.sqrt(jnp.concatenate([key_sq, value_sq]) + EPSILON)
    grad_norm = jnp.sqrt(grad_sq + EPSILON)
    clipped = raw * jnp.minimum(1.0, CLIP_RATE * total * weight_norm / grad_norm)[None, :]
    return (query_grad, clipped[:, :columns], clipped[:, columns:])


SIDES = 2
MEMBERS = 2
DIGIT = 64


def pack_kernel(
    ids, keys, values, queries, out_grad, positions, hidden, kv_out, qd_out, held, place, sems
):
    tok_dev = queries.shape[0]
    columns = pl.ds(pl.multiple_of(ids[2] * DH, DH), DH)
    copies = [
        pltpu.make_async_copy(source, target, sems.at[i])
        for i, (source, target) in enumerate(
            (
                (positions, place),
                (keys.at[:, columns], kv_out.at[:, :DH]),
                (values.at[:, columns], kv_out.at[:, DH:]),
                (queries, qd_out.at[:tok_dev]),
                (out_grad, qd_out.at[tok_dev : 2 * tok_dev]),
                (hidden, held),
            )
        )
    ]
    for copy in copies:
        copy.start()
    rest = qd_out.shape[1] - tok_dev
    if rest > 0:
        qd_out[2 * tok_dev :, tok_dev:] = jnp.zeros((qd_out.shape[0] - 2 * tok_dev, rest), jnp.bfloat16)
    copies[0].wait()
    high = place[...] // DIGIT
    low = place[...] - high * DIGIT
    pad = jnp.zeros((qd_out.shape[0] - 2 * tok_dev - 2, tok_dev), jnp.float32)
    digits = jnp.concatenate([high.astype(jnp.float32), low.astype(jnp.float32), pad], axis=0)
    qd_out[2 * tok_dev :, :tok_dev] = digits.astype(jnp.bfloat16)
    for copy in copies[1:]:
        copy.wait()


def nothing_kernel(*refs):
    pass


def after(xs, *events):
    count = len(xs)
    return pl.pallas_call(
        nothing_kernel,
        out_shape=tuple(jax.ShapeDtypeStruct(x.shape, x.dtype) for x in xs),
        in_specs=[ANY] * (count + len(events)),
        out_specs=(ANY,) * count,
        input_output_aliases={i: i for i in range(count)},
        compiler_params=pltpu.CompilerParams(vmem_limit_bytes=2**20),
    )(*xs, *events)


def halves_kernel(*refs):
    up, down, (up_half, down_half, sems) = refs[0], refs[1], refs[-3:]
    half = up_half.shape[0]
    copies = [
        pltpu.make_async_copy(up.at[:half], up_half, sems.at[0]),
        pltpu.make_async_copy(down.at[half:], down_half, sems.at[1]),
    ]
    for copy in copies:
        copy.start()
    for copy in copies:
        copy.wait()


def halves_after(up, down, *events):
    half = jax.ShapeDtypeStruct((up.shape[0] // 2, up.shape[1]), up.dtype)
    return pl.pallas_call(
        halves_kernel,
        out_shape=(half, half),
        in_specs=[ANY] * (2 + len(events)),
        out_specs=(ANY, ANY),
        scratch_shapes=[pltpu.SemaphoreType.DMA((2,))],
        compiler_params=pltpu.CompilerParams(vmem_limit_bytes=2**20),
    )(up, down, *events)


def seen_pairs(ids, owner, planes, tok_dev, qd):
    last = 2 * planes * SIDES - 1
    half = tok_dev // 2

    def place_of(at, block):
        stretch = owner[block]
        return jnp.where(at < half, at + stretch * half, at - half + (last - stretch) * half)

    row = lax.broadcasted_iota(jnp.int32, (tok_dev, tok_dev), 0)
    key_place = jnp.concatenate(
        [place_of(row, (ids[0] ^ j) * SIDES + ids[1]) for j in range(planes)], axis=0
    )
    lane = lax.broadcasted_iota(jnp.int32, (1, tok_dev), 1)
    seen = []
    for side in range(SIDES):
        place = place_of(lane, ids[0] * SIDES + (ids[1] ^ side))
        digits = qd[side][2 * tok_dev :, :tok_dev].astype(jnp.float32)
        back = (digits[0:1] * DIGIT + digits[1:2]).astype(jnp.int32)
        seen.append((key_place <= place) & (key_place >= place - back))
    return seen


def scaled_scores(k, q, scale):
    return lax.dot_general(k, q, CONTRACT_LAST, preferred_element_type=jnp.float32) * scale


def stats_kernel(planes, ids, owner, *refs):
    kv_refs, qd, stats = refs[:planes], refs[planes : planes + SIDES], refs[-1]
    tok_dev = kv_refs[0].shape[0]
    heads = qd[0].shape[1] // DH
    scale = 1.0 / math.sqrt(DH)
    kv = jnp.concatenate([ref[...] for ref in kv_refs], axis=0)
    k, v = kv[:, :DH], kv[:, DH:]
    seen = seen_pairs(ids, owner, planes, tok_dev, qd)
    tiles = SIDES * heads
    for side in range(SIDES):
        for head in range(heads):
            q = qd[side][:tok_dev, head * DH : (head + 1) * DH]
            d = qd[side][tok_dev : 2 * tok_dev, head * DH : (head + 1) * DH]
            scores = jnp.where(seen[side], scaled_scores(k, q, scale), NEGATIVE)
            dprobs = lax.dot_general(v, d, CONTRACT_LAST, preferred_element_type=jnp.float32)
            top = jnp.max(scores, axis=0, keepdims=True)
            weights = jnp.where(seen[side], jnp.exp(scores - top), 0.0)
            tile = side * heads + head
            stats[tile : tile + 1] = top
            stats[tiles + tile : tiles + tile + 1] = jnp.sum(weights, axis=0, keepdims=True)
            stats[2 * tiles + tile : 2 * tiles + tile + 1] = jnp.sum(
                weights * dprobs, axis=0, keepdims=True
            )


def grads_kernel(planes, ids, owner, *refs):
    kv_refs, refs = refs[:planes], refs[planes:]
    qd, refs = refs[:SIDES], refs[SIDES:]
    stats, (keep, give, slopes_out, acc) = refs[:SIDES], refs[SIDES:]
    tok_dev = kv_refs[0].shape[0]
    half = tok_dev // 2
    heads = qd[0].shape[1] // DH
    scale = 1.0 / math.sqrt(DH)
    kv = jnp.concatenate([ref[...] for ref in kv_refs], axis=0)
    k, v = kv[:, :DH], kv[:, DH:]
    seen = seen_pairs(ids, owner, planes, tok_dev, qd)
    tiles = SIDES * heads
    key_acc = jnp.zeros((planes * tok_dev, DH), jnp.float32)
    value_acc = jnp.zeros((planes * tok_dev, DH), jnp.float32)
    for side in range(SIDES):
        q_rows, d_rows, slope_tiles, prob_tiles = [], [], [], []
        parts = [
            [
                stats[other][kind * tiles + (side ^ other) * heads :][:heads]
                for other in range(SIDES)
            ]
            for kind in range(3)
        ]
        top = functools.reduce(jnp.maximum, parts[0])
        shares = [jnp.exp(part - top) for part in parts[0]]
        mass = sum(share * part for share, part in zip(shares, parts[1], strict=True))
        lse = top + jnp.log(mass)
        delta = sum(share * part for share, part in zip(shares, parts[2], strict=True)) / mass
        for head in range(heads):
            q = qd[side][:tok_dev, head * DH : (head + 1) * DH]
            d = qd[side][tok_dev : 2 * tok_dev, head * DH : (head + 1) * DH]
            scores = scaled_scores(k, q, scale)
            dprobs = lax.dot_general(v, d, CONTRACT_LAST, preferred_element_type=jnp.float32)
            probs = jnp.where(seen[side], jnp.exp(scores - lse[head : head + 1]), 0.0)
            slopes = (probs * (dprobs - delta[head : head + 1]) * scale).astype(jnp.bfloat16)
            q_rows.append(q)
            d_rows.append(d)
            slope_tiles.append(slopes)
            prob_tiles.append(probs.astype(jnp.bfloat16))
        slope_tile = jnp.concatenate(slope_tiles, axis=1)
        slopes_out[side] = slope_tile
        key_acc += jnp.dot(
            slope_tile,
            jnp.concatenate(q_rows, axis=0),
            preferred_element_type=jnp.float32,
        )
        value_acc += jnp.dot(
            jnp.concatenate(prob_tiles, axis=1),
            jnp.concatenate(d_rows, axis=0),
            preferred_element_type=jnp.float32,
        )
    acc[:, :DH] = key_acc
    acc[:, DH:] = value_acc
    for j in range(planes):
        rows = slice(j * half, (j + 1) * half)
        own = pl.multiple_of(j * tok_dev + ids[3] * half, half)
        other = pl.multiple_of(j * tok_dev + (1 - ids[3]) * half, half)
        keep[rows] = acc[pl.ds(own, half)]
        give[rows] = acc[pl.ds(other, half)].astype(give.dtype)


def members_kernel(keep, got, *outs):
    half = outs[0].shape[0]
    for j, out in enumerate(outs):
        rows = slice(j * half, (j + 1) * half)
        out[...] = (keep[rows] + got[rows].astype(jnp.float32)).astype(out.dtype)


def query_kernel(planes, *refs):
    kv_refs, slopes, q_out = refs[:planes], refs[planes], refs[planes + 3 :]
    k = jnp.concatenate([ref[:, :DH] for ref in kv_refs], axis=0)
    for source, out in enumerate(q_out):
        tok_dev, width = out.shape
        for head in range(width // DH):
            tile = slopes[source, :, head * tok_dev : (head + 1) * tok_dev]
            part = lax.dot_general(tile, k, CONTRACT_FIRST, preferred_element_type=jnp.float32)
            out[:, head * DH : (head + 1) * DH] = part.astype(out.dtype)


def join_kernel(event, *refs):
    rows = refs[0].shape[0]
    for i, ref in enumerate(refs[:-1]):
        refs[-1][i * rows : (i + 1) * rows] = ref[...]


def sum_kernel(*refs):
    total = refs[0][...].astype(jnp.float32)
    for ref in refs[1:-1]:
        total += ref[...].astype(jnp.float32)
    refs[-1][...] = total.astype(refs[-1].dtype)


def square_kernel(key_weight, value_weight, out):
    width = key_weight.shape[1]

    @pl.when(pl.program_id(0) == 0)
    def _():
        out[...] = jnp.zeros_like(out)

    k = key_weight[...].astype(jnp.float32)
    v = value_weight[...].astype(jnp.float32)
    out[:, :width] += jnp.sum((k * k).reshape(-1, 8, width), axis=0)
    out[:, width:] += jnp.sum((v * v).reshape(-1, 8, width), axis=0)


def project_kernel(planes, steps, ids, squares, *refs):
    count = planes * SIDES
    hidden, refs = refs[: count + 1], refs[count + 1 :]
    pieces, (raw, sums, grads, held) = refs[:8], refs[8:]
    tok_dev = hidden[0].shape[0]
    half = tok_dev // 2
    tile = raw.shape[0] // steps
    mine = jnp.where(ids[1] == 0, ids[0], count - 1 - ids[0])
    for r, block in enumerate(hidden):
        spot = mine + (r if r < count else count // 2)
        spot = jnp.where(spot >= count, spot - count, spot)
        first = half if r == count else 0
        held[spot, first : first + block.shape[0]] = block[...]
    for index, piece in enumerate(pieces):
        side = ids[1] ^ (index & 1)
        group = ids[2] ^ ((index >> 1) & 1)
        member = ids[3] ^ ((index >> 2) & 1)
        for j in range(planes):
            plane = ids[0] ^ j
            spot = jnp.where(side == 0, plane, count - 1 - plane)
            rows = pl.ds(pl.multiple_of(spot * tok_dev + member * half, half), half)
            for kind in range(2):
                columns = pl.ds(pl.multiple_of((kind * KVG + group) * DH, DH), DH)
                grads[rows, columns] = piece[
                    j * half : (j + 1) * half, kind * DH : (kind + 1) * DH
                ]
    width = raw.shape[1]
    acc = jnp.zeros((8, width), jnp.float32)
    for i in range(steps):
        rows = slice(i * tile, (i + 1) * tile)
        block = held[:, :, rows].reshape(count * tok_dev, tile)
        out = lax.dot_general(
            block, grads[...], CONTRACT_FIRST, preferred_element_type=jnp.float32
        )
        raw[rows] = out
        acc += jnp.sum((out * out).reshape(-1, 8, width), axis=0)
    total = jnp.sum(acc, axis=0, keepdims=True)
    weights = jnp.sum(squares[...], axis=0, keepdims=True)
    row = lax.broadcasted_iota(jnp.int32, sums.shape, 0)
    sums[...] = jnp.where(row == 0, total, weights)


def scale_kernel(factor, steps, sums, sums_1, sums_2, sums_3, raw, *refs):
    outs, helds, sems = refs[:2], refs[2:4], refs[4]
    total = (sums[...] + sums_1[...]) + (sums_2[...] + sums_3[...])
    grad_norm = jnp.sqrt(total[0:1] + EPSILON)
    weight_norm = jnp.sqrt(total[1:2] + EPSILON)
    clip = jnp.minimum(1.0, factor * weight_norm / grad_norm)
    width = outs[0].shape[1]
    tile = raw.shape[0] // steps
    copies = []
    for i in range(steps):
        rows = pl.ds(i * tile, tile)
        for kind, (out, held) in enumerate(zip(outs, helds, strict=True)):
            columns = slice(kind * width, (kind + 1) * width)
            held[rows] = raw[rows, columns] * clip[:, columns]
            copy = pltpu.make_async_copy(held.at[rows], out.at[rows], sems.at[2 * i + kind])
            copy.start()
            copies.append(copy)
    for copy in copies:
        copy.wait()


def local_small(
    queries, keys, values, out_grad, hidden, key_weight, value_weight, stretch_owner, positions
):
    tok_dev, width = queries.shape
    half = tok_dev // 2
    count = lax.axis_size("ctx")
    planes = count // SIDES
    groups = lax.axis_size("fsdp") // MEMBERS
    total = tok_dev * count
    ctx, fsdp = lax.axis_index("ctx"), lax.axis_index("fsdp")
    ids = jnp.stack([ctx // SIDES, ctx % SIDES, fsdp // MEMBERS, fsdp % MEMBERS]).astype(jnp.int32)
    bf16, f32 = jnp.bfloat16, jnp.float32
    shape = jax.ShapeDtypeStruct

    def call(kernel, ins, outs, mib=8, **more):
        return pl.pallas_call(
            kernel,
            out_shape=outs,
            in_specs=ins,
            out_specs=jax.tree.map(lambda _: VMEM, outs),
            compiler_params=pltpu.CompilerParams(vmem_limit_bytes=mib * 2**20),
            **more,
        )

    def move(x, plane=0, side=0, group=0, member=0):
        pairs = []
        fs = groups * MEMBERS
        for i in range(count):
            for j in range(fs):
                p, s = i // SIDES ^ plane, i % SIDES ^ side
                g, m = j // MEMBERS ^ group, j % MEMBERS ^ member
                pairs.append((i * fs + j, (p * SIDES + s) * fs + g * MEMBERS + m))
        return lax.ppermute(x, ("ctx", "fsdp"), pairs)

    ring = [p * SIDES for p in range(planes)] + [p * SIDES + 1 for p in reversed(range(planes))]

    def around(x, step):
        pairs = [(ring[i], ring[(i + step) % count]) for i in range(count)]
        return lax.ppermute(x, "ctx", pairs)

    rows = hidden.shape[1]

    far = [
        pltpu.with_memory_space_constraint(x, pltpu.HBM)
        for x in (keys, values, queries, out_grad, positions.reshape(1, tok_dev), hidden)
    ]
    kv, qd, held = call(
        pack_kernel,
        [SMEM] + [ANY] * 6,
        (
            shape((tok_dev, 2 * DH), bf16),
            shape((2 * tok_dev + 16, width), bf16),
            shape(hidden.shape, bf16),
        ),
        scratch_shapes=[
            pltpu.VMEM((1, tok_dev), jnp.int32),
            pltpu.SemaphoreType.DMA((6,)),
        ],
    )(ids, *far)
    qd_side = move(qd, side=1)
    kv_all = [kv] + [move(kv, plane=j) for j in range(1, planes)]
    qd_all = [qd, qd_side]
    (held,) = after((held,), qd_side, *kv_all[1:])
    blocks = {0: held}
    up, down = around(held, 1), around(held, -1)

    columns = 2 * KVG * DH
    steps = 8
    tile = rows // steps
    weight = pl.BlockSpec((tile, columns // 2), lambda i: (i, 0))
    squares = pl.pallas_call(
        square_kernel,
        grid=(steps,),
        out_shape=shape((8, columns), f32),
        in_specs=[weight] * 2,
        out_specs=pl.BlockSpec((8, columns), lambda i: (0, 0)),
        compiler_params=pltpu.CompilerParams(vmem_limit_bytes=8 * 2**20),
    )(key_weight, value_weight)

    tiles = SIDES * width // DH
    stats = call(
        functools.partial(stats_kernel, planes),
        [SMEM] * 2 + [VMEM] * (planes + SIDES),
        shape((3 * tiles, tok_dev), f32),
    )(ids, stretch_owner, *kv_all, *qd_all)
    stats_side = move(stats, side=1)
    blocks[count - 1], blocks[1] = after((up, down), stats_side)
    up, down = around(blocks[count - 1], 1), around(blocks[1], -1)
    grads_shape = (planes * half, 2 * DH)
    keep, give, slopes = call(
        functools.partial(grads_kernel, planes),
        [SMEM] * 2 + [VMEM] * (planes + 2 * SIDES),
        (
            shape(grads_shape, f32),
            shape(grads_shape, bf16),
            shape((SIDES, planes * tok_dev, tok_dev * width // DH), bf16),
        ),
        scratch_shapes=[pltpu.VMEM((planes * tok_dev, 2 * DH), f32)],
    )(ids, stretch_owner, *kv_all, *qd_all, stats, stats_side)
    kv_parts = call(
        members_kernel,
        [VMEM] * 2,
        tuple(shape((half, 2 * DH), bf16 if j else f32) for j in range(planes)),
    )(keep, move(give, member=1))
    piece = call(sum_kernel, [VMEM] * planes, shape((half, 2 * DH), bf16))(
        kv_parts[0], *[move(kv_parts[j], plane=j) for j in range(1, planes)]
    )
    blocks[count - 2], blocks[2] = after((up, down), piece)
    up, down = around(blocks[count - 2], 1), around(blocks[2], -1)
    parts = [move(piece, plane=j) for j in range(1, planes)]
    q_parts = call(
        functools.partial(query_kernel, planes),
        [VMEM] * (planes + 1) + [ANY] * 2,
        tuple(shape((tok_dev, width), bf16 if j else f32) for j in range(SIDES)),
    )(*kv_all, slopes, piece, squares)
    piece_all = call(join_kernel, [ANY] + [VMEM] * planes, shape(grads_shape, bf16))(
        q_parts[1], piece, *parts
    )
    blocks[count - 3], blocks[3] = up, down
    up, down = halves_after(up, down, piece_all)
    blocks[4], blocks[count] = around(up, 1), around(down, -1)
    piece_side = move(piece_all, side=1)
    (piece_side,) = after((piece_side,), up)
    near = [piece_all, piece_side, move(piece_all, group=1), move(piece_side, group=1)]
    pieces = near + [move(part, member=1) for part in near]

    query_grad = call(sum_kernel, [VMEM] * SIDES, shape((tok_dev, width), bf16))(
        q_parts[0], move(q_parts[1], side=1)
    )

    steps = 2
    raw, sums = call(
        functools.partial(project_kernel, planes, steps),
        [SMEM] + [VMEM] * (count + 2 + len(pieces)),
        (pltpu.VMEM((rows, columns), f32), shape((8, columns), f32)),
        mib=12,
        scratch_shapes=[
            pltpu.VMEM((total, columns), bf16),
            pltpu.VMEM((count,) + hidden.shape, bf16),
        ],
    )(ids, squares, *[blocks[r] for r in range(count + 1)], *pieces)
    sums_all = [sums, move(sums, member=1), move(sums, group=1), move(sums, group=1, member=1)]
    steps = 8
    key_grad, value_grad = pl.pallas_call(
        functools.partial(scale_kernel, CLIP_RATE * total, steps),
        out_shape=(shape((rows, columns // 2), f32),) * 2,
        in_specs=[VMEM] * 5,
        out_specs=(ANY, ANY),
        scratch_shapes=[pltpu.VMEM((rows, columns // 2), f32)] * 2
        + [pltpu.SemaphoreType.DMA((2 * steps,))],
        compiler_params=pltpu.CompilerParams(vmem_limit_bytes=8 * 2**20),
    )(*sums_all, pltpu.with_memory_space_constraint(raw, pltpu.VMEM))
    return (query_grad, key_grad, value_grad)


def solution(mesh):
    ctx_count, fsdp_count = mesh.shape["ctx"], mesh.shape["fsdp"]

    def program(queries, keys, values, out_grad, hidden, *rest):
        tok_dev = queries.shape[0] // ctx_count
        heads = queries.shape[1] // fsdp_count // DH
        gathered = hidden.size // fsdp_count * hidden.dtype.itemsize
        planes = ctx_count // SIDES
        small = (
            ctx_count == 8
            and gathered <= GATHER_LIMIT
            and planes * SIDES == ctx_count
            and planes & (planes - 1) == 0
            and heads * MEMBERS == HPG
            and fsdp_count == KVG * MEMBERS
            and tok_dev == DH
        )
        return jax.shard_map(
            local_small if small else local_large,
            mesh=mesh,
            in_specs=(
                P("ctx", "fsdp"),
                P("ctx", None),
                P("ctx", None),
                P("ctx", "fsdp"),
                P("ctx", "fsdp"),
                P("fsdp", None),
                P("fsdp", None),
                P(),
                P("ctx"),
            ),
            out_specs=(P("ctx", "fsdp"), P("fsdp", None), P("fsdp", None)),
            check_vma=False,
        )(queries, keys, values, out_grad, hidden, *rest)

    return program
```

```python
import functools
import math

import jax
import jax.numpy as jnp
from jax import lax
from jax.experimental import pallas as pl
from jax.experimental.pallas import tpu as pltpu
from jax.sharding import PartitionSpec as P

DH = 128
HPG = 8
KVG = 2


CLIP_RATE = 0.02
EPSILON = 1e-06
NEGATIVE = -1e30
GATHER_LIMIT = 8 * 2**20

CONTRACT_LAST = (((1,), (1,)), ((), ()))
CONTRACT_FIRST = (((0,), (0,)), ((), ()))
VMEM = pl.BlockSpec(memory_space=pltpu.VMEM)
SMEM = pl.BlockSpec(memory_space=pltpu.SMEM)
ANY = pl.BlockSpec(memory_space=pl.ANY)


def rows_by_head(block, heads, width):
    count = block.shape[0]
    return block.reshape(count, heads, width).transpose(1, 0, 2).reshape(heads * count, width)


def local_large(
    queries, keys, values, out_grad, hidden, key_weight, value_weight, stretch_owner, positions
):
    tok_dev = queries.shape[0]
    heads = queries.shape[1] // DH
    ctx_count = lax.axis_size("ctx")
    total = tok_dev * ctx_count
    half = tok_dev // 2
    ctx_index = lax.axis_index("ctx")
    group = lax.axis_index("fsdp") * heads // HPG
    scale = 1.0 / math.sqrt(DH)
    block = min(512, total)
    blocks = total // block
    query_count = heads * tok_dev
    own_keys = lax.dynamic_slice_in_dim(keys, group * DH, DH, 1)
    own_values = lax.dynamic_slice_in_dim(values, group * DH, DH, 1)
    all_keys, all_values = (
        lax.all_gather(own_keys, "ctx", axis=0, tiled=True),
        lax.all_gather(own_values, "ctx", axis=0, tiled=True),
    )
    offsets = jnp.arange(half, dtype=jnp.int32)
    stretches = jnp.stack([stretch_owner, 2 * ctx_count - 1 - stretch_owner], axis=1)
    key_place = (stretches[:, :, None] * half + offsets[None, None, :]).reshape(total)
    mine = lax.dynamic_slice_in_dim(stretches, ctx_index, 1, 0)[0]
    local_place = (mine[:, None] * half + offsets[None, :]).reshape(tok_dev)
    query_place = jnp.tile(local_place, heads)
    query_floor = jnp.tile(local_place - positions, heads)
    query_rows = rows_by_head(queries, heads, DH)
    grad_rows = rows_by_head(out_grad, heads, DH)

    def scores_at(start, width):
        key_block = lax.dynamic_slice_in_dim(all_keys, start, width, 0)
        place = lax.dynamic_slice_in_dim(key_place, start, width, 0)
        raw = (
            lax.dot_general(
                query_rows, key_block, CONTRACT_LAST, preferred_element_type=jnp.float32
            )
            * scale
        )
        seen = (place[None, :] <= query_place[:, None]) & (place[None, :] >= query_floor[:, None])
        return (jnp.where(seen, raw, NEGATIVE), seen, key_block)

    def stats_step(step, carry):
        top, mass = carry
        masked, seen, key_block = scores_at(step * block, block)
        new_top = jnp.maximum(top, jnp.max(masked, axis=1))
        weights = jnp.where(seen, jnp.exp(masked - new_top[:, None]), 0.0)
        mass = mass * jnp.exp(top - new_top) + jnp.sum(weights, axis=1)
        return (new_top, mass)

    start_top = jnp.full((query_count,), NEGATIVE, jnp.float32)
    start_mass = jnp.zeros((query_count,), jnp.float32)
    top, mass = lax.fori_loop(0, blocks, stats_step, (start_top, start_mass))
    lse = top + jnp.log(mass)

    def probs_at(start, width):
        masked, seen, key_block = scores_at(start, width)
        probs = jnp.where(seen, jnp.exp(masked - lse[:, None]), 0.0)
        value_block = lax.dynamic_slice_in_dim(all_values, start, width, 0)
        dprobs = lax.dot_general(
            grad_rows, value_block, CONTRACT_LAST, preferred_element_type=jnp.float32
        )
        return (probs, dprobs, key_block)

    def delta_step(step, acc):
        probs, dprobs, key_block = probs_at(step * block, block)
        return acc + jnp.sum(probs * dprobs, axis=1)

    delta = lax.fori_loop(0, blocks, delta_step, jnp.zeros((query_count,), jnp.float32))

    def slopes_at(start, width):
        probs, dprobs, key_block = probs_at(start, width)
        slopes = (probs * (dprobs - delta[:, None]) * scale).astype(jnp.bfloat16)
        return (probs.astype(jnp.bfloat16), slopes, key_block)

    def key_terms(probs_b, slopes):
        key_part = lax.dot_general(
            slopes, query_rows, CONTRACT_FIRST, preferred_element_type=jnp.float32
        )
        value_part = lax.dot_general(
            probs_b, grad_rows, CONTRACT_FIRST, preferred_element_type=jnp.float32
        )
        return jnp.concatenate([key_part, value_part], axis=1)

    start_query = jnp.zeros((query_count, DH), jnp.float32)

    def query_step(step, query_acc):
        probs_b, slopes, key_block = slopes_at(step * block, block)
        return query_acc + jnp.dot(slopes, key_block, preferred_element_type=jnp.float32)

    query_acc = lax.fori_loop(0, blocks, query_step, start_query)
    width = math.gcd(tok_dev * lax.axis_size("ctx"), block)

    def inner(step, acc):
        offset = step * width
        probs_b, slopes, key_block = slopes_at(offset, width)
        return lax.dynamic_update_slice_in_dim(acc, key_terms(probs_b, slopes), offset, 0)

    own_grads = lax.psum_scatter(
        lax.fori_loop(
            0,
            tok_dev * lax.axis_size("ctx") // width,
            inner,
            jnp.zeros((tok_dev * lax.axis_size("ctx"), 2 * DH), jnp.float32),
        ),
        "ctx",
        scatter_dimension=0,
        tiled=True,
    )
    query_grad = (
        query_acc.reshape(heads, tok_dev, DH)
        .transpose(1, 0, 2)
        .reshape(tok_dev, heads * DH)
        .astype(jnp.bfloat16)
    )
    members = lax.all_gather(own_grads.astype(jnp.bfloat16), "fsdp", axis=0, tiled=True).astype(
        own_grads.dtype
    )
    per_group = members.reshape(KVG, -1, tok_dev, 2 * DH).sum(axis=1)
    key_grads = (
        per_group[:, :, :DH].transpose(1, 0, 2).reshape(tok_dev, KVG * DH).astype(jnp.bfloat16)
    )
    value_grads = (
        per_group[:, :, DH:].transpose(1, 0, 2).reshape(tok_dev, KVG * DH).astype(jnp.bfloat16)
    )
    both_grads = jnp.concatenate([key_grads, value_grads], axis=1)
    columns = KVG * DH
    raw = lax.psum(
        lax.dot_general(hidden, both_grads, CONTRACT_FIRST, preferred_element_type=jnp.float32),
        "ctx",
    )
    key_f = key_weight.astype(jnp.float32)
    value_f = value_weight.astype(jnp.float32)
    grad_sq, key_sq, value_sq = lax.psum(
        (
            jnp.sum(raw * raw, axis=0),
            jnp.sum(key_f * key_f, axis=0),
            jnp.sum(value_f * value_f, axis=0),
        ),
        "fsdp",
    )
    weight_norm = jnp.sqrt(jnp.concatenate([key_sq, value_sq]) + EPSILON)
    grad_norm = jnp.sqrt(grad_sq + EPSILON)
    clipped = raw * jnp.minimum(1.0, CLIP_RATE * total * weight_norm / grad_norm)[None, :]
    return (query_grad, clipped[:, :columns], clipped[:, columns:])


SIDES = 2
MEMBERS = 2
DIGIT = 64


def pack_kernel(
    ids, keys, values, queries, out_grad, positions, hidden, kv_out, qd_out, held, place, sems
):
    tok_dev = queries.shape[0]
    columns = pl.ds(pl.multiple_of(ids[2] * DH, DH), DH)
    copies = [
        pltpu.make_async_copy(source, target, sems.at[i])
        for i, (source, target) in enumerate(
            (
                (positions, place),
                (keys.at[:, columns], kv_out.at[:, :DH]),
                (values.at[:, columns], kv_out.at[:, DH:]),
                (queries, qd_out.at[:tok_dev]),
                (out_grad, qd_out.at[tok_dev : 2 * tok_dev]),
                (hidden, held),
            )
        )
    ]
    for copy in copies:
        copy.start()
    rest = qd_out.shape[1] - tok_dev
    if rest > 0:
        qd_out[2 * tok_dev :, tok_dev:] = jnp.zeros((qd_out.shape[0] - 2 * tok_dev, rest), jnp.bfloat16)
    copies[0].wait()
    high = place[...] // DIGIT
    low = place[...] - high * DIGIT
    pad = jnp.zeros((qd_out.shape[0] - 2 * tok_dev - 2, tok_dev), jnp.float32)
    digits = jnp.concatenate([high.astype(jnp.float32), low.astype(jnp.float32), pad], axis=0)
    qd_out[2 * tok_dev :, :tok_dev] = digits.astype(jnp.bfloat16)
    for copy in copies[1:]:
        copy.wait()


def nothing_kernel(*refs):
    pass


def after(xs, *events):
    count = len(xs)
    return pl.pallas_call(
        nothing_kernel,
        out_shape=tuple(jax.ShapeDtypeStruct(x.shape, x.dtype) for x in xs),
        in_specs=[ANY] * (count + len(events)),
        out_specs=(ANY,) * count,
        input_output_aliases={i: i for i in range(count)},
        compiler_params=pltpu.CompilerParams(vmem_limit_bytes=2**20),
    )(*xs, *events)


def halves_kernel(*refs):
    up, down, (up_half, down_half, sems) = refs[0], refs[1], refs[-3:]
    half = up_half.shape[0]
    copies = [
        pltpu.make_async_copy(up.at[:half], up_half, sems.at[0]),
        pltpu.make_async_copy(down.at[half:], down_half, sems.at[1]),
    ]
    for copy in copies:
        copy.start()
    for copy in copies:
        copy.wait()


def halves_after(up, down, *events):
    half = jax.ShapeDtypeStruct((up.shape[0] // 2, up.shape[1]), up.dtype)
    return pl.pallas_call(
        halves_kernel,
        out_shape=(half, half),
        in_specs=[ANY] * (2 + len(events)),
        out_specs=(ANY, ANY),
        scratch_shapes=[pltpu.SemaphoreType.DMA((2,))],
        compiler_params=pltpu.CompilerParams(vmem_limit_bytes=2**20),
    )(up, down, *events)


def seen_pairs(ids, owner, planes, tok_dev, qd):
    last = 2 * planes * SIDES - 1
    half = tok_dev // 2

    def place_of(at, block):
        stretch = owner[block]
        return jnp.where(at < half, at + stretch * half, at - half + (last - stretch) * half)

    row = lax.broadcasted_iota(jnp.int32, (tok_dev, tok_dev), 0)
    key_place = jnp.concatenate(
        [place_of(row, (ids[0] ^ j) * SIDES + ids[1]) for j in range(planes)], axis=0
    )
    lane = lax.broadcasted_iota(jnp.int32, (1, tok_dev), 1)
    seen = []
    for side in range(SIDES):
        place = place_of(lane, ids[0] * SIDES + (ids[1] ^ side))
        digits = qd[side][2 * tok_dev :, :tok_dev].astype(jnp.float32)
        back = (digits[0:1] * DIGIT + digits[1:2]).astype(jnp.int32)
        seen.append((key_place <= place) & (key_place >= place - back))
    return seen


def scaled_scores(k, q, scale):
    return lax.dot_general(k, q, CONTRACT_LAST, preferred_element_type=jnp.float32) * scale


def stats_kernel(planes, ids, owner, *refs):
    kv_refs, qd, stats = refs[:planes], refs[planes : planes + SIDES], refs[-1]
    tok_dev = kv_refs[0].shape[0]
    heads = qd[0].shape[1] // DH
    scale = 1.0 / math.sqrt(DH)
    kv = jnp.concatenate([ref[...] for ref in kv_refs], axis=0)
    k, v = kv[:, :DH], kv[:, DH:]
    seen = seen_pairs(ids, owner, planes, tok_dev, qd)
    tiles = SIDES * heads
    for side in range(SIDES):
        for head in range(heads):
            q = qd[side][:tok_dev, head * DH : (head + 1) * DH]
            d = qd[side][tok_dev : 2 * tok_dev, head * DH : (head + 1) * DH]
            scores = jnp.where(seen[side], scaled_scores(k, q, scale), NEGATIVE)
            dprobs = lax.dot_general(v, d, CONTRACT_LAST, preferred_element_type=jnp.float32)
            top = jnp.max(scores, axis=0, keepdims=True)
            weights = jnp.where(seen[side], jnp.exp(scores - top), 0.0)
            tile = side * heads + head
            stats[tile : tile + 1] = top
            stats[tiles + tile : tiles + tile + 1] = jnp.sum(weights, axis=0, keepdims=True)
            stats[2 * tiles + tile : 2 * tiles + tile + 1] = jnp.sum(
                weights * dprobs, axis=0, keepdims=True
            )


def grads_kernel(planes, ids, owner, *refs):
    kv_refs, refs = refs[:planes], refs[planes:]
    qd, refs = refs[:SIDES], refs[SIDES:]
    stats, (keep, give, slopes_out, acc) = refs[:SIDES], refs[SIDES:]
    tok_dev = kv_refs[0].shape[0]
    half = tok_dev // 2
    heads = qd[0].shape[1] // DH
    scale = 1.0 / math.sqrt(DH)
    kv = jnp.concatenate([ref[...] for ref in kv_refs], axis=0)
    k, v = kv[:, :DH], kv[:, DH:]
    seen = seen_pairs(ids, owner, planes, tok_dev, qd)
    tiles = SIDES * heads
    key_acc = jnp.zeros((planes * tok_dev, DH), jnp.float32)
    value_acc = jnp.zeros((planes * tok_dev, DH), jnp.float32)
    for side in range(SIDES):
        q_rows, d_rows, slope_tiles, prob_tiles = [], [], [], []
        parts = [
            [
                stats[other][kind * tiles + (side ^ other) * heads :][:heads]
                for other in range(SIDES)
            ]
            for kind in range(3)
        ]
        top = functools.reduce(jnp.maximum, parts[0])
        shares = [jnp.exp(part - top) for part in parts[0]]
        mass = sum(share * part for share, part in zip(shares, parts[1], strict=True))
        lse = top + jnp.log(mass)
        delta = sum(share * part for share, part in zip(shares, parts[2], strict=True)) / mass
        for head in range(heads):
            q = qd[side][:tok_dev, head * DH : (head + 1) * DH]
            d = qd[side][tok_dev : 2 * tok_dev, head * DH : (head + 1) * DH]
            scores = scaled_scores(k, q, scale)
            dprobs = lax.dot_general(v, d, CONTRACT_LAST, preferred_element_type=jnp.float32)
            probs = jnp.where(seen[side], jnp.exp(scores - lse[head : head + 1]), 0.0)
            slopes = (probs * (dprobs - delta[head : head + 1]) * scale).astype(jnp.bfloat16)
            q_rows.append(q)
            d_rows.append(d)
            slope_tiles.append(slopes)
            prob_tiles.append(probs.astype(jnp.bfloat16))
        slope_tile = jnp.concatenate(slope_tiles, axis=1)
        slopes_out[side] = slope_tile
        key_acc += jnp.dot(
            slope_tile,
            jnp.concatenate(q_rows, axis=0),
            preferred_element_type=jnp.float32,
        )
        value_acc += jnp.dot(
            jnp.concatenate(prob_tiles, axis=1),
            jnp.concatenate(d_rows, axis=0),
            preferred_element_type=jnp.float32,
        )
    acc[:, :DH] = key_acc
    acc[:, DH:] = value_acc
    for j in range(planes):
        rows = slice(j * half, (j + 1) * half)
        own = pl.multiple_of(j * tok_dev + ids[3] * half, half)
        other = pl.multiple_of(j * tok_dev + (1 - ids[3]) * half, half)
        keep[rows] = acc[pl.ds(own, half)]
        give[rows] = acc[pl.ds(other, half)].astype(give.dtype)


def members_kernel(keep, got, *outs):
    half = outs[0].shape[0]
    for j, out in enumerate(outs):
        rows = slice(j * half, (j + 1) * half)
        out[...] = (keep[rows] + got[rows].astype(jnp.float32)).astype(out.dtype)


def query_kernel(planes, *refs):
    kv_refs, slopes, q_out = refs[:planes], refs[planes], refs[planes + 3 :]
    k = jnp.concatenate([ref[:, :DH] for ref in kv_refs], axis=0)
    for source, out in enumerate(q_out):
        tok_dev, width = out.shape
        for head in range(width // DH):
            tile = slopes[source, :, head * tok_dev : (head + 1) * tok_dev]
            part = lax.dot_general(tile, k, CONTRACT_FIRST, preferred_element_type=jnp.float32)
            out[:, head * DH : (head + 1) * DH] = part.astype(out.dtype)


def join_kernel(event, other_event, *refs):
    rows = refs[0].shape[0]
    for i, ref in enumerate(refs[:-1]):
        refs[-1][i * rows : (i + 1) * rows] = ref[...]


def sum_kernel(*refs):
    total = refs[0][...].astype(jnp.float32)
    for ref in refs[1:-1]:
        total += ref[...].astype(jnp.float32)
    refs[-1][...] = total.astype(refs[-1].dtype)


def square_kernel(key_weight, value_weight, out):
    width = key_weight.shape[1]

    @pl.when(pl.program_id(0) == 0)
    def _():
        out[...] = jnp.zeros_like(out)

    k = key_weight[...].astype(jnp.float32)
    v = value_weight[...].astype(jnp.float32)
    out[:, :width] += jnp.sum((k * k).reshape(-1, 8, width), axis=0)
    out[:, width:] += jnp.sum((v * v).reshape(-1, 8, width), axis=0)


def spot_of(ids, planes, distance):
    count = planes * SIDES
    spot = jnp.where(ids[1] == 0, ids[0], count - 1 - ids[0]) + distance
    return jnp.where(spot >= count, spot - count, spot)


def order_kernel(planes, distances, ids, *refs):
    for r, block in zip(distances, refs[:-1], strict=True):
        refs[-1][spot_of(ids, planes, r)] = block[...]


def project_kernel(planes, steps, ids, squares, *refs):
    count = planes * SIDES
    before, beyond, first, second, refs = *refs[1:5], refs[5:]
    pieces, (raw, sums, held, grads) = refs[:8], refs[8:]
    tok_dev = held.shape[1]
    half = tok_dev // 2
    tile = raw.shape[0] // steps
    spot = spot_of(ids, planes, count // 2)
    held[spot, :half] = first[...]
    held[spot, half:] = second[...]
    held[spot_of(ids, planes, count // 2 - 1)] = before[...]
    held[spot_of(ids, planes, count // 2 + 1)] = beyond[...]
    for index, piece in enumerate(pieces):
        side = ids[1] ^ (index & 1)
        group = ids[2] ^ ((index >> 1) & 1)
        member = ids[3] ^ ((index >> 2) & 1)
        for j in range(planes):
            plane = ids[0] ^ j
            spot = jnp.where(side == 0, plane, count - 1 - plane)
            rows = pl.ds(pl.multiple_of(spot * tok_dev + member * half, half), half)
            for kind in range(2):
                columns = pl.ds(pl.multiple_of((kind * KVG + group) * DH, DH), DH)
                grads[rows, columns] = piece[
                    j * half : (j + 1) * half, kind * DH : (kind + 1) * DH
                ]
    width = raw.shape[1]
    acc = jnp.zeros((8, width), jnp.float32)
    for i in range(steps):
        rows = slice(i * tile, (i + 1) * tile)
        block = held[:, :, rows].reshape(count * tok_dev, tile)
        out = lax.dot_general(
            block, grads[...], CONTRACT_FIRST, preferred_element_type=jnp.float32
        )
        raw[rows] = out
        acc += jnp.sum((out * out).reshape(-1, 8, width), axis=0)
    total = jnp.sum(acc, axis=0, keepdims=True)
    weights = jnp.sum(squares[...], axis=0, keepdims=True)
    row = lax.broadcasted_iota(jnp.int32, sums.shape, 0)
    sums[...] = jnp.where(row == 0, total, weights)


def scale_kernel(factor, steps, sums, sums_1, sums_2, sums_3, raw, *refs):
    outs, helds, sems = refs[:2], refs[2:4], refs[4]
    total = (sums[...] + sums_1[...]) + (sums_2[...] + sums_3[...])
    grad_norm = jnp.sqrt(total[0:1] + EPSILON)
    weight_norm = jnp.sqrt(total[1:2] + EPSILON)
    clip = jnp.minimum(1.0, factor * weight_norm / grad_norm)
    width = outs[0].shape[1]
    tile = raw.shape[0] // steps
    copies = []
    for i in range(steps):
        rows = pl.ds(i * tile, tile)
        for kind, (out, held) in enumerate(zip(outs, helds, strict=True)):
            columns = slice(kind * width, (kind + 1) * width)
            held[rows] = raw[rows, columns] * clip[:, columns]
            copy = pltpu.make_async_copy(held.at[rows], out.at[rows], sems.at[2 * i + kind])
            copy.start()
            copies.append(copy)
    for copy in copies:
        copy.wait()


def local_small(
    queries, keys, values, out_grad, hidden, key_weight, value_weight, stretch_owner, positions
):
    tok_dev, width = queries.shape
    half = tok_dev // 2
    count = lax.axis_size("ctx")
    planes = count // SIDES
    groups = lax.axis_size("fsdp") // MEMBERS
    total = tok_dev * count
    ctx, fsdp = lax.axis_index("ctx"), lax.axis_index("fsdp")
    ids = jnp.stack([ctx // SIDES, ctx % SIDES, fsdp // MEMBERS, fsdp % MEMBERS]).astype(jnp.int32)
    bf16, f32 = jnp.bfloat16, jnp.float32
    shape = jax.ShapeDtypeStruct

    def call(kernel, ins, outs, mib=8, **more):
        return pl.pallas_call(
            kernel,
            out_shape=outs,
            in_specs=ins,
            out_specs=jax.tree.map(lambda _: VMEM, outs),
            compiler_params=pltpu.CompilerParams(vmem_limit_bytes=mib * 2**20),
            **more,
        )

    def move(x, plane=0, side=0, group=0, member=0):
        pairs = []
        fs = groups * MEMBERS
        for i in range(count):
            for j in range(fs):
                p, s = i // SIDES ^ plane, i % SIDES ^ side
                g, m = j // MEMBERS ^ group, j % MEMBERS ^ member
                pairs.append((i * fs + j, (p * SIDES + s) * fs + g * MEMBERS + m))
        return lax.ppermute(x, ("ctx", "fsdp"), pairs)

    ring = [p * SIDES for p in range(planes)] + [p * SIDES + 1 for p in reversed(range(planes))]

    def around(x, step):
        pairs = [(ring[i], ring[(i + step) % count]) for i in range(count)]
        return lax.ppermute(x, "ctx", pairs)

    rows = hidden.shape[1]

    far = [
        pltpu.with_memory_space_constraint(x, pltpu.HBM)
        for x in (keys, values, queries, out_grad, positions.reshape(1, tok_dev), hidden)
    ]
    kv, qd, held = call(
        pack_kernel,
        [SMEM] + [ANY] * 6,
        (
            shape((tok_dev, 2 * DH), bf16),
            shape((2 * tok_dev + 16, width), bf16),
            shape(hidden.shape, bf16),
        ),
        scratch_shapes=[
            pltpu.VMEM((1, tok_dev), jnp.int32),
            pltpu.SemaphoreType.DMA((6,)),
        ],
    )(ids, *far)
    qd_side = move(qd, side=1)
    kv_all = [kv] + [move(kv, plane=j) for j in range(1, planes)]
    qd_all = [qd, qd_side]
    (held,) = after((held,), qd_side, *kv_all[1:])
    blocks = {0: held}
    up, down = around(held, 1), around(held, -1)

    columns = 2 * KVG * DH
    steps = 8
    tile = rows // steps
    weight = pl.BlockSpec((tile, columns // 2), lambda i: (i, 0))
    squares = pl.pallas_call(
        square_kernel,
        grid=(steps,),
        out_shape=shape((8, columns), f32),
        in_specs=[weight] * 2,
        out_specs=pl.BlockSpec((8, columns), lambda i: (0, 0)),
        compiler_params=pltpu.CompilerParams(vmem_limit_bytes=8 * 2**20),
    )(key_weight, value_weight)

    tiles = SIDES * width // DH
    stats = call(
        functools.partial(stats_kernel, planes),
        [SMEM] * 2 + [VMEM] * (planes + SIDES),
        shape((3 * tiles, tok_dev), f32),
    )(ids, stretch_owner, *kv_all, *qd_all)
    stats_side = move(stats, side=1)
    blocks[count - 1], blocks[1] = after((up, down), stats_side)
    up, down = around(blocks[count - 1], 1), around(blocks[1], -1)
    grads_shape = (planes * half, 2 * DH)
    keep, give, slopes = call(
        functools.partial(grads_kernel, planes),
        [SMEM] * 2 + [VMEM] * (planes + 2 * SIDES),
        (
            shape(grads_shape, f32),
            shape(grads_shape, bf16),
            shape((SIDES, planes * tok_dev, tok_dev * width // DH), bf16),
        ),
        scratch_shapes=[pltpu.VMEM((planes * tok_dev, 2 * DH), f32)],
    )(ids, stretch_owner, *kv_all, *qd_all, stats, stats_side)
    kv_parts = call(
        members_kernel,
        [VMEM] * 2,
        tuple(shape((half, 2 * DH), bf16 if j else f32) for j in range(planes)),
    )(keep, move(give, member=1))
    piece = call(sum_kernel, [VMEM] * planes, shape((half, 2 * DH), bf16))(
        kv_parts[0], *[move(kv_parts[j], plane=j) for j in range(1, planes)]
    )
    blocks[count - 2], blocks[2] = after((up, down), piece)
    up, down = around(blocks[count - 2], 1), around(blocks[2], -1)
    parts = [move(piece, plane=j) for j in range(1, planes)]
    q_parts = call(
        functools.partial(query_kernel, planes),
        [VMEM] * (planes + 1) + [ANY] * 2,
        tuple(shape((tok_dev, width), bf16 if j else f32) for j in range(SIDES)),
    )(*kv_all, slopes, piece, squares)
    early = tuple(range(count // 2 - 1)) + tuple(range(count // 2 + 2, count))
    ordered = call(
        functools.partial(order_kernel, planes, early),
        [SMEM] + [VMEM] * len(early),
        pltpu.VMEM((count,) + hidden.shape, bf16),
    )(ids, *[blocks[r] for r in early])
    piece_all = call(join_kernel, [ANY] * 2 + [VMEM] * planes, shape(grads_shape, bf16))(
        q_parts[1], ordered, piece, *parts
    )
    blocks[count - 3], blocks[3] = up, down
    up, down = halves_after(up, down, piece_all)
    blocks[4], blocks[count] = around(up, 1), around(down, -1)
    piece_side = move(piece_all, side=1)
    (piece_side,) = after((piece_side,), up)
    near = [piece_all, piece_side, move(piece_all, group=1), move(piece_side, group=1)]
    pieces = near + [move(part, member=1) for part in near]

    query_grad = call(sum_kernel, [VMEM] * SIDES, shape((tok_dev, width), bf16))(
        q_parts[0], move(q_parts[1], side=1)
    )

    steps = 2
    raw, sums, _ = call(
        functools.partial(project_kernel, planes, steps),
        [SMEM] + [VMEM] * (6 + len(pieces)),
        (
            pltpu.VMEM((rows, columns), f32),
            shape((8, columns), f32),
            pltpu.VMEM(ordered.shape, bf16),
        ),
        mib=12,
        scratch_shapes=[pltpu.VMEM((total, columns), bf16)],
        input_output_aliases={2: 2},
    )(
        ids,
        squares,
        pltpu.with_memory_space_constraint(ordered, pltpu.VMEM),
        blocks[count // 2 - 1],
        blocks[count // 2 + 1],
        blocks[count // 2],
        blocks[count],
        *pieces,
    )
    sums_all = [sums, move(sums, member=1), move(sums, group=1), move(sums, group=1, member=1)]
    steps = 8
    key_grad, value_grad = pl.pallas_call(
        functools.partial(scale_kernel, CLIP_RATE * total, steps),
        out_shape=(shape((rows, columns // 2), f32),) * 2,
        in_specs=[VMEM] * 5,
        out_specs=(ANY, ANY),
        scratch_shapes=[pltpu.VMEM((rows, columns // 2), f32)] * 2
        + [pltpu.SemaphoreType.DMA((2 * steps,))],
        compiler_params=pltpu.CompilerParams(vmem_limit_bytes=8 * 2**20),
    )(*sums_all, pltpu.with_memory_space_constraint(raw, pltpu.VMEM))
    return (query_grad, key_grad, value_grad)


def solution(mesh):
    ctx_count, fsdp_count = mesh.shape["ctx"], mesh.shape["fsdp"]

    def program(queries, keys, values, out_grad, hidden, *rest):
        tok_dev = queries.shape[0] // ctx_count
        heads = queries.shape[1] // fsdp_count // DH
        gathered = hidden.size // fsdp_count * hidden.dtype.itemsize
        planes = ctx_count // SIDES
        small = (
            ctx_count == 8
            and gathered <= GATHER_LIMIT
            and planes * SIDES == ctx_count
            and planes & (planes - 1) == 0
            and heads * MEMBERS == HPG
            and fsdp_count == KVG * MEMBERS
            and tok_dev == DH
        )
        return jax.shard_map(
            local_small if small else local_large,
            mesh=mesh,
            in_specs=(
                P("ctx", "fsdp"),
                P("ctx", None),
                P("ctx", None),
                P("ctx", "fsdp"),
                P("ctx", "fsdp"),
                P("fsdp", None),
                P("fsdp", None),
                P(),
                P("ctx"),
            ),
            out_specs=(P("ctx", "fsdp"), P("fsdp", None), P("fsdp", None)),
            check_vma=False,
        )(queries, keys, values, out_grad, hidden, *rest)

    return program
```

```python
import functools
import math

import jax
import jax.numpy as jnp
from jax import lax
from jax.experimental import pallas as pl
from jax.experimental.pallas import tpu as pltpu
from jax.sharding import PartitionSpec as P

DH = 128
HPG = 8
KVG = 2


CLIP_RATE = 0.02
EPSILON = 1e-06
NEGATIVE = -1e30
GATHER_LIMIT = 8 * 2**20

CONTRACT_LAST = (((1,), (1,)), ((), ()))
CONTRACT_FIRST = (((0,), (0,)), ((), ()))
VMEM = pl.BlockSpec(memory_space=pltpu.VMEM)
SMEM = pl.BlockSpec(memory_space=pltpu.SMEM)
ANY = pl.BlockSpec(memory_space=pl.ANY)


def rows_by_head(block, heads, width):
    count = block.shape[0]
    return block.reshape(count, heads, width).transpose(1, 0, 2).reshape(heads * count, width)


def local_large(
    queries, keys, values, out_grad, hidden, key_weight, value_weight, stretch_owner, positions
):
    tok_dev = queries.shape[0]
    heads = queries.shape[1] // DH
    ctx_count = lax.axis_size("ctx")
    total = tok_dev * ctx_count
    half = tok_dev // 2
    ctx_index = lax.axis_index("ctx")
    group = lax.axis_index("fsdp") * heads // HPG
    scale = 1.0 / math.sqrt(DH)
    block = min(512, total)
    blocks = total // block
    query_count = heads * tok_dev
    own_keys = lax.dynamic_slice_in_dim(keys, group * DH, DH, 1)
    own_values = lax.dynamic_slice_in_dim(values, group * DH, DH, 1)
    all_keys, all_values = (
        lax.all_gather(own_keys, "ctx", axis=0, tiled=True),
        lax.all_gather(own_values, "ctx", axis=0, tiled=True),
    )
    offsets = jnp.arange(half, dtype=jnp.int32)
    stretches = jnp.stack([stretch_owner, 2 * ctx_count - 1 - stretch_owner], axis=1)
    key_place = (stretches[:, :, None] * half + offsets[None, None, :]).reshape(total)
    mine = lax.dynamic_slice_in_dim(stretches, ctx_index, 1, 0)[0]
    local_place = (mine[:, None] * half + offsets[None, :]).reshape(tok_dev)
    query_place = jnp.tile(local_place, heads)
    query_floor = jnp.tile(local_place - positions, heads)
    query_rows = rows_by_head(queries, heads, DH)
    grad_rows = rows_by_head(out_grad, heads, DH)

    def scores_at(start, width):
        key_block = lax.dynamic_slice_in_dim(all_keys, start, width, 0)
        place = lax.dynamic_slice_in_dim(key_place, start, width, 0)
        raw = (
            lax.dot_general(
                query_rows, key_block, CONTRACT_LAST, preferred_element_type=jnp.float32
            )
            * scale
        )
        seen = (place[None, :] <= query_place[:, None]) & (place[None, :] >= query_floor[:, None])
        return (jnp.where(seen, raw, NEGATIVE), seen, key_block)

    def stats_step(step, carry):
        top, mass = carry
        masked, seen, key_block = scores_at(step * block, block)
        new_top = jnp.maximum(top, jnp.max(masked, axis=1))
        weights = jnp.where(seen, jnp.exp(masked - new_top[:, None]), 0.0)
        mass = mass * jnp.exp(top - new_top) + jnp.sum(weights, axis=1)
        return (new_top, mass)

    start_top = jnp.full((query_count,), NEGATIVE, jnp.float32)
    start_mass = jnp.zeros((query_count,), jnp.float32)
    top, mass = lax.fori_loop(0, blocks, stats_step, (start_top, start_mass))
    lse = top + jnp.log(mass)

    def probs_at(start, width):
        masked, seen, key_block = scores_at(start, width)
        probs = jnp.where(seen, jnp.exp(masked - lse[:, None]), 0.0)
        value_block = lax.dynamic_slice_in_dim(all_values, start, width, 0)
        dprobs = lax.dot_general(
            grad_rows, value_block, CONTRACT_LAST, preferred_element_type=jnp.float32
        )
        return (probs, dprobs, key_block)

    def delta_step(step, acc):
        probs, dprobs, key_block = probs_at(step * block, block)
        return acc + jnp.sum(probs * dprobs, axis=1)

    delta = lax.fori_loop(0, blocks, delta_step, jnp.zeros((query_count,), jnp.float32))

    def slopes_at(start, width):
        probs, dprobs, key_block = probs_at(start, width)
        slopes = (probs * (dprobs - delta[:, None]) * scale).astype(jnp.bfloat16)
        return (probs.astype(jnp.bfloat16), slopes, key_block)

    def key_terms(probs_b, slopes):
        key_part = lax.dot_general(
            slopes, query_rows, CONTRACT_FIRST, preferred_element_type=jnp.float32
        )
        value_part = lax.dot_general(
            probs_b, grad_rows, CONTRACT_FIRST, preferred_element_type=jnp.float32
        )
        return jnp.concatenate([key_part, value_part], axis=1)

    start_query = jnp.zeros((query_count, DH), jnp.float32)

    def query_step(step, query_acc):
        probs_b, slopes, key_block = slopes_at(step * block, block)
        return query_acc + jnp.dot(slopes, key_block, preferred_element_type=jnp.float32)

    query_acc = lax.fori_loop(0, blocks, query_step, start_query)
    width = math.gcd(tok_dev * lax.axis_size("ctx"), block)

    def inner(step, acc):
        offset = step * width
        probs_b, slopes, key_block = slopes_at(offset, width)
        return lax.dynamic_update_slice_in_dim(acc, key_terms(probs_b, slopes), offset, 0)

    own_grads = lax.psum_scatter(
        lax.fori_loop(
            0,
            tok_dev * lax.axis_size("ctx") // width,
            inner,
            jnp.zeros((tok_dev * lax.axis_size("ctx"), 2 * DH), jnp.float32),
        ),
        "ctx",
        scatter_dimension=0,
        tiled=True,
    )
    query_grad = (
        query_acc.reshape(heads, tok_dev, DH)
        .transpose(1, 0, 2)
        .reshape(tok_dev, heads * DH)
        .astype(jnp.bfloat16)
    )
    members = lax.all_gather(own_grads.astype(jnp.bfloat16), "fsdp", axis=0, tiled=True).astype(
        own_grads.dtype
    )
    per_group = members.reshape(KVG, -1, tok_dev, 2 * DH).sum(axis=1)
    key_grads = (
        per_group[:, :, :DH].transpose(1, 0, 2).reshape(tok_dev, KVG * DH).astype(jnp.bfloat16)
    )
    value_grads = (
        per_group[:, :, DH:].transpose(1, 0, 2).reshape(tok_dev, KVG * DH).astype(jnp.bfloat16)
    )
    both_grads = jnp.concatenate([key_grads, value_grads], axis=1)
    columns = KVG * DH
    raw = lax.psum(
        lax.dot_general(hidden, both_grads, CONTRACT_FIRST, preferred_element_type=jnp.float32),
        "ctx",
    )
    key_f = key_weight.astype(jnp.float32)
    value_f = value_weight.astype(jnp.float32)
    grad_sq, key_sq, value_sq = lax.psum(
        (
            jnp.sum(raw * raw, axis=0),
            jnp.sum(key_f * key_f, axis=0),
            jnp.sum(value_f * value_f, axis=0),
        ),
        "fsdp",
    )
    weight_norm = jnp.sqrt(jnp.concatenate([key_sq, value_sq]) + EPSILON)
    grad_norm = jnp.sqrt(grad_sq + EPSILON)
    clipped = raw * jnp.minimum(1.0, CLIP_RATE * total * weight_norm / grad_norm)[None, :]
    return (query_grad, clipped[:, :columns], clipped[:, columns:])


SIDES = 2
MEMBERS = 2
DIGIT = 64


def pack_kernel(
    ids, keys, values, queries, out_grad, positions, kv_out, qd_out, place, sems
):
    tok_dev = queries.shape[0]
    columns = pl.ds(pl.multiple_of(ids[2] * DH, DH), DH)
    copies = [
        pltpu.make_async_copy(source, target, sems.at[i])
        for i, (source, target) in enumerate(
            (
                (positions, place),
                (keys.at[:, columns], kv_out.at[:, :DH]),
                (values.at[:, columns], kv_out.at[:, DH:]),
                (queries, qd_out.at[:tok_dev]),
                (out_grad, qd_out.at[tok_dev : 2 * tok_dev]),
            )
        )
    ]
    for copy in copies:
        copy.start()
    rest = qd_out.shape[1] - tok_dev
    if rest > 0:
        qd_out[2 * tok_dev :, tok_dev:] = jnp.zeros((qd_out.shape[0] - 2 * tok_dev, rest), jnp.bfloat16)
    copies[0].wait()
    high = place[...] // DIGIT
    low = place[...] - high * DIGIT
    pad = jnp.zeros((qd_out.shape[0] - 2 * tok_dev - 2, tok_dev), jnp.float32)
    digits = jnp.concatenate([high.astype(jnp.float32), low.astype(jnp.float32), pad], axis=0)
    qd_out[2 * tok_dev :, :tok_dev] = digits.astype(jnp.bfloat16)
    for copy in copies[1:]:
        copy.wait()


def nothing_kernel(*refs):
    pass


def after(xs, *events):
    count = len(xs)
    return pl.pallas_call(
        nothing_kernel,
        out_shape=tuple(jax.ShapeDtypeStruct(x.shape, x.dtype) for x in xs),
        in_specs=[ANY] * (count + len(events)),
        out_specs=(ANY,) * count,
        input_output_aliases={i: i for i in range(count)},
        compiler_params=pltpu.CompilerParams(vmem_limit_bytes=2**20),
    )(*xs, *events)


def halves_kernel(*refs):
    up, down, (up_half, down_half, sems) = refs[0], refs[1], refs[-3:]
    half = up_half.shape[0]
    copies = [
        pltpu.make_async_copy(up.at[:half], up_half, sems.at[0]),
        pltpu.make_async_copy(down.at[half:], down_half, sems.at[1]),
    ]
    for copy in copies:
        copy.start()
    for copy in copies:
        copy.wait()


def halves_after(up, down, *events):
    half = jax.ShapeDtypeStruct((up.shape[0] // 2, up.shape[1]), up.dtype)
    return pl.pallas_call(
        halves_kernel,
        out_shape=(half, half),
        in_specs=[ANY] * (2 + len(events)),
        out_specs=(ANY, ANY),
        scratch_shapes=[pltpu.SemaphoreType.DMA((2,))],
        compiler_params=pltpu.CompilerParams(vmem_limit_bytes=2**20),
    )(up, down, *events)


def seen_pairs(ids, owner, planes, tok_dev, qd):
    last = 2 * planes * SIDES - 1
    half = tok_dev // 2

    def place_of(at, block):
        stretch = owner[block]
        return jnp.where(at < half, at + stretch * half, at - half + (last - stretch) * half)

    row = lax.broadcasted_iota(jnp.int32, (tok_dev, tok_dev), 0)
    key_place = jnp.concatenate(
        [place_of(row, (ids[0] ^ j) * SIDES + ids[1]) for j in range(planes)], axis=0
    )
    lane = lax.broadcasted_iota(jnp.int32, (1, tok_dev), 1)
    seen = []
    for side in range(SIDES):
        place = place_of(lane, ids[0] * SIDES + (ids[1] ^ side))
        digits = qd[side][2 * tok_dev :, :tok_dev].astype(jnp.float32)
        back = (digits[0:1] * DIGIT + digits[1:2]).astype(jnp.int32)
        seen.append((key_place <= place) & (key_place >= place - back))
    return seen


def scaled_scores(k, q, scale):
    return lax.dot_general(k, q, CONTRACT_LAST, preferred_element_type=jnp.float32) * scale


def stats_kernel(planes, ids, owner, *refs):
    kv_refs, qd, stats = refs[:planes], refs[planes : planes + SIDES], refs[-1]
    tok_dev = kv_refs[0].shape[0]
    heads = qd[0].shape[1] // DH
    scale = 1.0 / math.sqrt(DH)
    kv = jnp.concatenate([ref[...] for ref in kv_refs], axis=0)
    k, v = kv[:, :DH], kv[:, DH:]
    seen = seen_pairs(ids, owner, planes, tok_dev, qd)
    tiles = SIDES * heads
    for side in range(SIDES):
        for head in range(heads):
            q = qd[side][:tok_dev, head * DH : (head + 1) * DH]
            d = qd[side][tok_dev : 2 * tok_dev, head * DH : (head + 1) * DH]
            scores = jnp.where(seen[side], scaled_scores(k, q, scale), NEGATIVE)
            dprobs = lax.dot_general(v, d, CONTRACT_LAST, preferred_element_type=jnp.float32)
            top = jnp.max(scores, axis=0, keepdims=True)
            weights = jnp.where(seen[side], jnp.exp(scores - top), 0.0)
            tile = side * heads + head
            stats[tile : tile + 1] = top
            stats[tiles + tile : tiles + tile + 1] = jnp.sum(weights, axis=0, keepdims=True)
            stats[2 * tiles + tile : 2 * tiles + tile + 1] = jnp.sum(
                weights * dprobs, axis=0, keepdims=True
            )


def grads_kernel(planes, ids, owner, *refs):
    kv_refs, refs = refs[:planes], refs[planes:]
    qd, refs = refs[:SIDES], refs[SIDES:]
    stats, (keep, give, slopes_out, acc) = refs[:SIDES], refs[SIDES:]
    tok_dev = kv_refs[0].shape[0]
    half = tok_dev // 2
    heads = qd[0].shape[1] // DH
    scale = 1.0 / math.sqrt(DH)
    kv = jnp.concatenate([ref[...] for ref in kv_refs], axis=0)
    k, v = kv[:, :DH], kv[:, DH:]
    seen = seen_pairs(ids, owner, planes, tok_dev, qd)
    tiles = SIDES * heads
    key_acc = jnp.zeros((planes * tok_dev, DH), jnp.float32)
    value_acc = jnp.zeros((planes * tok_dev, DH), jnp.float32)
    for side in range(SIDES):
        q_rows, d_rows, slope_tiles, prob_tiles = [], [], [], []
        parts = [
            [
                stats[other][kind * tiles + (side ^ other) * heads :][:heads]
                for other in range(SIDES)
            ]
            for kind in range(3)
        ]
        top = functools.reduce(jnp.maximum, parts[0])
        shares = [jnp.exp(part - top) for part in parts[0]]
        mass = sum(share * part for share, part in zip(shares, parts[1], strict=True))
        lse = top + jnp.log(mass)
        delta = sum(share * part for share, part in zip(shares, parts[2], strict=True)) / mass
        for head in range(heads):
            q = qd[side][:tok_dev, head * DH : (head + 1) * DH]
            d = qd[side][tok_dev : 2 * tok_dev, head * DH : (head + 1) * DH]
            scores = scaled_scores(k, q, scale)
            dprobs = lax.dot_general(v, d, CONTRACT_LAST, preferred_element_type=jnp.float32)
            probs = jnp.where(seen[side], jnp.exp(scores - lse[head : head + 1]), 0.0)
            slopes = (probs * (dprobs - delta[head : head + 1]) * scale).astype(jnp.bfloat16)
            q_rows.append(q)
            d_rows.append(d)
            slope_tiles.append(slopes)
            prob_tiles.append(probs.astype(jnp.bfloat16))
        slope_tile = jnp.concatenate(slope_tiles, axis=1)
        slopes_out[side] = slope_tile
        key_acc += jnp.dot(
            slope_tile,
            jnp.concatenate(q_rows, axis=0),
            preferred_element_type=jnp.float32,
        )
        value_acc += jnp.dot(
            jnp.concatenate(prob_tiles, axis=1),
            jnp.concatenate(d_rows, axis=0),
            preferred_element_type=jnp.float32,
        )
    acc[:, :DH] = key_acc
    acc[:, DH:] = value_acc
    for j in range(planes):
        rows = slice(j * half, (j + 1) * half)
        own = pl.multiple_of(j * tok_dev + ids[3] * half, half)
        other = pl.multiple_of(j * tok_dev + (1 - ids[3]) * half, half)
        keep[rows] = acc[pl.ds(own, half)]
        give[rows] = acc[pl.ds(other, half)].astype(give.dtype)


def members_kernel(keep, got, *outs):
    half = outs[0].shape[0]
    for j, out in enumerate(outs):
        rows = slice(j * half, (j + 1) * half)
        out[...] = (keep[rows] + got[rows].astype(jnp.float32)).astype(out.dtype)


def query_kernel(planes, *refs):
    kv_refs, slopes, q_out = refs[:planes], refs[planes], refs[planes + 3 :]
    k = jnp.concatenate([ref[:, :DH] for ref in kv_refs], axis=0)
    for source, out in enumerate(q_out):
        tok_dev, width = out.shape
        for head in range(width // DH):
            tile = slopes[source, :, head * tok_dev : (head + 1) * tok_dev]
            part = lax.dot_general(tile, k, CONTRACT_FIRST, preferred_element_type=jnp.float32)
            out[:, head * DH : (head + 1) * DH] = part.astype(out.dtype)


def copy_kernel(event, source, out):
    out[...] = source[...]


def join_kernel(event, other_event, *refs):
    rows = refs[0].shape[0]
    for i, ref in enumerate(refs[:-1]):
        refs[-1][i * rows : (i + 1) * rows] = ref[...]


def sum_kernel(*refs):
    total = refs[0][...].astype(jnp.float32)
    for ref in refs[1:-1]:
        total += ref[...].astype(jnp.float32)
    refs[-1][...] = total.astype(refs[-1].dtype)


def square_kernel(key_weight, value_weight, out):
    width = key_weight.shape[1]

    @pl.when(pl.program_id(0) == 0)
    def _():
        out[...] = jnp.zeros_like(out)

    k = key_weight[...].astype(jnp.float32)
    v = value_weight[...].astype(jnp.float32)
    out[:, :width] += jnp.sum((k * k).reshape(-1, 8, width), axis=0)
    out[:, width:] += jnp.sum((v * v).reshape(-1, 8, width), axis=0)


def spot_of(ids, planes, distance):
    count = planes * SIDES
    spot = jnp.where(ids[1] == 0, ids[0], count - 1 - ids[0]) + distance
    return jnp.where(spot >= count, spot - count, spot)


def order_kernel(planes, distances, ids, *refs):
    for r, block in zip(distances, refs[:-1], strict=True):
        refs[-1][spot_of(ids, planes, r)] = block[...]


def project_kernel(planes, steps, ids, squares, *refs):
    count = planes * SIDES
    before, beyond, first, second, refs = *refs[1:5], refs[5:]
    pieces, (raw, sums, held, grads) = refs[:8], refs[8:]
    tok_dev = held.shape[1]
    half = tok_dev // 2
    tile = raw.shape[0] // steps
    spot = spot_of(ids, planes, count // 2)
    held[spot, :half] = first[...]
    held[spot, half:] = second[...]
    held[spot_of(ids, planes, count // 2 - 1)] = before[...]
    held[spot_of(ids, planes, count // 2 + 1)] = beyond[...]
    for index, piece in enumerate(pieces):
        side = ids[1] ^ (index & 1)
        group = ids[2] ^ ((index >> 1) & 1)
        member = ids[3] ^ ((index >> 2) & 1)
        for j in range(planes):
            plane = ids[0] ^ j
            spot = jnp.where(side == 0, plane, count - 1 - plane)
            rows = pl.ds(pl.multiple_of(spot * tok_dev + member * half, half), half)
            for kind in range(2):
                columns = pl.ds(pl.multiple_of((kind * KVG + group) * DH, DH), DH)
                grads[rows, columns] = piece[
                    j * half : (j + 1) * half, kind * DH : (kind + 1) * DH
                ]
    width = raw.shape[1]
    acc = jnp.zeros((8, width), jnp.float32)
    for i in range(steps):
        rows = slice(i * tile, (i + 1) * tile)
        block = held[:, :, rows].reshape(count * tok_dev, tile)
        out = lax.dot_general(
            block, grads[...], CONTRACT_FIRST, preferred_element_type=jnp.float32
        )
        raw[rows] = out
        acc += jnp.sum((out * out).reshape(-1, 8, width), axis=0)
    total = jnp.sum(acc, axis=0, keepdims=True)
    weights = jnp.sum(squares[...], axis=0, keepdims=True)
    row = lax.broadcasted_iota(jnp.int32, sums.shape, 0)
    sums[...] = jnp.where(row == 0, total, weights)


def scale_kernel(factor, steps, sums, sums_1, sums_2, sums_3, raw, *refs):
    outs, helds, sems = refs[:2], refs[2:4], refs[4]
    total = (sums[...] + sums_1[...]) + (sums_2[...] + sums_3[...])
    grad_norm = jnp.sqrt(total[0:1] + EPSILON)
    weight_norm = jnp.sqrt(total[1:2] + EPSILON)
    clip = jnp.minimum(1.0, factor * weight_norm / grad_norm)
    width = outs[0].shape[1]
    tile = raw.shape[0] // steps
    copies = []
    for i in range(steps):
        rows = pl.ds(i * tile, tile)
        for kind, (out, held) in enumerate(zip(outs, helds, strict=True)):
            columns = slice(kind * width, (kind + 1) * width)
            held[rows] = raw[rows, columns] * clip[:, columns]
            copy = pltpu.make_async_copy(held.at[rows], out.at[rows], sems.at[2 * i + kind])
            copy.start()
            copies.append(copy)
    for copy in copies:
        copy.wait()


def local_small(
    queries, keys, values, out_grad, hidden, key_weight, value_weight, stretch_owner, positions
):
    tok_dev, width = queries.shape
    half = tok_dev // 2
    count = lax.axis_size("ctx")
    planes = count // SIDES
    groups = lax.axis_size("fsdp") // MEMBERS
    total = tok_dev * count
    ctx, fsdp = lax.axis_index("ctx"), lax.axis_index("fsdp")
    ids = jnp.stack([ctx // SIDES, ctx % SIDES, fsdp // MEMBERS, fsdp % MEMBERS]).astype(jnp.int32)
    bf16, f32 = jnp.bfloat16, jnp.float32
    shape = jax.ShapeDtypeStruct

    def call(kernel, ins, outs, mib=8, **more):
        return pl.pallas_call(
            kernel,
            out_shape=outs,
            in_specs=ins,
            out_specs=jax.tree.map(lambda _: VMEM, outs),
            compiler_params=pltpu.CompilerParams(vmem_limit_bytes=mib * 2**20),
            **more,
        )

    def move(x, plane=0, side=0, group=0, member=0):
        pairs = []
        fs = groups * MEMBERS
        for i in range(count):
            for j in range(fs):
                p, s = i // SIDES ^ plane, i % SIDES ^ side
                g, m = j // MEMBERS ^ group, j % MEMBERS ^ member
                pairs.append((i * fs + j, (p * SIDES + s) * fs + g * MEMBERS + m))
        return lax.ppermute(x, ("ctx", "fsdp"), pairs)

    ring = [p * SIDES for p in range(planes)] + [p * SIDES + 1 for p in reversed(range(planes))]

    def around(x, step):
        pairs = [(ring[i], ring[(i + step) % count]) for i in range(count)]
        return lax.ppermute(x, "ctx", pairs)

    rows = hidden.shape[1]

    far = [
        pltpu.with_memory_space_constraint(x, pltpu.HBM)
        for x in (keys, values, queries, out_grad, positions.reshape(1, tok_dev))
    ]
    kv, qd = call(
        pack_kernel,
        [SMEM] + [ANY] * 5,
        (
            shape((tok_dev, 2 * DH), bf16),
            shape((2 * tok_dev + 16, width), bf16),
        ),
        scratch_shapes=[
            pltpu.VMEM((1, tok_dev), jnp.int32),
            pltpu.SemaphoreType.DMA((5,)),
        ],
    )(ids, *far)
    qd_side = move(qd, side=1)
    kv_all = [kv] + [move(kv, plane=j) for j in range(1, planes)]
    qd_all = [qd, qd_side]
    held = call(copy_kernel, [ANY, VMEM], shape(hidden.shape, bf16))(qd, hidden)
    (held,) = after((held,), qd_side, *kv_all[1:])
    blocks = {0: held}
    up, down = around(held, 1), around(held, -1)

    columns = 2 * KVG * DH
    steps = 8
    tile = rows // steps
    weight = pl.BlockSpec((tile, columns // 2), lambda i: (i, 0))
    squares = pl.pallas_call(
        square_kernel,
        grid=(steps,),
        out_shape=shape((8, columns), f32),
        in_specs=[weight] * 2,
        out_specs=pl.BlockSpec((8, columns), lambda i: (0, 0)),
        compiler_params=pltpu.CompilerParams(vmem_limit_bytes=8 * 2**20),
    )(key_weight, value_weight)

    tiles = SIDES * width // DH
    stats = call(
        functools.partial(stats_kernel, planes),
        [SMEM] * 2 + [VMEM] * (planes + SIDES),
        shape((3 * tiles, tok_dev), f32),
    )(ids, stretch_owner, *kv_all, *qd_all)
    stats_side = move(stats, side=1)
    blocks[count - 1], blocks[1] = after((up, down), stats_side)
    up, down = around(blocks[count - 1], 1), around(blocks[1], -1)
    grads_shape = (planes * half, 2 * DH)
    keep, give, slopes = call(
        functools.partial(grads_kernel, planes),
        [SMEM] * 2 + [VMEM] * (planes + 2 * SIDES),
        (
            shape(grads_shape, f32),
            shape(grads_shape, bf16),
            shape((SIDES, planes * tok_dev, tok_dev * width // DH), bf16),
        ),
        scratch_shapes=[pltpu.VMEM((planes * tok_dev, 2 * DH), f32)],
    )(ids, stretch_owner, *kv_all, *qd_all, stats, stats_side)
    kv_parts = call(
        members_kernel,
        [VMEM] * 2,
        tuple(shape((half, 2 * DH), bf16 if j else f32) for j in range(planes)),
    )(keep, move(give, member=1))
    piece = call(sum_kernel, [VMEM] * planes, shape((half, 2 * DH), bf16))(
        kv_parts[0], *[move(kv_parts[j], plane=j) for j in range(1, planes)]
    )
    blocks[count - 2], blocks[2] = after((up, down), piece)
    up, down = around(blocks[count - 2], 1), around(blocks[2], -1)
    parts = [move(piece, plane=j) for j in range(1, planes)]
    q_parts = call(
        functools.partial(query_kernel, planes),
        [VMEM] * (planes + 1) + [ANY] * 2,
        tuple(shape((tok_dev, width), bf16 if j else f32) for j in range(SIDES)),
    )(*kv_all, slopes, piece, squares)
    early = tuple(range(count // 2 - 1)) + tuple(range(count // 2 + 2, count))
    ordered = call(
        functools.partial(order_kernel, planes, early),
        [SMEM] + [VMEM] * len(early),
        pltpu.VMEM((count,) + hidden.shape, bf16),
    )(ids, *[blocks[r] for r in early])
    piece_all = call(join_kernel, [ANY] * 2 + [VMEM] * planes, shape(grads_shape, bf16))(
        q_parts[1], ordered, piece, *parts
    )
    blocks[count - 3], blocks[3] = up, down
    up, down = halves_after(up, down, piece_all)
    blocks[4], blocks[count] = around(up, 1), around(down, -1)
    piece_side = move(piece_all, side=1)
    (piece_side,) = after((piece_side,), up)
    near = [piece_all, piece_side, move(piece_all, group=1), move(piece_side, group=1)]
    pieces = near + [move(part, member=1) for part in near]

    query_grad = call(sum_kernel, [VMEM] * SIDES, shape((tok_dev, width), bf16))(
        q_parts[0], move(q_parts[1], side=1)
    )

    steps = 2
    raw, sums, _ = call(
        functools.partial(project_kernel, planes, steps),
        [SMEM] + [VMEM] * (6 + len(pieces)),
        (
            pltpu.VMEM((rows, columns), f32),
            shape((8, columns), f32),
            pltpu.VMEM(ordered.shape, bf16),
        ),
        mib=12,
        scratch_shapes=[pltpu.VMEM((total, columns), bf16)],
        input_output_aliases={2: 2},
    )(
        ids,
        squares,
        pltpu.with_memory_space_constraint(ordered, pltpu.VMEM),
        blocks[count // 2 - 1],
        blocks[count // 2 + 1],
        blocks[count // 2],
        blocks[count],
        *pieces,
    )
    sums_all = [sums, move(sums, member=1), move(sums, group=1), move(sums, group=1, member=1)]
    steps = 8
    key_grad, value_grad = pl.pallas_call(
        functools.partial(scale_kernel, CLIP_RATE * total, steps),
        out_shape=(shape((rows, columns // 2), f32),) * 2,
        in_specs=[VMEM] * 5,
        out_specs=(ANY, ANY),
        scratch_shapes=[pltpu.VMEM((rows, columns // 2), f32)] * 2
        + [pltpu.SemaphoreType.DMA((2 * steps,))],
        compiler_params=pltpu.CompilerParams(vmem_limit_bytes=8 * 2**20),
    )(*sums_all, pltpu.with_memory_space_constraint(raw, pltpu.VMEM))
    return (query_grad, key_grad, value_grad)


def solution(mesh):
    ctx_count, fsdp_count = mesh.shape["ctx"], mesh.shape["fsdp"]

    def program(queries, keys, values, out_grad, hidden, *rest):
        tok_dev = queries.shape[0] // ctx_count
        heads = queries.shape[1] // fsdp_count // DH
        gathered = hidden.size // fsdp_count * hidden.dtype.itemsize
        planes = ctx_count // SIDES
        small = (
            ctx_count == 8
            and gathered <= GATHER_LIMIT
            and planes * SIDES == ctx_count
            and planes & (planes - 1) == 0
            and heads * MEMBERS == HPG
            and fsdp_count == KVG * MEMBERS
            and tok_dev == DH
        )
        return jax.shard_map(
            local_small if small else local_large,
            mesh=mesh,
            in_specs=(
                P("ctx", "fsdp"),
                P("ctx", None),
                P("ctx", None),
                P("ctx", "fsdp"),
                P("ctx", "fsdp"),
                P("fsdp", None),
                P("fsdp", None),
                P(),
                P("ctx"),
            ),
            out_specs=(P("ctx", "fsdp"), P("fsdp", None), P("fsdp", None)),
            check_vma=False,
        )(queries, keys, values, out_grad, hidden, *rest)

    return program
```
